32 devices in a mesh: frow: 2 (over core), fcol: 16 (over z, y, x).
Axes of the slice: x: 2, y: 2, z: 4, core: 2. Of those that a mesh axis runs over, the one named last changes fastest.
Arguments:
- right_side: float32 [16, 512, 256], P('frow', 'fcol'), may hold values from -6 to 6
- noise_weight: float32 [16, 512, 256], P('frow', 'fcol'), may hold values from 3 to 4.5
- stencils: bfloat16 [9, 256, 256], replicated, may hold values from -1 to 1, as said below
- neighbours: int32 [16, 512, 9], P('frow', 'fcol'), may hold values from -1 to 8191, as said below
Outputs:
- solution: float32 [16, 512, 256], P('frow', 'fcol')
- coarse_residual: float32 [8, 256, 256], P('frow')
The draws below stay inside these ranges and needn't reach their ends.
Inputs may be any that keep to these rules, and one draw needn't show every extreme that they name: `neighbours`: each entry is -1 (an empty slot) or the index r * 512 + c of the tile at row r = own row + k // 3 - 1 and column c = own column + k % 3 - 1 for slot k; slot 4 always holds the tile itself; if tile t holds tile s in slot k, then s holds t in slot 8 - k. stencils[8 - k] is the transpose of stencils[k], and stencils[4] is symmetric.
All inputs are finite; a program needn't handle non-finite values.
Results may differ from the reference program's by a relative error of at most 0.0031.
Values may be sent and summed in bfloat16 or wider, within the bound.
No kernel may reach another device: no remote copies, remote signals or barrier semaphores. Data moves between devices by JAX's collectives and lax.ppermute only.
A program may use at most 64 MiB of HBM per device.

```python
import math
import jax
import jax.numpy as jnp
from jax import lax

PIX = 256
STENCILS = 9
DEG = 3
GRID_ROWS = 16
GRID_COLS = 512


def draw_neighbours(key, part):
    shape_three = (GRID_ROWS, GRID_COLS, STENCILS)
    tile_row = lax.broadcasted_iota(jnp.int32, shape_three, 0)
    tile_col = lax.broadcasted_iota(jnp.int32, shape_three, 1)
    slot_index = lax.broadcasted_iota(jnp.int32, shape_three, 2)
    base_drop = jax.random.randint(jax.random.fold_in(key, 17), shape_three, 0, 16) == 0
    near_row = tile_row + slot_index // 3 - 1
    near_col = tile_col + slot_index % 3 - 1
    inside = (near_row >= 0) & (near_row < GRID_ROWS) & (near_col >= 0) & (near_col < GRID_COLS)
    clamp_row = jnp.clip(near_row, 0, GRID_ROWS - 1)
    clamp_col = jnp.clip(near_col, 0, GRID_COLS - 1)
    mirror_index = ((clamp_row * GRID_COLS + clamp_col) * STENCILS + (8 - slot_index)).astype(jnp.int32)
    mirrored = jnp.take(base_drop.reshape(-1), mirror_index.reshape(-1), axis=0).reshape(shape_three)
    dropped = jnp.where(slot_index < 4, base_drop, jnp.where(slot_index > 4, mirrored, False))
    keep = inside & jnp.logical_not(dropped)
    return jnp.where(keep, near_row * GRID_COLS + near_col, -1).astype(jnp.int32)


def draw_stencils(key, part):
    first_key, second_key = jax.random.split(jax.random.fold_in(key, 29))
    scale = (16.0 * PIX) ** (-0.5)
    lower_blocks = jnp.clip(jax.random.normal(first_key, (4, PIX, PIX), jnp.float32), -6.0, 6.0) * scale
    square = jax.random.normal(second_key, (PIX, PIX), jnp.float32)
    middle = jnp.clip((square + square.T) * 0.5 ** 0.5, -6.0, 6.0) * scale
    lower_blocks = lower_blocks.astype(jnp.bfloat16)
    middle = middle.astype(jnp.bfloat16)
    upper_blocks = jnp.transpose(lower_blocks[::-1], (0, 2, 1))
    return jnp.concatenate([lower_blocks, middle[None], upper_blocks], 0)


def shard_levels(rng, extent, cuts, low, top_value):
    factor_of = 1.0
    for position, blocks in cuts:
        draws = jax.random.uniform(jax.random.fold_in(jax.random.fold_in(rng, 6), position), (blocks,), jnp.float32, low / len(cuts), top_value / len(cuts))
        factor_of = factor_of * jnp.repeat(jnp.exp(draws), extent[position] // blocks).reshape((-1,) + (1,) * (len(extent) - 1 - position))
    return factor_of


def centred(key, dims, deviation, bound, cuts=(), dtype=jnp.bfloat16):
    values = jax.random.normal(key, dims, jnp.float32) * deviation
    if len(cuts) > 0:
        values = shard_levels(key, dims, cuts, -0.22, 0.18) * values
    return jnp.clip(values, min=-bound, max=bound).astype(dtype)


def setup_inputs(seed: int = 0) -> dict:
    keys = jax.random.split(jax.random.key(seed), 5)
    right_side = centred(keys[0], (GRID_ROWS, GRID_COLS, PIX), 1.0, 6.0, ((0, 2), (1, 16)), jnp.float32)
    noise_weight = jnp.clip(jnp.exp(math.log(4.5) - 0.4054651 * jax.random.uniform(keys[1], (GRID_ROWS, GRID_COLS, PIX), jnp.float32) ** shard_levels(keys[1], (GRID_ROWS, GRID_COLS, PIX), ((0, 2), (1, 16)), -0.2, 0.2)), 3.0, 4.5)
    stencils = draw_stencils(jax.random.fold_in(keys[4], 71), 0)
    neighbours = draw_neighbours(jax.random.fold_in(keys[4], 71), 0)
    return {"right_side": right_side, "noise_weight": noise_weight, "stencils": stencils, "neighbours": neighbours}


lower_edge = 1.5
upper_edge = 6.0


def restrict(paired_block):
    height, width, doubled = paired_block.shape
    pixels = doubled // 2
    summed = jnp.sum(paired_block.reshape(height // 2, 2, width, 2, pixels // 4, 4), axis=5)
    return jnp.transpose(summed, (0, 2, 1, 3, 4)).reshape(height // 2, width, pixels)


def smooth(right_side, operate):
    center = 0.5 * (upper_edge + lower_edge)
    half_width = 0.5 * (upper_edge - lower_edge)
    spread_ratio = center / half_width
    solution = jnp.zeros_like(right_side)
    residual = right_side
    for sweep_index in range(2):
        ratio_now = 1.0 / spread_ratio
        direction = residual / center
        for step_index in range(DEG):
            solution = solution + direction
            residual = residual - operate(direction)
            if step_index < DEG - 1:
                ratio_next = 1.0 / (2.0 * spread_ratio - ratio_now)
                direction = (ratio_next * ratio_now) * direction + (2.0 * ratio_next / half_width) * residual
                ratio_now = ratio_next
    return solution, residual


def reference(right_side, noise_weight, stencils, neighbours):
    tiles = GRID_ROWS * GRID_COLS
    stencil_matrix = stencils.reshape(STENCILS * PIX, PIX)
    targets = jnp.where(neighbours < 0, tiles, neighbours).astype(jnp.int32)

    def operate(direction):
        rounded = direction.astype(jnp.bfloat16)
        flattened = jnp.concatenate([rounded.reshape(tiles, PIX), jnp.zeros((1, PIX), jnp.bfloat16)], 0)

        def one_row(row_targets):
            picked = jnp.take(flattened, row_targets.reshape(-1), axis=0).reshape(GRID_COLS, STENCILS * PIX)
            return jnp.dot(picked, stencil_matrix, preferred_element_type=jnp.float32)

        coupled = lax.map(one_row, targets)
        return noise_weight * direction + coupled

    solution, residual = smooth(right_side, operate)
    coarse_residual = restrict(residual.reshape(GRID_ROWS, GRID_COLS // 2, 2 * PIX))
    return solution, coarse_residual
```

```python
import functools

import jax
import jax.numpy as jnp
from jax import lax
from jax.experimental import pallas as pl
from jax.experimental.pallas import tpu as pltpu
from jax.sharding import PartitionSpec as P

DEG = 3
SWEEPS = 2
STEPS = DEG * SWEEPS
SIDE = 8
LANES = 128

lower_edge = 1.5
upper_edge = 6.0
center = 0.5 * (upper_edge + lower_edge)
half_width = 0.5 * (upper_edge - lower_edge)
weight_middle = 3.75

F32 = jnp.float32
BF16 = jnp.bfloat16
VMEM_SPEC = pl.BlockSpec(memory_space=pltpu.VMEM)


def step_factors():
    spread_ratio = center / half_width
    factors = []
    for sweep in range(SWEEPS):
        ratio = 1.0 / spread_ratio
        for step in range(DEG):
            if step < DEG - 1:
                ratio_next = 1.0 / (2.0 * spread_ratio - ratio)
                factors.append((ratio_next * ratio, 2.0 * ratio_next / half_width))
                ratio = ratio_next
            else:
                factors.append((0.0, 1.0 / center))
    return factors


def pack_kernel(right_ref, weight_ref, near_ref, first_ref, last_ref, whole_ref, held_ref):
    rows, cols, pixels = right_ref.shape
    slots = near_ref.shape[0]
    flags = jnp.where(near_ref[...] >= 0, 1.0, 0.0).astype(F32).reshape(slots * rows, cols)
    flags = jnp.concatenate([flags, jnp.zeros((slots * rows, LANES - cols), F32)], 1)
    flags = jnp.concatenate([flags, jnp.zeros((LANES - slots * rows, LANES), F32)], 0)
    turned = jnp.transpose(flags)[:cols]
    held_ref[...] = turned
    right = right_ref[...]
    weight = weight_ref[...] - weight_middle
    whole_ref[:rows, :cols, :] = right.astype(BF16)
    whole_ref[:rows, cols:, :] = weight.astype(BF16)
    whole_ref[rows, :cols, :LANES] = turned.astype(BF16)
    for ref, start in ((first_ref, 0), (last_ref, cols - SIDE)):
        part = slice(start, start + SIDE)
        ref[:rows] = jnp.concatenate([right[:, part], weight[:, part]], 1).astype(BF16)
        strip = jnp.concatenate([turned[part], jnp.zeros((SIDE, LANES), F32)], 0)
        ref[rows, :, :LANES] = strip.astype(BF16)


def smooth_kernel(ends, *refs):
    right_ref, weight_ref, held_ref, stencil_ref, after_ref, before_ref = refs[:6]
    halos = [refs[6 + 2 * i : 8 + 2 * i] for i in range(ends)]
    solution_ref, coarse_ref = refs[6 + 2 * ends : 8 + 2 * ends]
    residual, direction, weight, shifted, mask, summed = refs[8 + 2 * ends :]
    own_rows, own_cols, pixels = right_ref.shape
    slots = mask.shape[0]
    rows, cols, _ = residual.shape
    after = slice(own_cols, own_cols + SIDE)
    before = slice(own_cols + SIDE, cols)
    if ends == 1:
        core = lax.axis_index("frow")
        own_start = core * STEPS
        places = [((1 - core) * own_rows, core * (own_rows - STEPS))]
    else:
        own_start = STEPS
        places = [(0, own_rows - STEPS), (STEPS + own_rows, 0)]

    own = pl.ds(own_start, own_rows)
    residual[own, :own_cols, :] = right_ref[...]
    weight[own, :own_cols, :] = weight_ref[...]
    for part, ref in ((after, after_ref), (before, before_ref)):
        strip = ref[:own_rows].astype(F32)
        residual[own, part, :] = strip[:, :SIDE]
        weight[own, part, :] = strip[:, SIDE:] + weight_middle
    turned = jnp.concatenate(
        [
            held_ref[...],
            after_ref[own_rows, :, :LANES].astype(F32)[:SIDE],
            before_ref[own_rows, :, :LANES].astype(F32)[:SIDE],
        ],
        0,
    )

    def spread(turned, base, count):
        for slot in range(slots):
            for row in range(count):
                lane = slot * own_rows + row
                column = jnp.broadcast_to(turned[:, lane : lane + 1], (cols, LANES))
                mask[slot, base + row] = column.astype(BF16)

    spread(turned, own_start, own_rows)

    for (base, first), (whole_ref, sides_ref) in zip(places, halos):
        here = pl.ds(base, STEPS)
        there = pl.ds(first, STEPS)
        strip = whole_ref[there].astype(F32)
        residual[here, :own_cols, :] = strip[:, :own_cols]
        weight[here, :own_cols, :] = strip[:, own_cols:] + weight_middle
        for part, side in ((after, 0), (before, 1)):
            strip = sides_ref[side, there].astype(F32)
            residual[here, part, :] = strip[:, :SIDE]
            weight[here, part, :] = strip[:, SIDE:] + weight_middle
        turned = jnp.concatenate(
            [
                whole_ref[own_rows, :own_cols, :LANES].astype(F32),
                sides_ref[0, own_rows, :, :LANES].astype(F32)[:SIDE],
                sides_ref[1, own_rows, :, :LANES].astype(F32)[:SIDE],
            ],
            0,
        )
        if ends == 1:
            turned = pltpu.roll(turned, lax.rem(LANES - first, LANES), 1)
            spread(turned, base, STEPS)
        else:
            spread(pltpu.roll(turned, (LANES - first) % LANES, 1), base, STEPS)

    def put_direction(slot, start, count, value):
        here = pl.ds(start + 1, count)
        shifted[slot, 1, here] = value.astype(BF16)
        shifted[slot, 0, here] = pltpu.roll(value, 1, 1).astype(BF16)
        shifted[slot, 2, here] = pltpu.roll(value, cols - 1, 1).astype(BF16)

    edge = jnp.zeros((cols, pixels), BF16)
    for slot in range(2):
        for move in range(3):
            shifted[slot, move, 0] = edge
            shifted[slot, move, rows + 1] = edge
    value = residual[...] * (1.0 / center)
    direction[...] = value
    put_direction(0, 0, rows, value)
    solution_ref[...] = jnp.zeros((own_rows, own_cols, pixels), F32)

    stencil = stencil_ref[...].reshape(slots * pixels, pixels)
    factors = step_factors()
    for step in range(STEPS):
        now, later = step % 2, 1 - step % 2
        last = step == STEPS - 1
        solution_ref[...] += direction[own, :own_cols, :]
        margin = STEPS - 1 - step
        if ends == 1:
            count = own_rows + margin + (own_rows + margin) % 2
            count = min(count, rows)
            start = core * (rows - count)
        else:
            count = own_rows + 2 * margin
            start = STEPS - margin
        width = own_cols if last else cols
        half = count // 2
        for piece in range(2):
            base = start + piece * half
            here = pl.ds(base, half)
            picked = []
            for slot in range(slots):
                across, along = slot // 3, slot % 3
                keep = mask[slot, here, :width, :]
                source = shifted[now, along, pl.ds(base + across, half), :width, :]
                picked.append(source[:, :, :LANES] * keep)
                picked.append(source[:, :, LANES:] * keep)
            picked = jnp.concatenate(picked, 2).reshape(half * width, slots * pixels)
            coupled = jnp.dot(picked, stencil, preferred_element_type=F32)
            coupled = coupled.reshape(half, width, pixels)
            moved = direction[here, :width, :]
            left = residual[here, :width, :] - (weight[here, :width, :] * moved + coupled)
            residual[here, :width, :] = left
            if not last:
                a, b = factors[step]
                value = b * left if a == 0.0 else a * moved + b * left
                direction[here, :width, :] = value
                put_direction(later, base, half, value)

    fine = residual[own, :own_cols, :].reshape(own_rows * own_cols, pixels)
    high = fine.astype(BF16)
    low = (fine - high.astype(F32)).astype(BF16)
    quarter = pixels // 4
    from_pixel = lax.broadcasted_iota(jnp.int32, (pixels, LANES), 0) // 4
    to_pixel = lax.broadcasted_iota(jnp.int32, (pixels, LANES), 1)
    adder = jnp.where(from_pixel == to_pixel, 1.0, 0.0).astype(BF16)
    total = jnp.dot(high, adder, preferred_element_type=F32) + jnp.dot(
        low, adder, preferred_element_type=F32
    )
    summed[...] = total.reshape(own_rows, own_cols, LANES)
    for row in range(own_rows // 2):
        pieces = []
        for across in range(2):
            for along in range(2):
                piece = summed[2 * row + across, pl.ds(along, own_cols // 2, stride=2), :]
                pieces.append(piece[:, :quarter])
        coarse_ref[row] = jnp.concatenate(pieces, 1).astype(BF16)


def body(right_side, noise_weight, stencils, neighbours):
    rows, cols, pixels = right_side.shape
    slots = stencils.shape[0]
    pairs, ring = lax.axis_size("frow"), lax.axis_size("fcol")
    forward = [(i, i + 1) for i in range(ring - 1)]
    backward = [(i + 1, i) for i in range(ring - 1)]

    first, last, whole, held = pl.pallas_call(
        pack_kernel,
        out_shape=(
            jax.ShapeDtypeStruct((rows + 1, 2 * SIDE, pixels), BF16),
            jax.ShapeDtypeStruct((rows + 1, 2 * SIDE, pixels), BF16),
            jax.ShapeDtypeStruct((rows + 1, 2 * cols, pixels), BF16),
            jax.ShapeDtypeStruct((cols, LANES), F32),
        ),
        in_specs=[VMEM_SPEC] * 3,
        out_specs=(VMEM_SPEC,) * 4,
        name="pack",
    )(right_side, noise_weight, jnp.transpose(neighbours, (2, 0, 1)))

    after = lax.ppermute(first, "fcol", backward)
    before = lax.ppermute(last, "fcol", forward)
    if pairs == 2:
        moves = [[(0, 1), (1, 0)]]
    else:
        moves = [
            [(i, i + 1) for i in range(pairs - 1)],
            [(i + 1, i) for i in range(pairs - 1)],
        ]
    wholes = [lax.ppermute(whole, "frow", move) for move in moves]
    sides = jnp.stack([after, before])
    halos = []
    for move, other in zip(moves, wholes):
        halos += [other, lax.ppermute(sides, "frow", move)]

    ends = len(moves)
    rows_held, cols_held = rows + ends * STEPS, cols + 2 * SIDE
    solution, coarse = pl.pallas_call(
        functools.partial(smooth_kernel, ends),
        out_shape=(
            jax.ShapeDtypeStruct((rows, cols, pixels), F32),
            jax.ShapeDtypeStruct((rows // 2, cols // 2, pixels), BF16),
        ),
        in_specs=[VMEM_SPEC] * (6 + 2 * ends),
        out_specs=(VMEM_SPEC,) * 2,
        scratch_shapes=[
            pltpu.VMEM((rows_held, cols_held, pixels), F32),
            pltpu.VMEM((rows_held, cols_held, pixels), F32),
            pltpu.VMEM((rows_held, cols_held, pixels), F32),
            pltpu.VMEM((2, 3, rows_held + 2, cols_held, pixels), BF16),
            pltpu.VMEM((slots, rows_held, cols_held, LANES), BF16),
            pltpu.VMEM((rows, cols, LANES), F32),
        ],
        compiler_params=pltpu.CompilerParams(vmem_limit_bytes=48 * 1024 * 1024),
        name="smooth",
    )(right_side, noise_weight, held, stencils, after, before, *halos)

    spread = jnp.broadcast_to(coarse[None], (ring,) + coarse.shape)
    gathered = lax.all_to_all(spread, "fcol", 0, 0)
    gathered = jnp.transpose(gathered, (1, 0, 2, 3)).astype(F32)
    return solution, gathered.reshape(rows // 2, ring * (cols // 2), pixels)


def solution(mesh):
    placed = (P("frow", "fcol", None), P("frow", "fcol", None), P(), P("frow", "fcol", None))
    return jax.shard_map(
        body,
        mesh=mesh,
        in_specs=placed,
        out_specs=(P("frow", "fcol", None), P("frow", None, None)),
        check_vma=False,
    )
```

```python
import functools

import jax
import jax.numpy as jnp
from jax import lax
from jax.experimental import pallas as pl
from jax.experimental.pallas import tpu as pltpu
from jax.sharding import PartitionSpec as P

DEG = 3
SWEEPS = 2
STEPS = DEG * SWEEPS
SIDE = 8
LANES = 128

lower_edge = 1.5
upper_edge = 6.0
center = 0.5 * (upper_edge + lower_edge)
half_width = 0.5 * (upper_edge - lower_edge)
weight_middle = 3.75

F32 = jnp.float32
BF16 = jnp.bfloat16
HBM_SPEC = pl.BlockSpec(memory_space=pl.ANY)
VMEM_SPEC = pl.BlockSpec(memory_space=pltpu.VMEM)


def step_factors():
    spread_ratio = center / half_width
    factors = []
    for sweep in range(SWEEPS):
        ratio = 1.0 / spread_ratio
        for step in range(DEG):
            if step < DEG - 1:
                ratio_next = 1.0 / (2.0 * spread_ratio - ratio)
                factors.append((ratio_next * ratio, 2.0 * ratio_next / half_width))
                ratio = ratio_next
            else:
                factors.append((0.0, 1.0 / center))
    return factors


def pack_kernel(right_hbm, weight_hbm, near_hbm, *refs):
    even_ref, odd_ref, whole_ref, held_ref, right_ref, weight_ref, near_ref, arrived = refs
    near_copy = pltpu.make_async_copy(near_hbm, near_ref, arrived.at[2])
    near_copy.start()
    copies = [
        pltpu.make_async_copy(right_hbm, right_ref, arrived.at[0]),
        pltpu.make_async_copy(weight_hbm, weight_ref, arrived.at[1]),
    ]
    for copy in copies:
        copy.start()
    rows, cols, pixels = right_ref.shape
    slots = near_ref.shape[0]
    near_copy.wait()
    flags = jnp.where(near_ref[...] >= 0, 1.0, 0.0).astype(F32).reshape(slots * rows, cols)
    flags = jnp.concatenate([flags, jnp.zeros((slots * rows, LANES - cols), F32)], 1)
    flags = jnp.concatenate([flags, jnp.zeros((LANES - slots * rows, LANES), F32)], 0)
    held_ref[...] = jnp.transpose(flags)[:cols]
    whole_ref[rows, :cols, :LANES] = held_ref[...].astype(BF16)
    parity = lax.rem(lax.axis_index("fcol"), 2)
    starts = [(cols - SIDE) * (1 - parity), (cols - SIDE) * parity]
    parts = [pl.ds(pl.multiple_of(start, SIDE), SIDE) for start in starts]
    for ref, part in zip((even_ref, odd_ref), parts):
        strip = jnp.concatenate([held_ref[part, :], jnp.zeros((SIDE, LANES), F32)], 0)
        ref[rows, :, :LANES] = strip.astype(BF16)
    for copy in copies:
        copy.wait()
    for ref, part in zip((odd_ref, even_ref), parts[::-1]):
        ref[:rows] = jnp.concatenate(
            [right_ref[:, part, :], weight_ref[:, part, :] - weight_middle], 1
        ).astype(BF16)
    whole_ref[:rows, :cols, :] = right_ref[...].astype(BF16)
    whole_ref[:rows, cols:, :] = (weight_ref[...] - weight_middle).astype(BF16)


def smooth_kernel(ends, *refs):
    right_ref, weight_ref, held_ref, stencil_hbm, even_ref, odd_ref = refs[:6]
    halos = [refs[6 + 2 * i : 8 + 2 * i] for i in range(ends)]
    solution_ref, coarse_ref = refs[6 + 2 * ends : 8 + 2 * ends]
    residual, direction, weight, shifted, mask, summed, turned, stencil_ref, arrived = refs[
        8 + 2 * ends :
    ]
    stencil_copy = pltpu.make_async_copy(stencil_hbm, stencil_ref, arrived)
    stencil_copy.start()
    own_rows, own_cols, pixels = right_ref.shape
    slots = mask.shape[0]
    rows, cols, _ = residual.shape
    parity = lax.rem(lax.axis_index("fcol"), 2)
    even_part = pl.ds(pl.multiple_of(own_cols + SIDE * parity, SIDE), SIDE)
    odd_part = pl.ds(pl.multiple_of(own_cols + SIDE * (1 - parity), SIDE), SIDE)
    if ends == 1:
        core = lax.axis_index("frow")
        own_start = core * STEPS
        places = [((1 - core) * own_rows, core * (own_rows - STEPS))]
    else:
        own_start = STEPS
        places = [(0, own_rows - STEPS), (STEPS + own_rows, 0)]

    def spread(first, base, count):
        flags = turned[...]
        if not (isinstance(first, int) and first == 0):
            flags = pltpu.roll(flags, lax.rem(LANES - first, LANES), 1)
        for slot in range(slots):
            for row in range(count):
                lane = slot * own_rows + row
                column = jnp.broadcast_to(flags[:, lane : lane + 1], (cols, LANES))
                mask[slot, base + row] = column.astype(BF16)

    own = pl.ds(own_start, own_rows)
    residual[own, :own_cols, :] = right_ref[...]
    weight[own, :own_cols, :] = weight_ref[...]
    turned[:own_cols, :] = held_ref[...]
    for part, ref in ((even_part, even_ref), (odd_part, odd_ref)):
        strip = ref[:own_rows].astype(F32)
        residual[own, part, :] = strip[:, :SIDE]
        weight[own, part, :] = strip[:, SIDE:] + weight_middle
        turned[part, :] = ref[own_rows, :, :LANES].astype(F32)[:SIDE]
    spread(0, own_start, own_rows)

    for (base, first), (whole_ref, sides_ref) in zip(places, halos):
        here = pl.ds(base, STEPS)
        there = pl.ds(first, STEPS)
        strip = whole_ref[there].astype(F32)
        residual[here, :own_cols, :] = strip[:, :own_cols]
        weight[here, :own_cols, :] = strip[:, own_cols:] + weight_middle
        turned[:own_cols, :] = whole_ref[own_rows, :own_cols, :LANES].astype(F32)
        for part, side in ((even_part, 0), (odd_part, 1)):
            strip = sides_ref[side, there].astype(F32)
            residual[here, part, :] = strip[:, :SIDE]
            weight[here, part, :] = strip[:, SIDE:] + weight_middle
            turned[part, :] = sides_ref[side, own_rows, :, :LANES].astype(F32)[:SIDE]
        spread(first, base, STEPS)

    def put_direction(slot, start, count, value):
        here = pl.ds(start + 1, count)
        shifted[slot, 1, here] = value.astype(BF16)
        shifted[slot, 0, here] = pltpu.roll(value, 1, 1).astype(BF16)
        shifted[slot, 2, here] = pltpu.roll(value, cols - 1, 1).astype(BF16)

    edge = jnp.zeros((cols, pixels), BF16)
    for slot in range(2):
        for move in range(3):
            shifted[slot, move, 0] = edge
            shifted[slot, move, rows + 1] = edge
    value = residual[...] * (1.0 / center)
    direction[...] = value
    put_direction(0, 0, rows, value)
    solution_ref[...] = jnp.zeros((own_rows, own_cols, pixels), F32)

    stencil_copy.wait()
    stencil = stencil_ref[...].reshape(slots * pixels, pixels)
    factors = step_factors()
    for step in range(STEPS):
        now, later = step % 2, 1 - step % 2
        last = step == STEPS - 1
        solution_ref[...] += direction[own, :own_cols, :]
        margin = STEPS - 1 - step
        if ends == 1:
            count = own_rows + margin + (own_rows + margin) % 2
            count = min(count, rows)
            start = core * (rows - count)
        else:
            count = own_rows + 2 * margin
            start = STEPS - margin
        width = own_cols if last else cols
        half = count // 2
        for piece in range(2):
            base = start + piece * half
            here = pl.ds(base, half)
            picked = []
            for slot in range(slots):
                across, along = slot // 3, slot % 3
                keep = mask[slot, here, :width, :]
                source = shifted[now, along, pl.ds(base + across, half), :width, :]
                picked.append(source[:, :, :LANES] * keep)
                picked.append(source[:, :, LANES:] * keep)
            picked = jnp.concatenate(picked, 2).reshape(half * width, slots * pixels)
            coupled = jnp.dot(picked, stencil, preferred_element_type=F32)
            coupled = coupled.reshape(half, width, pixels)
            moved = direction[here, :width, :]
            left = residual[here, :width, :] - (weight[here, :width, :] * moved + coupled)
            residual[here, :width, :] = left
            if not last:
                a, b = factors[step]
                value = b * left if a == 0.0 else a * moved + b * left
                direction[here, :width, :] = value
                put_direction(later, base, half, value)

    fine = residual[own, :own_cols, :].reshape(own_rows * own_cols, pixels)
    high = fine.astype(BF16)
    low = (fine - high.astype(F32)).astype(BF16)
    quarter = pixels // 4
    from_pixel = lax.broadcasted_iota(jnp.int32, (pixels, LANES), 0) // 4
    to_pixel = lax.broadcasted_iota(jnp.int32, (pixels, LANES), 1)
    adder = jnp.where(from_pixel == to_pixel, 1.0, 0.0).astype(BF16)
    total = jnp.dot(high, adder, preferred_element_type=F32) + jnp.dot(
        low, adder, preferred_element_type=F32
    )
    summed[...] = total.reshape(own_rows, own_cols, LANES)
    for row in range(own_rows // 2):
        pieces = []
        for across in range(2):
            for along in range(2):
                piece = summed[2 * row + across, pl.ds(along, own_cols // 2, stride=2), :]
                pieces.append(piece[:, :quarter])
        coarse_ref[row] = jnp.concatenate(pieces, 1).astype(BF16)


def body(right_side, noise_weight, stencils, neighbours):
    rows, cols, pixels = right_side.shape
    slots = stencils.shape[0]
    pairs, ring = lax.axis_size("frow"), lax.axis_size("fcol")
    swaps = [
        [(i, j) for low in range(first, ring - 1, 2) for i, j in ((low, low + 1), (low + 1, low))]
        for first in (0, 1)
    ]
    near = jnp.transpose(neighbours, (2, 0, 1))
    right_hbm, weight_hbm, stencil_hbm, near_hbm = [
        pltpu.with_memory_space_constraint(array, pltpu.HBM)
        for array in (right_side, noise_weight, stencils, near)
    ]

    even, odd, whole, held, right, weight = pl.pallas_call(
        pack_kernel,
        out_shape=(
            pltpu.VMEM((rows + 1, 2 * SIDE, pixels), BF16),
            pltpu.VMEM((rows + 1, 2 * SIDE, pixels), BF16),
            pltpu.VMEM((rows + 1, 2 * cols, pixels), BF16),
            pltpu.VMEM((cols, LANES), F32),
            pltpu.VMEM((rows, cols, pixels), F32),
            pltpu.VMEM((rows, cols, pixels), F32),
        ),
        in_specs=[HBM_SPEC] * 3,
        out_specs=(VMEM_SPEC,) * 6,
        scratch_shapes=[
            pltpu.VMEM((slots, rows, cols), jnp.int32),
            pltpu.SemaphoreType.DMA((3,)),
        ],
        compiler_params=pltpu.CompilerParams(vmem_limit_bytes=8 * 1024 * 1024),
        name="pack",
    )(right_hbm, weight_hbm, near_hbm)

    odd_side = lax.ppermute(odd, "fcol", swaps[1])
    even_side = lax.ppermute(even, "fcol", swaps[0])
    if pairs == 2:
        moves = [[(0, 1), (1, 0)]]
    else:
        moves = [
            [(i, i + 1) for i in range(pairs - 1)],
            [(i + 1, i) for i in range(pairs - 1)],
        ]
    wholes = [lax.ppermute(whole, "frow", move) for move in moves]
    sides = jnp.stack([even_side, odd_side])
    halos = []
    for move, other in zip(moves, wholes):
        halos += [other, lax.ppermute(sides, "frow", move)]

    ends = len(moves)
    rows_held, cols_held = rows + ends * STEPS, cols + 2 * SIDE
    solution, coarse = pl.pallas_call(
        functools.partial(smooth_kernel, ends),
        out_shape=(
            jax.ShapeDtypeStruct((rows, cols, pixels), F32),
            pltpu.VMEM((rows // 2, cols // 2, pixels), BF16),
        ),
        in_specs=[VMEM_SPEC] * 3 + [HBM_SPEC] + [VMEM_SPEC] * (2 + 2 * ends),
        out_specs=(VMEM_SPEC,) * 2,
        scratch_shapes=[
            pltpu.VMEM((rows_held, cols_held, pixels), F32),
            pltpu.VMEM((rows_held, cols_held, pixels), F32),
            pltpu.VMEM((rows_held, cols_held, pixels), F32),
            pltpu.VMEM((2, 3, rows_held + 2, cols_held, pixels), BF16),
            pltpu.VMEM((slots, rows_held, cols_held, LANES), BF16),
            pltpu.VMEM((rows, cols, LANES), F32),
            pltpu.VMEM((cols_held, LANES), F32),
            pltpu.VMEM(stencils.shape, stencils.dtype),
            pltpu.SemaphoreType.DMA,
        ],
        compiler_params=pltpu.CompilerParams(vmem_limit_bytes=32 * 1024 * 1024),
        name="smooth",
    )(right, weight, held, stencil_hbm, even_side, odd_side, *halos)

    inner = max(size for size in range(1, ring + 1) if ring % size == 0 and size * size <= ring)
    outer = ring // inner
    columns = [[i * inner + j for i in range(outer)] for j in range(inner)]
    planes = [[i * inner + j for j in range(inner)] for i in range(outer)]
    block = coarse
    for groups in (columns, planes):
        spread = jnp.broadcast_to(block[None], (len(groups[0]),) + block.shape)
        block = lax.all_to_all(spread, "fcol", 0, 0, axis_index_groups=groups)
    gathered = jnp.transpose(block, (2, 1, 0, 3, 4)).astype(F32)
    return solution, gathered.reshape(rows // 2, ring * (cols // 2), pixels)


def solution(mesh):
    placed = (P("frow", "fcol", None), P("frow", "fcol", None), P(), P("frow", "fcol", None))
    return jax.shard_map(
        body,
        mesh=mesh,
        in_specs=placed,
        out_specs=(P("frow", "fcol", None), P("frow", None, None)),
        check_vma=False,
    )
```

```python
import functools

import jax
import jax.numpy as jnp
from jax import lax
from jax.experimental import pallas as pl
from jax.experimental.pallas import tpu as pltpu
from jax.sharding import PartitionSpec as P

DEG = 3
SWEEPS = 2
STEPS = DEG * SWEEPS
SIDE = 8
LANES = 128

lower_edge = 1.5
upper_edge = 6.0
center = 0.5 * (upper_edge + lower_edge)
half_width = 0.5 * (upper_edge - lower_edge)
weight_middle = 3.75

F32 = jnp.float32
BF16 = jnp.bfloat16
HBM_SPEC = pl.BlockSpec(memory_space=pl.ANY)
VMEM_SPEC = pl.BlockSpec(memory_space=pltpu.VMEM)


def step_factors():
    spread_ratio = center / half_width
    factors = []
    for sweep in range(SWEEPS):
        ratio = 1.0 / spread_ratio
        for step in range(DEG):
            if step < DEG - 1:
                ratio_next = 1.0 / (2.0 * spread_ratio - ratio)
                factors.append((ratio_next * ratio, 2.0 * ratio_next / half_width))
                ratio = ratio_next
            else:
                factors.append((0.0, 1.0 / center))
    return factors


def pack_kernel(right_hbm, weight_hbm, near_hbm, *refs):
    even_ref, odd_ref, whole_ref, held_ref, right_ref, weight_ref, near_ref, arrived = refs
    near_copy = pltpu.make_async_copy(near_hbm, near_ref, arrived.at[2])
    near_copy.start()
    copies = [
        pltpu.make_async_copy(right_hbm, right_ref, arrived.at[0]),
        pltpu.make_async_copy(weight_hbm, weight_ref, arrived.at[1]),
    ]
    for copy in copies:
        copy.start()
    rows, cols, pixels = right_ref.shape
    slots = near_ref.shape[0]
    near_copy.wait()
    flags = jnp.where(near_ref[...] >= 0, 1.0, 0.0).astype(F32).reshape(slots * rows, cols)
    flags = jnp.concatenate([flags, jnp.zeros((slots * rows, LANES - cols), F32)], 1)
    flags = jnp.concatenate([flags, jnp.zeros((LANES - slots * rows, LANES), F32)], 0)
    held_ref[...] = jnp.transpose(flags)[:cols]
    whole_ref[rows, :cols, :LANES] = held_ref[...].astype(BF16)
    parity = lax.rem(lax.axis_index("fcol"), 2)
    starts = [(cols - SIDE) * (1 - parity), (cols - SIDE) * parity]
    parts = [pl.ds(pl.multiple_of(start, SIDE), SIDE) for start in starts]
    for ref, part in zip((even_ref, odd_ref), parts):
        strip = jnp.concatenate([held_ref[part, :], jnp.zeros((SIDE, LANES), F32)], 0)
        ref[rows, :, :LANES] = strip.astype(BF16)
    for copy in copies:
        copy.wait()
    for ref, part in zip((odd_ref, even_ref), parts[::-1]):
        ref[:rows] = jnp.concatenate(
            [right_ref[:, part, :], weight_ref[:, part, :] - weight_middle], 1
        ).astype(BF16)
    whole_ref[:rows, :cols, :] = right_ref[...].astype(BF16)
    whole_ref[:rows, cols:, :] = (weight_ref[...] - weight_middle).astype(BF16)


def row_places(ends, own_rows):
    if ends == 1:
        flip = lax.axis_index("frow")
        place = [row + flip * (own_rows - 1 - 2 * row) for row in range(own_rows)]
        return 2 * own_rows, 0, place, [[(row, own_rows + at) for row, at in enumerate(place)]]
    place = [STEPS + row for row in range(own_rows)]
    above = [(own_rows - STEPS + row, row) for row in range(STEPS)]
    below = [(row, STEPS + own_rows + row) for row in range(STEPS)]
    return own_rows + 2 * STEPS, STEPS, place, [above, below]


def slot_places(ends):
    if ends == 1:
        flip = lax.axis_index("frow")
        return [(slot // 3 + flip * (2 - 2 * (slot // 3))) * 3 + slot % 3 for slot in range(9)]
    return list(range(9))


def prepare_kernel(ends, *refs):
    stencil_hbm, held_ref, right_ref, weight_ref = refs[:4]
    wholes = refs[4 : 4 + ends]
    stencil_ref, mask, residual, weight, arrived = refs[4 + ends :]
    slots = mask.shape[0]
    own_rows, own_cols, pixels = right_ref.shape
    _, _, place, halos = row_places(ends, own_rows)
    slot_place = slot_places(ends)
    copies = [
        pltpu.make_async_copy(
            stencil_hbm.at[pl.ds(slot, 3)],
            stencil_ref.at[pl.ds(slot_place[slot], 3)],
            arrived.at[slot // 3],
        )
        for slot in range(0, slots, 3)
    ]
    for copy in copies:
        copy.start()

    def spread(flags, places):
        for slot in range(slots):
            for row, at in places:
                lane = slot * own_rows + row
                column = jnp.broadcast_to(flags[:, lane : lane + 1], (own_cols, LANES))
                mask[slot_place[slot], at] = column.astype(BF16)

    for row, at in enumerate(place):
        residual[at] = right_ref[row]
        weight[at] = weight_ref[row]
    spread(held_ref[...], list(enumerate(place)))
    for whole_ref, places in zip(wholes, halos):
        for row, at in places:
            strip = whole_ref[row].astype(F32)
            residual[at] = strip[:own_cols]
            weight[at] = strip[own_cols:] + weight_middle
        spread(whole_ref[own_rows, :own_cols, :LANES].astype(F32), places)
    for copy in copies:
        copy.wait()


def smooth_kernel(ends, *refs):
    stencil_ref, mask, residual_ref, weight_ref, odd_ref, even_ref = refs[:6]
    sides = refs[6 : 6 + ends]
    solution_ref, coarse_ref = refs[6 + ends : 8 + ends]
    residual, weight, direction, shifted, side_mask, smoothed, summed = refs[8 + ends :]
    own_rows, own_cols, pixels = solution_ref.shape
    slots = mask.shape[0]
    rows, cols, _ = residual.shape
    held_rows, own_start, place, halos = row_places(ends, own_rows)
    slot_place = slot_places(ends)

    parity = lax.rem(lax.axis_index("fcol"), 2)

    def fill_sides(odd, even, places):
        flags = []
        for piece in (even, odd):
            flags.append(piece[own_rows, :, :LANES].astype(F32)[:SIDE])
        first = parity == 0
        after = jnp.where(first, flags[0], flags[1])
        before = jnp.where(first, flags[1], flags[0])
        flags = jnp.concatenate([after, before], 0)
        for slot in range(slots):
            for row, at in places:
                lane = slot * own_rows + row
                column = jnp.broadcast_to(flags[:, lane : lane + 1], (2 * SIDE, LANES))
                side_mask[slot_place[slot], at] = column.astype(BF16)
        for row, at in places:
            pieces = even[row].astype(F32), odd[row].astype(F32)
            after = jnp.where(first, pieces[0], pieces[1])
            before = jnp.where(first, pieces[1], pieces[0])
            residual[at, own_cols : own_cols + SIDE, :] = after[:SIDE]
            residual[at, own_cols + SIDE :, :] = before[:SIDE]
            weight[at, own_cols : own_cols + SIDE, :] = after[SIDE:] + weight_middle
            weight[at, own_cols + SIDE :, :] = before[SIDE:] + weight_middle

    residual[:, :own_cols, :] = residual_ref[...]
    weight[:, :own_cols, :] = weight_ref[...]
    fill_sides(odd_ref, even_ref, list(enumerate(place)))
    for sides_ref, places in zip(sides, halos):
        fill_sides(sides_ref.at[0], sides_ref.at[1], places)

    def put_direction(slot, start, count, value):
        here = slice(start + 1, start + 1 + count)
        shifted[slot, 1, here] = value.astype(BF16)
        shifted[slot, 0, here] = pltpu.roll(value, 1, 1).astype(BF16)
        shifted[slot, 2, here] = pltpu.roll(value, cols - 1, 1).astype(BF16)

    edge = jnp.zeros((cols, pixels), BF16)
    for slot in range(2):
        for move in range(3):
            shifted[slot, move, 0] = edge
            shifted[slot, move, rows + 1] = edge
    value = residual[...] * (1.0 / center)
    direction[...] = value
    put_direction(0, 0, rows, value)

    own = slice(own_start, own_start + own_rows)
    stencil = stencil_ref[...].reshape(slots * pixels, pixels)
    factors = step_factors()
    for step in range(STEPS):
        now, later = step % 2, 1 - step % 2
        last = step == STEPS - 1
        moved = direction[own, :own_cols, :]
        smoothed[...] = moved if step == 0 else smoothed[...] + moved
        margin = STEPS - 1 - step
        count = own_rows + ends * margin
        start = own_start - (ends - 1) * margin
        width = own_cols if last else cols
        half = (count + 1) // 2
        for base, size in ((start, half), (start + half, count - half)):
            here = slice(base, base + size)
            picked = []
            for slot in range(slots):
                across, along = slot // 3, slot % 3
                keep = mask[slot, here]
                if not last:
                    keep = jnp.concatenate([keep, side_mask[slot, here]], 1)
                source = shifted[now, along, base + across : base + across + size, :width, :]
                picked.append(source[:, :, :LANES] * keep)
                picked.append(source[:, :, LANES:] * keep)
            picked = jnp.concatenate(picked, 2).reshape(size * width, slots * pixels)
            coupled = jnp.dot(picked, stencil, preferred_element_type=F32)
            coupled = coupled.reshape(size, width, pixels)
            moved = direction[here, :width, :]
            left = residual[here, :width, :] - (weight[here, :width, :] * moved + coupled)
            residual[here, :width, :] = left
            if not last:
                a, b = factors[step]
                value = b * left if a == 0.0 else a * moved + b * left
                direction[here, :width, :] = value
                put_direction(later, base, size, value)

    fine = residual[own, :own_cols, :].reshape(own_rows * own_cols, pixels)
    high = fine.astype(BF16)
    low = (fine - high.astype(F32)).astype(BF16)
    quarter = pixels // 4
    from_pixel = lax.broadcasted_iota(jnp.int32, (pixels, LANES), 0) // 4
    to_pixel = lax.broadcasted_iota(jnp.int32, (pixels, LANES), 1)
    adder = jnp.where(from_pixel == to_pixel, 1.0, 0.0).astype(BF16)
    total = jnp.dot(high, adder, preferred_element_type=F32) + jnp.dot(
        low, adder, preferred_element_type=F32
    )
    summed[...] = total.reshape(own_rows, own_cols, LANES)
    for row in range(own_rows // 2):
        pieces = []
        for across in range(2):
            for along in range(2):
                at = place[2 * row + across] - own_start
                piece = summed[at, pl.ds(along, own_cols // 2, stride=2), :]
                pieces.append(piece[:, :quarter])
        coarse_ref[row] = jnp.concatenate(pieces, 1).astype(BF16)
    for row, at in enumerate(place):
        solution_ref[row] = smoothed[at - own_start]


def body(right_side, noise_weight, stencils, neighbours):
    rows, cols, pixels = right_side.shape
    slots = stencils.shape[0]
    pairs, ring = lax.axis_size("frow"), lax.axis_size("fcol")
    swaps = [
        [(i, j) for low in range(first, ring - 1, 2) for i, j in ((low, low + 1), (low + 1, low))]
        for first in (0, 1)
    ]
    near = jnp.transpose(neighbours, (2, 0, 1))
    right_hbm, weight_hbm, near_hbm, stencil_hbm = [
        pltpu.with_memory_space_constraint(array, pltpu.HBM)
        for array in (right_side, noise_weight, near, stencils)
    ]

    even, odd, whole, held, right, weight = pl.pallas_call(
        pack_kernel,
        out_shape=(
            pltpu.VMEM((rows + 1, 2 * SIDE, pixels), BF16),
            pltpu.VMEM((rows + 1, 2 * SIDE, pixels), BF16),
            pltpu.VMEM((rows + 1, 2 * cols, pixels), BF16),
            pltpu.VMEM((cols, LANES), F32),
            pltpu.VMEM((rows, cols, pixels), F32),
            pltpu.VMEM((rows, cols, pixels), F32),
        ),
        in_specs=[HBM_SPEC] * 3,
        out_specs=(VMEM_SPEC,) * 6,
        scratch_shapes=[
            pltpu.VMEM((slots, rows, cols), jnp.int32),
            pltpu.SemaphoreType.DMA((3,)),
        ],
        compiler_params=pltpu.CompilerParams(vmem_limit_bytes=8 * 1024 * 1024),
        name="pack",
    )(right_hbm, weight_hbm, near_hbm)

    odd_side = lax.ppermute(odd, "fcol", swaps[1])
    even_side = lax.ppermute(even, "fcol", swaps[0])
    if pairs == 2:
        moves = [[(0, 1), (1, 0)]]
    else:
        moves = [
            [(i, i + 1) for i in range(pairs - 1)],
            [(i + 1, i) for i in range(pairs - 1)],
        ]
    wholes = [lax.ppermute(whole, "frow", move) for move in moves]
    sides = jnp.stack([odd_side, even_side])
    sides_held = [lax.ppermute(sides, "frow", move) for move in moves]

    ends = len(moves)
    cols_held = cols + 2 * SIDE
    rows_held = 2 * rows if ends == 1 else rows + 2 * STEPS
    held_types = (
        pltpu.VMEM((slots, rows_held, cols, LANES), BF16),
        pltpu.VMEM((rows_held, cols, pixels), F32),
        pltpu.VMEM((rows_held, cols, pixels), F32),
    )
    stencil, mask, residual, weight = pl.pallas_call(
        functools.partial(prepare_kernel, ends),
        out_shape=(pltpu.VMEM(stencils.shape, stencils.dtype),) + held_types,
        in_specs=[HBM_SPEC] + [VMEM_SPEC] * (3 + ends),
        out_specs=(VMEM_SPEC,) * 4,
        scratch_shapes=[pltpu.SemaphoreType.DMA((3,))],
        compiler_params=pltpu.CompilerParams(vmem_limit_bytes=8 * 1024 * 1024),
        cost_estimate=pl.CostEstimate(flops=0, bytes_accessed=6000000, transcendentals=0),
        name="prepare",
    )(stencil_hbm, held, right, weight, *wholes)

    solution, coarse = pl.pallas_call(
        functools.partial(smooth_kernel, ends),
        out_shape=(
            jax.ShapeDtypeStruct((rows, cols, pixels), F32),
            pltpu.VMEM((rows // 2, cols // 2, pixels), BF16),
        ),
        in_specs=[VMEM_SPEC] * (6 + ends),
        out_specs=(VMEM_SPEC,) * 2,
        scratch_shapes=[
            pltpu.VMEM((rows_held, cols_held, pixels), F32),
            pltpu.VMEM((rows_held, cols_held, pixels), F32),
            pltpu.VMEM((rows_held, cols_held, pixels), F32),
            pltpu.VMEM((2, 3, rows_held + 2, cols_held, pixels), BF16),
            pltpu.VMEM((slots, rows_held, 2 * SIDE, LANES), BF16),
            pltpu.VMEM((rows, cols, pixels), F32),
            pltpu.VMEM((rows, cols, LANES), F32),
        ],
        compiler_params=pltpu.CompilerParams(vmem_limit_bytes=24 * 1024 * 1024),
        name="smooth",
    )(stencil, mask, residual, weight, odd_side, even_side, *sides_held)

    inner = max(size for size in range(1, ring + 1) if ring % size == 0 and size * size <= ring)
    outer = ring // inner
    columns = [[i * inner + j for i in range(outer)] for j in range(inner)]
    planes = [[i * inner + j for j in range(inner)] for i in range(outer)]
    block = coarse
    for groups in (columns, planes):
        spread = jnp.broadcast_to(block[None], (len(groups[0]),) + block.shape)
        block = lax.all_to_all(spread, "fcol", 0, 0, axis_index_groups=groups)
    gathered = jnp.transpose(block, (2, 1, 0, 3, 4)).astype(F32)
    return solution, gathered.reshape(rows // 2, ring * (cols // 2), pixels)


def solution(mesh):
    placed = (P("frow", "fcol", None), P("frow", "fcol", None), P(), P("frow", "fcol", None))
    return jax.shard_map(
        body,
        mesh=mesh,
        in_specs=placed,
        out_specs=(P("frow", "fcol", None), P("frow", None, None)),
        check_vma=False,
    )
```

```python
import functools

import jax
import jax.numpy as jnp
from jax import lax
from jax.experimental import pallas as pl
from jax.experimental.pallas import tpu as pltpu
from jax.sharding import PartitionSpec as P

DEG = 3
SWEEPS = 2
STEPS = DEG * SWEEPS
SIDE = 8
LANES = 128

lower_edge = 1.5
upper_edge = 6.0
center = 0.5 * (upper_edge + lower_edge)
half_width = 0.5 * (upper_edge - lower_edge)
weight_middle = 3.75

F32 = jnp.float32
BF16 = jnp.bfloat16
HBM_SPEC = pl.BlockSpec(memory_space=pl.ANY)
VMEM_SPEC = pl.BlockSpec(memory_space=pltpu.VMEM)


def step_factors():
    spread_ratio = center / half_width
    factors = []
    for sweep in range(SWEEPS):
        ratio = 1.0 / spread_ratio
        for step in range(DEG):
            if step < DEG - 1:
                ratio_next = 1.0 / (2.0 * spread_ratio - ratio)
                factors.append((ratio_next * ratio, 2.0 * ratio_next / half_width))
                ratio = ratio_next
            else:
                factors.append((0.0, 1.0 / center))
    return factors


def row_places(ends, own_rows):
    if ends == 1:
        flip = lax.axis_index("frow")
        place = [row + flip * (own_rows - 1 - 2 * row) for row in range(own_rows)]
        return place, [list(enumerate(place))], 0
    above = [(own_rows - STEPS + row, row) for row in range(STEPS)]
    below = [(row, row) for row in range(STEPS)]
    return list(range(own_rows)), [above, below], 1


def slot_places(ends, slots):
    if ends == 1:
        flip = lax.axis_index("frow")
        return [(slot // 3 + flip * (2 - 2 * (slot // 3))) * 3 + slot % 3 for slot in range(slots)]
    return list(range(slots))


def spread_flags(ends, mask, flags, own_rows, places):
    slots, _, cols, _ = mask.shape
    slot_place = slot_places(ends, slots)
    for slot in range(slots):
        for row, at in places:
            lane = slot * own_rows + row
            column = jnp.broadcast_to(flags[:, lane : lane + 1], (cols, LANES))
            mask[slot_place[slot], at] = column.astype(BF16)


def edge_kernel(right_hbm, weight_hbm, near_hbm, *refs):
    odd_ref, even_ref, held_ref, strips, near_ref, arrived = refs
    slots, rows, cols = near_ref.shape
    copies = [pltpu.make_async_copy(near_hbm, near_ref, arrived.at[4])]
    for end, start in enumerate((0, cols - SIDE)):
        for kind, source in enumerate((right_hbm, weight_hbm)):
            copies.append(
                pltpu.make_async_copy(
                    source.at[:, pl.ds(start, SIDE)],
                    strips.at[end, kind],
                    arrived.at[2 * end + kind],
                )
            )
    for copy in copies:
        copy.start()
    copies[0].wait()
    flags = jnp.where(near_ref[...] >= 0, 1.0, 0.0).astype(F32).reshape(slots * rows, cols)
    flags = jnp.concatenate([flags, jnp.zeros((slots * rows, LANES - cols), F32)], 1)
    flags = jnp.concatenate([flags, jnp.zeros((LANES - slots * rows, LANES), F32)], 0)
    turned = jnp.transpose(flags)[:cols]
    held_ref[...] = turned
    for copy in copies[1:]:
        copy.wait()
    parity = lax.rem(lax.axis_index("fcol"), 2)
    flags = [turned[:SIDE], turned[cols - SIDE :]]
    for ref, end in ((odd_ref, parity), (even_ref, 1 - parity)):
        ref[:rows] = jnp.concatenate([strips[end, 0], strips[end, 1] - weight_middle], 1).astype(
            BF16
        )
        strip = jnp.where(end == 0, flags[0], flags[1])
        strip = jnp.concatenate([strip, jnp.zeros((SIDE, LANES), F32)], 0)
        ref[rows, :, :LANES] = strip.astype(BF16)


def own_kernel(ends, stencil_hbm, right_hbm, weight_hbm, held_ref, *refs):
    whole_ref, stencil_ref, mask, residual, weight, arrived = refs
    slots = mask.shape[0]
    own_rows, own_cols, _ = residual.shape
    place, _, _ = row_places(ends, own_rows)
    slot_place = slot_places(ends, slots)
    copies = []
    for row in range(own_rows):
        for source, target in ((right_hbm, residual), (weight_hbm, weight)):
            copies.append(
                pltpu.make_async_copy(
                    source.at[row], target.at[place[row]], arrived.at[3 + len(copies)]
                )
            )
    stencil_copies = [
        pltpu.make_async_copy(
            stencil_hbm.at[pl.ds(slot, 3)],
            stencil_ref.at[pl.ds(slot_place[slot], 3)],
            arrived.at[slot // 3],
        )
        for slot in range(0, slots, 3)
    ]
    for copy in copies + stencil_copies:
        copy.start()
    flags = held_ref[...]
    spread_flags(ends, mask, flags, own_rows, list(enumerate(place)))
    whole_ref[own_rows, :own_cols, :LANES] = flags.astype(BF16)
    for copy in copies:
        copy.wait()
    for row, at in enumerate(place):
        whole_ref[row, :own_cols] = residual[at].astype(BF16)
        whole_ref[row, own_cols:] = (weight[at] - weight_middle).astype(BF16)
    for copy in stencil_copies:
        copy.wait()


def rows_kernel(ends, *refs):
    for index in range(ends):
        whole_ref = refs[index]
        mask, residual, weight = refs[ends + 3 * index : ends + 3 * index + 3]
        own_rows = whole_ref.shape[0] - 1
        own_cols = residual.shape[1]
        places = row_places(ends, own_rows)[1][index]
        for row, at in places:
            strip = whole_ref[row].astype(F32)
            residual[at] = strip[:own_cols]
            weight[at] = strip[own_cols:] + weight_middle
        flags = whole_ref[own_rows, :own_cols, :LANES].astype(F32)
        spread_flags(ends, mask, flags, own_rows, places)


def smooth_kernel(ends, *refs):
    stencil_ref, odd_ref, even_ref = refs[:3]
    sides = refs[3 : 3 + ends]
    own_block = refs[3 + ends : 6 + ends]
    halo_blocks = [refs[6 + ends + 3 * i : 9 + ends + 3 * i] for i in range(ends)]
    solution_ref, coarse_ref = refs[6 + 4 * ends : 8 + 4 * ends]
    residual, weight, direction, shifted, side_mask, smoothed, summed = refs[8 + 4 * ends :]
    own_rows, own_cols, pixels = solution_ref.shape
    slots = side_mask.shape[0]
    rows, cols, _ = residual.shape
    place, halos, ahead = row_places(ends, own_rows)
    blocks = halo_blocks[:ahead] + [own_block] + halo_blocks[ahead:]
    bases = [0]
    for block in blocks:
        bases.append(bases[-1] + block[1].shape[0])
    own_start = bases[ahead]

    def flags_of(slot, first, last):
        pieces = []
        for base, block in zip(bases, blocks):
            low, high = max(first - base, 0), min(last - base, block[1].shape[0])
            if low < high:
                pieces.append(block[0][slot, low:high])
        return pieces[0] if len(pieces) == 1 else jnp.concatenate(pieces, 0)

    first_of_even = lax.rem(lax.axis_index("fcol"), 2) == 0

    def fill(base, block, odd, even, places):
        here = slice(base, base + block[1].shape[0])
        residual[here, :own_cols, :] = block[1][...]
        weight[here, :own_cols, :] = block[2][...]

        def in_order(odd_piece, even_piece):
            after = jnp.where(first_of_even, even_piece, odd_piece)
            before = jnp.where(first_of_even, odd_piece, even_piece)
            return after, before

        flags = in_order(*(piece[own_rows, :, :LANES].astype(F32)[:SIDE] for piece in (odd, even)))
        places = [(row, base + at) for row, at in places]
        spread_flags(ends, side_mask, jnp.concatenate(flags, 0), own_rows, places)
        for row, at in places:
            after, before = in_order(odd[row].astype(F32), even[row].astype(F32))
            residual[at, own_cols : own_cols + SIDE, :] = after[:SIDE]
            residual[at, own_cols + SIDE :, :] = before[:SIDE]
            weight[at, own_cols : own_cols + SIDE, :] = after[SIDE:] + weight_middle
            weight[at, own_cols + SIDE :, :] = before[SIDE:] + weight_middle

    fill(own_start, own_block, odd_ref, even_ref, list(enumerate(place)))
    halo_bases = bases[:ahead] + bases[ahead + 1 : -1]
    for base, block, sides_ref, places in zip(halo_bases, halo_blocks, sides, halos):
        fill(base, block, sides_ref.at[0], sides_ref.at[1], places)

    def put_direction(slot, start, count, value):
        here = slice(start + 1, start + 1 + count)
        shifted[slot, 1, here] = value.astype(BF16)
        shifted[slot, 0, here] = pltpu.roll(value, 1, 1).astype(BF16)
        shifted[slot, 2, here] = pltpu.roll(value, cols - 1, 1).astype(BF16)

    edge = jnp.zeros((cols, pixels), BF16)
    for slot in range(2):
        for move in range(3):
            shifted[slot, move, 0] = edge
            shifted[slot, move, rows + 1] = edge
    value = residual[...] * (1.0 / center)
    direction[...] = value
    put_direction(0, 0, rows, value)

    own = slice(own_start, own_start + own_rows)
    stencil = stencil_ref[...].reshape(slots * pixels, pixels)
    factors = step_factors()
    for step in range(STEPS):
        now, later = step % 2, 1 - step % 2
        last = step == STEPS - 1
        moved = direction[own, :own_cols, :]
        smoothed[...] = moved if step == 0 else smoothed[...] + moved
        margin = STEPS - 1 - step
        count = own_rows + ends * margin
        start = own_start - (ends - 1) * margin
        width = own_cols if last else cols
        half = (count + 1) // 2
        for base, size in ((start, half), (start + half, count - half)):
            here = slice(base, base + size)
            picked = []
            for slot in range(slots):
                across, along = slot // 3, slot % 3
                keep = flags_of(slot, base, base + size)
                if not last:
                    keep = jnp.concatenate([keep, side_mask[slot, here]], 1)
                source = shifted[now, along, base + across : base + across + size, :width, :]
                picked.append(source[:, :, :LANES] * keep)
                picked.append(source[:, :, LANES:] * keep)
            picked = jnp.concatenate(picked, 2).reshape(size * width, slots * pixels)
            coupled = jnp.dot(picked, stencil, preferred_element_type=F32)
            coupled = coupled.reshape(size, width, pixels)
            moved = direction[here, :width, :]
            left = residual[here, :width, :] - (weight[here, :width, :] * moved + coupled)
            residual[here, :width, :] = left
            if not last:
                a, b = factors[step]
                value = b * left if a == 0.0 else a * moved + b * left
                direction[here, :width, :] = value
                put_direction(later, base, size, value)

    fine = residual[own, :own_cols, :].reshape(own_rows * own_cols, pixels)
    high = fine.astype(BF16)
    low = (fine - high.astype(F32)).astype(BF16)
    quarter = pixels // 4
    from_pixel = lax.broadcasted_iota(jnp.int32, (pixels, LANES), 0) // 4
    to_pixel = lax.broadcasted_iota(jnp.int32, (pixels, LANES), 1)
    adder = jnp.where(from_pixel == to_pixel, 1.0, 0.0).astype(BF16)
    total = jnp.dot(high, adder, preferred_element_type=F32) + jnp.dot(
        low, adder, preferred_element_type=F32
    )
    summed[...] = total.reshape(own_rows, own_cols, LANES)
    for row in range(own_rows // 2):
        pieces = []
        for across in range(2):
            for along in range(2):
                at = place[2 * row + across]
                piece = summed[at, pl.ds(along, own_cols // 2, stride=2), :]
                pieces.append(piece[:, :quarter])
        coarse_ref[row] = jnp.concatenate(pieces, 1).astype(BF16)
    for row, at in enumerate(place):
        solution_ref[row] = smoothed[at]


def widen_kernel(block_ref, out_hbm, wide, sent):
    rows, outer, inner, _, _ = wide.shape
    copies = []
    for row in range(rows):
        for i in range(outer):
            for j in range(inner):
                wide[row, i, j] = block_ref[j, i, row].astype(F32)
        copies.append(pltpu.make_async_copy(wide.at[row], out_hbm.at[row], sent.at[row]))
        copies[-1].start()
    for copy in copies:
        copy.wait()


def body(right_side, noise_weight, stencils, neighbours):
    rows, cols, pixels = right_side.shape
    slots = stencils.shape[0]
    pairs, ring = lax.axis_size("frow"), lax.axis_size("fcol")
    swaps = [
        [(i, j) for low in range(first, ring - 1, 2) for i, j in ((low, low + 1), (low + 1, low))]
        for first in (0, 1)
    ]
    near = jnp.transpose(neighbours, (2, 0, 1))
    right_hbm, weight_hbm, near_hbm, stencil_hbm = [
        pltpu.with_memory_space_constraint(array, pltpu.HBM)
        for array in (right_side, noise_weight, near, stencils)
    ]
    small = pltpu.CompilerParams(vmem_limit_bytes=8 * 1024 * 1024)

    side = pltpu.VMEM((rows + 1, 2 * SIDE, pixels), BF16)
    odd, even, held = pl.pallas_call(
        edge_kernel,
        out_shape=(side, side, pltpu.VMEM((cols, LANES), F32)),
        in_specs=[HBM_SPEC] * 3,
        out_specs=(VMEM_SPEC,) * 3,
        scratch_shapes=[
            pltpu.VMEM((2, 2, rows, SIDE, pixels), F32),
            pltpu.VMEM((slots, rows, cols), jnp.int32),
            pltpu.SemaphoreType.DMA((5,)),
        ],
        compiler_params=small,
        name="edges",
    )(right_hbm, weight_hbm, near_hbm)

    odd_side = lax.ppermute(odd, "fcol", swaps[1])
    even_side = lax.ppermute(even, "fcol", swaps[0])
    if pairs == 2:
        moves = [[(0, 1), (1, 0)]]
    else:
        moves = [
            [(i, i + 1) for i in range(pairs - 1)],
            [(i + 1, i) for i in range(pairs - 1)],
        ]
    ends = len(moves)

    def block_types(count):
        return (
            pltpu.VMEM((slots, count, cols, LANES), BF16),
            pltpu.VMEM((count, cols, pixels), F32),
            pltpu.VMEM((count, cols, pixels), F32),
        )

    whole, stencil, *own_block = pl.pallas_call(
        functools.partial(own_kernel, ends),
        out_shape=(
            pltpu.VMEM((rows + 1, 2 * cols, pixels), BF16),
            pltpu.VMEM(stencils.shape, stencils.dtype),
        )
        + block_types(rows),
        in_specs=[HBM_SPEC] * 3 + [VMEM_SPEC],
        out_specs=(VMEM_SPEC,) * 5,
        scratch_shapes=[pltpu.SemaphoreType.DMA((3 + 2 * rows,))],
        compiler_params=small,
        cost_estimate=pl.CostEstimate(flops=0, bytes_accessed=6000000, transcendentals=0),
        name="own",
    )(stencil_hbm, right_hbm, weight_hbm, held)

    wholes = [lax.ppermute(whole, "frow", move) for move in moves]
    sides = jnp.stack([odd_side, even_side])
    sides_held = [lax.ppermute(sides, "frow", move) for move in moves]
    far_rows = rows if ends == 1 else STEPS
    halo_blocks = pl.pallas_call(
        functools.partial(rows_kernel, ends),
        out_shape=block_types(far_rows) * ends,
        in_specs=[VMEM_SPEC] * ends,
        out_specs=(VMEM_SPEC,) * (3 * ends),
        compiler_params=small,
        cost_estimate=pl.CostEstimate(flops=0, bytes_accessed=4000000, transcendentals=0),
        name="rows",
    )(*wholes)

    cols_held = cols + 2 * SIDE
    rows_held = rows + ends * far_rows
    solution, coarse = pl.pallas_call(
        functools.partial(smooth_kernel, ends),
        out_shape=(
            jax.ShapeDtypeStruct((rows, cols, pixels), F32),
            pltpu.VMEM((rows // 2, cols // 2, pixels), BF16),
        ),
        in_specs=[VMEM_SPEC] * (6 + 4 * ends),
        out_specs=(VMEM_SPEC,) * 2,
        scratch_shapes=[
            pltpu.VMEM((rows_held, cols_held, pixels), F32),
            pltpu.VMEM((rows_held, cols_held, pixels), F32),
            pltpu.VMEM((rows_held, cols_held, pixels), F32),
            pltpu.VMEM((2, 3, rows_held + 2, cols_held, pixels), BF16),
            pltpu.VMEM((slots, rows_held, 2 * SIDE, LANES), BF16),
            pltpu.VMEM((rows, cols, pixels), F32),
            pltpu.VMEM((rows, cols, LANES), F32),
        ],
        compiler_params=pltpu.CompilerParams(vmem_limit_bytes=24 * 1024 * 1024),
        name="smooth",
    )(stencil, odd_side, even_side, *sides_held, *own_block, *halo_blocks)

    inner = max(size for size in range(1, ring + 1) if ring % size == 0 and size * size <= ring)
    outer = ring // inner
    columns = [[i * inner + j for i in range(outer)] for j in range(inner)]
    planes = [[i * inner + j for j in range(inner)] for i in range(outer)]
    block = coarse
    for groups in (columns, planes):
        spread = jnp.broadcast_to(block[None], (len(groups[0]),) + block.shape)
        block = lax.all_to_all(spread, "fcol", 0, 0, axis_index_groups=groups)
    widened = (rows // 2, outer, inner, cols // 2, pixels)
    gathered = pl.pallas_call(
        widen_kernel,
        out_shape=jax.ShapeDtypeStruct(widened, F32),
        in_specs=[VMEM_SPEC],
        out_specs=HBM_SPEC,
        scratch_shapes=[pltpu.VMEM(widened, F32), pltpu.SemaphoreType.DMA((rows // 2,))],
        compiler_params=small,
        name="widen",
    )(block)
    return solution, gathered.reshape(rows // 2, ring * (cols // 2), pixels)


def solution(mesh):
    placed = (P("frow", "fcol", None), P("frow", "fcol", None), P(), P("frow", "fcol", None))
    return jax.shard_map(
        body,
        mesh=mesh,
        in_specs=placed,
        out_specs=(P("frow", "fcol", None), P("frow", None, None)),
        check_vma=False,
    )
```

```python
import functools

import jax
import jax.numpy as jnp
from jax import lax
from jax.experimental import pallas as pl
from jax.experimental.pallas import tpu as pltpu
from jax.sharding import PartitionSpec as P

DEG = 3
SWEEPS = 2
STEPS = DEG * SWEEPS
SIDE = 8
LANES = 128

lower_edge = 1.5
upper_edge = 6.0
center = 0.5 * (upper_edge + lower_edge)
half_width = 0.5 * (upper_edge - lower_edge)
weight_middle = 3.75

F32 = jnp.float32
BF16 = jnp.bfloat16
HBM_SPEC = pl.BlockSpec(memory_space=pl.ANY)
VMEM_SPEC = pl.BlockSpec(memory_space=pltpu.VMEM)


def step_factors():
    spread_ratio = center / half_width
    factors = []
    for sweep in range(SWEEPS):
        ratio = 1.0 / spread_ratio
        for step in range(DEG):
            if step < DEG - 1:
                ratio_next = 1.0 / (2.0 * spread_ratio - ratio)
                factors.append((ratio_next * ratio, 2.0 * ratio_next / half_width))
                ratio = ratio_next
            else:
                factors.append((0.0, 1.0 / center))
    return factors


def row_places(ends, own_rows):
    if ends == 1:
        flip = lax.axis_index("frow")
        place = [row + flip * (own_rows - 1 - 2 * row) for row in range(own_rows)]
        return place, [list(enumerate(place))], 0
    above = [(own_rows - STEPS + row, row) for row in range(STEPS)]
    below = [(row, row) for row in range(STEPS)]
    return list(range(own_rows)), [above, below], 1


def slot_places(ends, slots):
    if ends == 1:
        flip = lax.axis_index("frow")
        return [(slot // 3 + flip * (2 - 2 * (slot // 3))) * 3 + slot % 3 for slot in range(slots)]
    return list(range(slots))


def spread_flags(ends, mask, flags, own_rows, places):
    slots, _, cols, _ = mask.shape
    slot_place = slot_places(ends, slots)
    for slot in range(slots):
        for row, at in places:
            lane = slot * own_rows + row
            column = jnp.broadcast_to(flags[:, lane : lane + 1], (cols, LANES))
            mask[slot_place[slot], at] = column.astype(BF16)


def edge_kernel(right_hbm, weight_hbm, near_hbm, *refs):
    odd_ref, even_ref, held_ref, strips, near_ref, arrived = refs
    slots, rows, cols = near_ref.shape
    copies = [pltpu.make_async_copy(near_hbm, near_ref, arrived.at[4])]
    for end, start in enumerate((0, cols - SIDE)):
        for kind, source in enumerate((right_hbm, weight_hbm)):
            copies.append(
                pltpu.make_async_copy(
                    source.at[:, pl.ds(start, SIDE)],
                    strips.at[end, kind],
                    arrived.at[2 * end + kind],
                )
            )
    for copy in copies:
        copy.start()
    copies[0].wait()
    flags = jnp.where(near_ref[...] >= 0, 1.0, 0.0).astype(F32).reshape(slots * rows, cols)
    flags = jnp.concatenate([flags, jnp.zeros((slots * rows, LANES - cols), F32)], 1)
    flags = jnp.concatenate([flags, jnp.zeros((LANES - slots * rows, LANES), F32)], 0)
    turned = jnp.transpose(flags)[:cols]
    held_ref[...] = turned
    for copy in copies[1:]:
        copy.wait()
    parity = lax.rem(lax.axis_index("fcol"), 2)
    flags = [turned[:SIDE], turned[cols - SIDE :]]
    for ref, end in ((odd_ref, parity), (even_ref, 1 - parity)):
        ref[:rows] = jnp.concatenate([strips[end, 0], strips[end, 1] - weight_middle], 1).astype(
            BF16
        )
        strip = jnp.where(end == 0, flags[0], flags[1])
        strip = jnp.concatenate([strip, jnp.zeros((SIDE, LANES), F32)], 0)
        ref[rows, :, :LANES] = strip.astype(BF16)


def own_kernel(ends, stencil_hbm, right_hbm, weight_hbm, held_ref, *refs):
    whole_ref, stencil_ref, mask, residual, weight, arrived = refs
    slots = mask.shape[0]
    own_rows, own_cols, _ = residual.shape
    place, _, _ = row_places(ends, own_rows)
    slot_place = slot_places(ends, slots)
    copies = []
    for row in range(own_rows):
        for source, target in ((right_hbm, residual), (weight_hbm, weight)):
            copies.append(
                pltpu.make_async_copy(
                    source.at[row], target.at[place[row]], arrived.at[3 + len(copies)]
                )
            )
    stencil_copies = [
        pltpu.make_async_copy(
            stencil_hbm.at[pl.ds(slot, 3)],
            stencil_ref.at[pl.ds(slot_place[slot], 3)],
            arrived.at[slot // 3],
        )
        for slot in range(0, slots, 3)
    ]
    for copy in copies + stencil_copies:
        copy.start()
    flags = held_ref[...]
    spread_flags(ends, mask, flags, own_rows, list(enumerate(place)))
    whole_ref[own_rows, :own_cols, :LANES] = flags.astype(BF16)
    for copy in copies:
        copy.wait()
    for row, at in enumerate(place):
        whole_ref[row, :own_cols] = residual[at].astype(BF16)
        whole_ref[row, own_cols:] = (weight[at] - weight_middle).astype(BF16)
    for copy in stencil_copies:
        copy.wait()


def rows_kernel(ends, *refs):
    for index in range(ends):
        whole_ref = refs[index]
        mask, residual, weight = refs[ends + 3 * index : ends + 3 * index + 3]
        own_rows = whole_ref.shape[0] - 1
        own_cols = residual.shape[1]
        places = row_places(ends, own_rows)[1][index]
        for row, at in places:
            strip = whole_ref[row].astype(F32)
            residual[at] = strip[:own_cols]
            weight[at] = strip[own_cols:] + weight_middle
        flags = whole_ref[own_rows, :own_cols, :LANES].astype(F32)
        spread_flags(ends, mask, flags, own_rows, places)


def smooth_kernel(ends, *refs):
    stencil_ref, odd_ref, even_ref = refs[:3]
    sides = refs[3 : 3 + ends]
    own_block = refs[3 + ends : 6 + ends]
    halo_blocks = [refs[6 + ends + 3 * i : 9 + ends + 3 * i] for i in range(ends)]
    solution_ref, coarse_ref = refs[6 + 4 * ends : 8 + 4 * ends]
    residual, weight, direction, shifted, side_mask, smoothed, summed = refs[8 + 4 * ends :]
    own_rows, own_cols, pixels = solution_ref.shape
    slots = side_mask.shape[0]
    rows, cols, _ = residual.shape
    place, halos, ahead = row_places(ends, own_rows)
    blocks = halo_blocks[:ahead] + [own_block] + halo_blocks[ahead:]
    bases = [0]
    for block in blocks:
        bases.append(bases[-1] + block[1].shape[0])
    own_start = bases[ahead]

    def flags_of(slot, first, last):
        pieces = []
        for base, block in zip(bases, blocks):
            low, high = max(first - base, 0), min(last - base, block[1].shape[0])
            if low < high:
                pieces.append(block[0][slot, low:high])
        return pieces[0] if len(pieces) == 1 else jnp.concatenate(pieces, 0)

    first_of_even = lax.rem(lax.axis_index("fcol"), 2) == 0

    def fill(base, block, odd, even, places):
        here = slice(base, base + block[1].shape[0])
        residual[here, :own_cols, :] = block[1][...]
        weight[here, :own_cols, :] = block[2][...]

        def in_order(odd_piece, even_piece):
            after = jnp.where(first_of_even, even_piece, odd_piece)
            before = jnp.where(first_of_even, odd_piece, even_piece)
            return after, before

        flags = in_order(*(piece[own_rows, :, :LANES].astype(F32)[:SIDE] for piece in (odd, even)))
        places = [(row, base + at) for row, at in places]
        spread_flags(ends, side_mask, jnp.concatenate(flags, 0), own_rows, places)
        for row, at in places:
            after, before = in_order(odd[row].astype(F32), even[row].astype(F32))
            residual[at, own_cols : own_cols + SIDE, :] = after[:SIDE]
            residual[at, own_cols + SIDE :, :] = before[:SIDE]
            weight[at, own_cols : own_cols + SIDE, :] = after[SIDE:] + weight_middle
            weight[at, own_cols + SIDE :, :] = before[SIDE:] + weight_middle

    fill(own_start, own_block, odd_ref, even_ref, list(enumerate(place)))
    halo_bases = bases[:ahead] + bases[ahead + 1 : -1]
    for base, block, sides_ref, places in zip(halo_bases, halo_blocks, sides, halos):
        fill(base, block, sides_ref.at[0], sides_ref.at[1], places)

    def put_direction(slot, start, count, value):
        here = slice(start + 1, start + 1 + count)
        shifted[slot, 1, here] = value.astype(BF16)
        shifted[slot, 0, here] = pltpu.roll(value, 1, 1).astype(BF16)
        shifted[slot, 2, here] = pltpu.roll(value, cols - 1, 1).astype(BF16)

    edge = jnp.zeros((cols, pixels), BF16)
    for slot in range(2):
        for move in range(3):
            shifted[slot, move, 0] = edge
            shifted[slot, move, rows + 1] = edge
    value = residual[...] * (1.0 / center)
    direction[...] = value
    put_direction(0, 0, rows, value)

    own = slice(own_start, own_start + own_rows)
    stencil = stencil_ref[...].reshape(slots * pixels, pixels)
    factors = step_factors()
    for step in range(STEPS):
        now, later = step % 2, 1 - step % 2
        last = step == STEPS - 1
        moved = direction[own, :own_cols, :]
        smoothed[...] = moved if step == 0 else smoothed[...] + moved
        margin = STEPS - 1 - step
        count = own_rows + ends * margin
        start = own_start - (ends - 1) * margin
        width = own_cols if last else cols
        half = (count + 1) // 2
        for base, size in ((start, half), (start + half, count - half)):
            here = slice(base, base + size)
            picked = []
            for slot in range(slots):
                across, along = slot // 3, slot % 3
                keep = flags_of(slot, base, base + size)
                if not last:
                    keep = jnp.concatenate([keep, side_mask[slot, here]], 1)
                source = shifted[now, along, base + across : base + across + size, :width, :]
                picked.append(source[:, :, :LANES] * keep)
                picked.append(source[:, :, LANES:] * keep)
            picked = jnp.concatenate(picked, 2).reshape(size * width, slots * pixels)
            coupled = jnp.dot(picked, stencil, preferred_element_type=F32)
            coupled = coupled.reshape(size, width, pixels)
            moved = direction[here, :width, :]
            left = residual[here, :width, :] - (weight[here, :width, :] * moved + coupled)
            residual[here, :width, :] = left
            if not last:
                a, b = factors[step]
                value = b * left if a == 0.0 else a * moved + b * left
                direction[here, :width, :] = value
                put_direction(later, base, size, value)

    fine = residual[own, :own_cols, :].reshape(own_rows * own_cols, pixels)
    high = fine.astype(BF16)
    low = (fine - high.astype(F32)).astype(BF16)
    quarter = pixels // 4
    from_pixel = lax.broadcasted_iota(jnp.int32, (pixels, LANES), 0) // 4
    to_pixel = lax.broadcasted_iota(jnp.int32, (pixels, LANES), 1)
    adder = jnp.where(from_pixel == to_pixel, 1.0, 0.0).astype(BF16)
    total = jnp.dot(high, adder, preferred_element_type=F32) + jnp.dot(
        low, adder, preferred_element_type=F32
    )
    summed[...] = total.reshape(own_rows, own_cols, LANES)
    for row in range(own_rows // 2):
        pieces = []
        for across in range(2):
            for along in range(2):
                at = place[2 * row + across]
                piece = summed[at, pl.ds(along, own_cols // 2, stride=2), :]
                pieces.append(piece[:, :quarter])
        coarse_ref[row] = jnp.concatenate(pieces, 1).astype(BF16)
    for row, at in enumerate(place):
        solution_ref[row] = smoothed[at]


def widen_kernel(block_ref, out_hbm, wide, sent):
    rows, ring, _, _ = wide.shape
    copies = []
    for row in range(rows):
        for i in range(ring):
            wide[row, i] = block_ref[i, row].astype(F32)
        copies.append(pltpu.make_async_copy(wide.at[row], out_hbm.at[row], sent.at[row]))
        copies[-1].start()
    for copy in copies:
        copy.wait()


def body(right_side, noise_weight, stencils, neighbours):
    rows, cols, pixels = right_side.shape
    slots = stencils.shape[0]
    pairs, ring = lax.axis_size("frow"), lax.axis_size("fcol")
    swaps = [
        [(i, j) for low in range(first, ring - 1, 2) for i, j in ((low, low + 1), (low + 1, low))]
        for first in (0, 1)
    ]
    near = jnp.transpose(neighbours, (2, 0, 1))
    right_hbm, weight_hbm, near_hbm, stencil_hbm = [
        pltpu.with_memory_space_constraint(array, pltpu.HBM)
        for array in (right_side, noise_weight, near, stencils)
    ]
    small = pltpu.CompilerParams(vmem_limit_bytes=8 * 1024 * 1024)

    side = pltpu.VMEM((rows + 1, 2 * SIDE, pixels), BF16)
    odd, even, held = pl.pallas_call(
        edge_kernel,
        out_shape=(side, side, pltpu.VMEM((cols, LANES), F32)),
        in_specs=[HBM_SPEC] * 3,
        out_specs=(VMEM_SPEC,) * 3,
        scratch_shapes=[
            pltpu.VMEM((2, 2, rows, SIDE, pixels), F32),
            pltpu.VMEM((slots, rows, cols), jnp.int32),
            pltpu.SemaphoreType.DMA((5,)),
        ],
        compiler_params=small,
        name="edges",
    )(right_hbm, weight_hbm, near_hbm)

    odd_side = lax.ppermute(odd, "fcol", swaps[1])
    even_side = lax.ppermute(even, "fcol", swaps[0])
    if pairs == 2:
        moves = [[(0, 1), (1, 0)]]
    else:
        moves = [
            [(i, i + 1) for i in range(pairs - 1)],
            [(i + 1, i) for i in range(pairs - 1)],
        ]
    ends = len(moves)

    def block_types(count):
        return (
            pltpu.VMEM((slots, count, cols, LANES), BF16),
            pltpu.VMEM((count, cols, pixels), F32),
            pltpu.VMEM((count, cols, pixels), F32),
        )

    whole, stencil, *own_block = pl.pallas_call(
        functools.partial(own_kernel, ends),
        out_shape=(
            pltpu.VMEM((rows + 1, 2 * cols, pixels), BF16),
            pltpu.VMEM(stencils.shape, stencils.dtype),
        )
        + block_types(rows),
        in_specs=[HBM_SPEC] * 3 + [VMEM_SPEC],
        out_specs=(VMEM_SPEC,) * 5,
        scratch_shapes=[pltpu.SemaphoreType.DMA((3 + 2 * rows,))],
        compiler_params=small,
        cost_estimate=pl.CostEstimate(flops=0, bytes_accessed=6000000, transcendentals=0),
        name="own",
    )(stencil_hbm, right_hbm, weight_hbm, held)

    wholes = [lax.ppermute(whole, "frow", move) for move in moves]
    sides = jnp.stack([odd_side, even_side])
    sides_held = [lax.ppermute(sides, "frow", move) for move in moves]
    far_rows = rows if ends == 1 else STEPS
    halo_blocks = pl.pallas_call(
        functools.partial(rows_kernel, ends),
        out_shape=block_types(far_rows) * ends,
        in_specs=[VMEM_SPEC] * ends,
        out_specs=(VMEM_SPEC,) * (3 * ends),
        compiler_params=small,
        cost_estimate=pl.CostEstimate(flops=0, bytes_accessed=4000000, transcendentals=0),
        name="rows",
    )(*wholes)

    cols_held = cols + 2 * SIDE
    rows_held = rows + ends * far_rows
    solution, coarse = pl.pallas_call(
        functools.partial(smooth_kernel, ends),
        out_shape=(
            jax.ShapeDtypeStruct((rows, cols, pixels), F32),
            pltpu.VMEM((rows // 2, cols // 2, pixels), BF16),
        ),
        in_specs=[VMEM_SPEC] * (6 + 4 * ends),
        out_specs=(VMEM_SPEC,) * 2,
        scratch_shapes=[
            pltpu.VMEM((rows_held, cols_held, pixels), F32),
            pltpu.VMEM((rows_held, cols_held, pixels), F32),
            pltpu.VMEM((rows_held, cols_held, pixels), F32),
            pltpu.VMEM((2, 3, rows_held + 2, cols_held, pixels), BF16),
            pltpu.VMEM((slots, rows_held, 2 * SIDE, LANES), BF16),
            pltpu.VMEM((rows, cols, pixels), F32),
            pltpu.VMEM((rows, cols, LANES), F32),
        ],
        compiler_params=pltpu.CompilerParams(vmem_limit_bytes=24 * 1024 * 1024),
        name="smooth",
    )(stencil, odd_side, even_side, *sides_held, *own_block, *halo_blocks)

    spread = jnp.broadcast_to(coarse[None], (ring,) + coarse.shape)
    block = lax.all_to_all(spread, "fcol", 0, 0)
    widened = (rows // 2, ring, cols // 2, pixels)
    gathered = pl.pallas_call(
        widen_kernel,
        out_shape=jax.ShapeDtypeStruct(widened, F32),
        in_specs=[VMEM_SPEC],
        out_specs=HBM_SPEC,
        scratch_shapes=[pltpu.VMEM(widened, F32), pltpu.SemaphoreType.DMA((rows // 2,))],
        compiler_params=small,
        name="widen",
    )(block)
    return solution, gathered.reshape(rows // 2, ring * (cols // 2), pixels)


def solution(mesh):
    placed = (P("frow", "fcol", None), P("frow", "fcol", None), P(), P("frow", "fcol", None))
    return jax.shard_map(
        body,
        mesh=mesh,
        in_specs=placed,
        out_specs=(P("frow", "fcol", None), P("frow", None, None)),
        check_vma=False,
    )
```

```python
import functools

import jax
import jax.numpy as jnp
from jax import lax
from jax.experimental import pallas as pl
from jax.experimental.pallas import tpu as pltpu
from jax.sharding import PartitionSpec as P

DEG = 3
SWEEPS = 2
STEPS = DEG * SWEEPS
SIDE = 8
LANES = 128

lower_edge = 1.5
upper_edge = 6.0
center = 0.5 * (upper_edge + lower_edge)
half_width = 0.5 * (upper_edge - lower_edge)
weight_middle = 3.75

F32 = jnp.float32
BF16 = jnp.bfloat16
HBM_SPEC = pl.BlockSpec(memory_space=pl.ANY)
VMEM_SPEC = pl.BlockSpec(memory_space=pltpu.VMEM)


def step_factors():
    spread_ratio = center / half_width
    factors = []
    for sweep in range(SWEEPS):
        ratio = 1.0 / spread_ratio
        for step in range(DEG):
            if step < DEG - 1:
                ratio_next = 1.0 / (2.0 * spread_ratio - ratio)
                factors.append((ratio_next * ratio, 2.0 * ratio_next / half_width))
                ratio = ratio_next
            else:
                factors.append((0.0, 1.0 / center))
    return factors


def row_places(ends, own_rows):
    if ends == 1:
        flip = lax.axis_index("frow")
        place = [row + flip * (own_rows - 1 - 2 * row) for row in range(own_rows)]
        return place, [list(enumerate(place))], 0
    above = [(own_rows - STEPS + row, row) for row in range(STEPS)]
    below = [(row, row) for row in range(STEPS)]
    return list(range(own_rows)), [above, below], 1


def slot_places(ends, slots):
    if ends == 1:
        flip = lax.axis_index("frow")
        return [(slot // 3 + flip * (2 - 2 * (slot // 3))) * 3 + slot % 3 for slot in range(slots)]
    return list(range(slots))


def spread_flags(ends, mask, flags, own_rows, places):
    slots, _, cols, _ = mask.shape
    slot_place = slot_places(ends, slots)
    for slot in range(slots):
        for row, at in places:
            lane = slot * own_rows + row
            column = jnp.broadcast_to(flags[:, lane : lane + 1], (cols, LANES))
            mask[slot_place[slot], at] = column.astype(BF16)


def edge_kernel(right_hbm, weight_hbm, near_hbm, *refs):
    odd_ref, even_ref, held_ref, strips, near_ref, arrived = refs
    slots, rows, cols = near_ref.shape
    copies = [pltpu.make_async_copy(near_hbm, near_ref, arrived.at[4])]
    for end, start in enumerate((0, cols - SIDE)):
        for kind, source in enumerate((right_hbm, weight_hbm)):
            copies.append(
                pltpu.make_async_copy(
                    source.at[:, pl.ds(start, SIDE)],
                    strips.at[end, kind],
                    arrived.at[2 * end + kind],
                )
            )
    for copy in copies:
        copy.start()
    copies[0].wait()
    flags = jnp.where(near_ref[...] >= 0, 1.0, 0.0).astype(F32).reshape(slots * rows, cols)
    flags = jnp.concatenate([flags, jnp.zeros((slots * rows, LANES - cols), F32)], 1)
    flags = jnp.concatenate([flags, jnp.zeros((LANES - slots * rows, LANES), F32)], 0)
    turned = jnp.transpose(flags)[:cols]
    held_ref[...] = turned
    for copy in copies[1:]:
        copy.wait()
    parity = lax.rem(lax.axis_index("fcol"), 2)
    flags = [turned[:SIDE], turned[cols - SIDE :]]
    for ref, end in ((odd_ref, parity), (even_ref, 1 - parity)):
        ref[:rows] = jnp.concatenate([strips[end, 0], strips[end, 1] - weight_middle], 1).astype(
            BF16
        )
        strip = jnp.where(end == 0, flags[0], flags[1])
        strip = jnp.concatenate([strip, jnp.zeros((SIDE, LANES), F32)], 0)
        ref[rows, :, :LANES] = strip.astype(BF16)


def own_kernel(ends, stencil_hbm, right_hbm, weight_hbm, held_ref, *refs):
    whole_ref, stencil_ref, mask, residual, weight, arrived = refs
    slots = mask.shape[0]
    own_rows, own_cols, _ = residual.shape
    place, _, _ = row_places(ends, own_rows)
    slot_place = slot_places(ends, slots)
    copies = []
    for row in range(own_rows):
        for source, target in ((right_hbm, residual), (weight_hbm, weight)):
            copies.append(
                pltpu.make_async_copy(
                    source.at[row], target.at[place[row]], arrived.at[3 + len(copies)]
                )
            )
    stencil_copies = [
        pltpu.make_async_copy(
            stencil_hbm.at[pl.ds(slot, 3)],
            stencil_ref.at[pl.ds(slot_place[slot], 3)],
            arrived.at[slot // 3],
        )
        for slot in range(0, slots, 3)
    ]
    for copy in copies + stencil_copies:
        copy.start()
    flags = held_ref[...]
    spread_flags(ends, mask, flags, own_rows, list(enumerate(place)))
    whole_ref[own_rows, :own_cols, :LANES] = flags.astype(BF16)
    for copy in copies:
        copy.wait()
    for row, at in enumerate(place):
        whole_ref[row, :own_cols] = residual[at].astype(BF16)
        whole_ref[row, own_cols:] = (weight[at] - weight_middle).astype(BF16)
    for copy in stencil_copies:
        copy.wait()


def rows_kernel(ends, *refs):
    for index in range(ends):
        whole_ref = refs[index]
        mask, residual, weight = refs[ends + 3 * index : ends + 3 * index + 3]
        own_rows = whole_ref.shape[0] - 1
        own_cols = residual.shape[1]
        places = row_places(ends, own_rows)[1][index]
        for row, at in places:
            strip = whole_ref[row].astype(F32)
            residual[at] = strip[:own_cols]
            weight[at] = strip[own_cols:] + weight_middle
        flags = whole_ref[own_rows, :own_cols, :LANES].astype(F32)
        spread_flags(ends, mask, flags, own_rows, places)


def smooth_kernel(ends, *refs):
    stencil_ref, odd_ref, even_ref = refs[:3]
    sides = refs[3 : 3 + ends]
    own_block = refs[3 + ends : 6 + ends]
    halo_blocks = [refs[6 + ends + 3 * i : 9 + ends + 3 * i] for i in range(ends)]
    solution_ref, coarse_ref = refs[6 + 4 * ends : 8 + 4 * ends]
    residual, weight, direction, shifted, side_mask, smoothed, summed = refs[8 + 4 * ends :]
    own_rows, own_cols, pixels = solution_ref.shape
    slots = side_mask.shape[0]
    rows, cols, _ = residual.shape
    place, halos, ahead = row_places(ends, own_rows)
    blocks = halo_blocks[:ahead] + [own_block] + halo_blocks[ahead:]
    bases = [0]
    for block in blocks:
        bases.append(bases[-1] + block[1].shape[0])
    own_start = bases[ahead]

    def flags_of(slot, first, last):
        pieces = []
        for base, block in zip(bases, blocks):
            low, high = max(first - base, 0), min(last - base, block[1].shape[0])
            if low < high:
                pieces.append(block[0][slot, low:high])
        return pieces[0] if len(pieces) == 1 else jnp.concatenate(pieces, 0)

    first_of_even = lax.rem(lax.axis_index("fcol"), 2) == 0

    def fill(base, block, odd, even, places):
        here = slice(base, base + block[1].shape[0])
        residual[here, :own_cols, :] = block[1][...]
        weight[here, :own_cols, :] = block[2][...]

        def in_order(odd_piece, even_piece):
            after = jnp.where(first_of_even, even_piece, odd_piece)
            before = jnp.where(first_of_even, odd_piece, even_piece)
            return after, before

        flags = in_order(*(piece[own_rows, :, :LANES].astype(F32)[:SIDE] for piece in (odd, even)))
        places = [(row, base + at) for row, at in places]
        spread_flags(ends, side_mask, jnp.concatenate(flags, 0), own_rows, places)
        for row, at in places:
            after, before = in_order(odd[row].astype(F32), even[row].astype(F32))
            residual[at, own_cols : own_cols + SIDE, :] = after[:SIDE]
            residual[at, own_cols + SIDE :, :] = before[:SIDE]
            weight[at, own_cols : own_cols + SIDE, :] = after[SIDE:] + weight_middle
            weight[at, own_cols + SIDE :, :] = before[SIDE:] + weight_middle

    fill(own_start, own_block, odd_ref, even_ref, list(enumerate(place)))
    halo_bases = bases[:ahead] + bases[ahead + 1 : -1]
    for base, block, sides_ref, places in zip(halo_bases, halo_blocks, sides, halos):
        fill(base, block, sides_ref.at[0], sides_ref.at[1], places)

    def put_direction(slot, start, count, value):
        here = slice(start + 1, start + 1 + count)
        shifted[slot, 1, here] = value.astype(BF16)
        shifted[slot, 0, here] = pltpu.roll(value, 1, 1).astype(BF16)
        shifted[slot, 2, here] = pltpu.roll(value, cols - 1, 1).astype(BF16)

    edge = jnp.zeros((cols, pixels), BF16)
    for slot in range(2):
        for move in range(3):
            shifted[slot, move, 0] = edge
            shifted[slot, move, rows + 1] = edge
    value = residual[...] * (1.0 / center)
    direction[...] = value
    put_direction(0, 0, rows, value)

    own = slice(own_start, own_start + own_rows)
    stencil = stencil_ref[...].reshape(slots * pixels, pixels)
    factors = step_factors()
    for step in range(STEPS):
        now, later = step % 2, 1 - step % 2
        last = step == STEPS - 1
        moved = direction[own, :own_cols, :]
        smoothed[...] = moved if step == 0 else smoothed[...] + moved
        margin = STEPS - 1 - step
        count = own_rows + ends * margin
        start = own_start - (ends - 1) * margin
        width = own_cols if last else cols
        for base, size in ((start, count),):
            here = slice(base, base + size)
            picked = []
            for slot in range(slots):
                across, along = slot // 3, slot % 3
                keep = flags_of(slot, base, base + size)
                if not last:
                    keep = jnp.concatenate([keep, side_mask[slot, here]], 1)
                source = shifted[now, along, base + across : base + across + size, :width, :]
                picked.append(source[:, :, :LANES] * keep)
                picked.append(source[:, :, LANES:] * keep)
            picked = jnp.concatenate(picked, 2).reshape(size * width, slots * pixels)
            coupled = jnp.dot(picked, stencil, preferred_element_type=F32)
            coupled = coupled.reshape(size, width, pixels)
            moved = direction[here, :width, :]
            left = residual[here, :width, :] - (weight[here, :width, :] * moved + coupled)
            residual[here, :width, :] = left
            if not last:
                a, b = factors[step]
                value = b * left if a == 0.0 else a * moved + b * left
                direction[here, :width, :] = value
                put_direction(later, base, size, value)

    fine = residual[own, :own_cols, :].reshape(own_rows * own_cols, pixels)
    high = fine.astype(BF16)
    low = (fine - high.astype(F32)).astype(BF16)
    quarter = pixels // 4
    from_pixel = lax.broadcasted_iota(jnp.int32, (pixels, LANES), 0) // 4
    to_pixel = lax.broadcasted_iota(jnp.int32, (pixels, LANES), 1)
    adder = jnp.where(from_pixel == to_pixel, 1.0, 0.0).astype(BF16)
    total = jnp.dot(high, adder, preferred_element_type=F32) + jnp.dot(
        low, adder, preferred_element_type=F32
    )
    summed[...] = total.reshape(own_rows, own_cols, LANES)
    for row in range(own_rows // 2):
        pieces = []
        for across in range(2):
            for along in range(2):
                at = place[2 * row + across]
                piece = summed[at, pl.ds(along, own_cols // 2, stride=2), :]
                pieces.append(piece[:, :quarter])
        coarse_ref[row] = jnp.concatenate(pieces, 1).astype(BF16)
    for row, at in enumerate(place):
        solution_ref[row] = smoothed[at]


def widen_kernel(block_ref, out_hbm, wide, sent):
    rows, ring, _, _ = wide.shape
    half = ring // 2
    own_half = lax.axis_index("fcol") // half
    copies = []
    for row in range(rows):
        for i in range(half):
            wide[row, own_half * half + i] = block_ref[i, 0, row].astype(F32)
            wide[row, (1 - own_half) * half + i] = block_ref[i, 1, row].astype(F32)
        copies.append(pltpu.make_async_copy(wide.at[row], out_hbm.at[row], sent.at[row]))
        copies[-1].start()
    for copy in copies:
        copy.wait()


def body(right_side, noise_weight, stencils, neighbours):
    rows, cols, pixels = right_side.shape
    slots = stencils.shape[0]
    pairs, ring = lax.axis_size("frow"), lax.axis_size("fcol")
    swaps = [
        [(i, j) for low in range(first, ring - 1, 2) for i, j in ((low, low + 1), (low + 1, low))]
        for first in (0, 1)
    ]
    near = jnp.transpose(neighbours, (2, 0, 1))
    right_hbm, weight_hbm, near_hbm, stencil_hbm = [
        pltpu.with_memory_space_constraint(array, pltpu.HBM)
        for array in (right_side, noise_weight, near, stencils)
    ]
    small = pltpu.CompilerParams(vmem_limit_bytes=8 * 1024 * 1024)

    side = pltpu.VMEM((rows + 1, 2 * SIDE, pixels), BF16)
    odd, even, held = pl.pallas_call(
        edge_kernel,
        out_shape=(side, side, pltpu.VMEM((cols, LANES), F32)),
        in_specs=[HBM_SPEC] * 3,
        out_specs=(VMEM_SPEC,) * 3,
        scratch_shapes=[
            pltpu.VMEM((2, 2, rows, SIDE, pixels), F32),
            pltpu.VMEM((slots, rows, cols), jnp.int32),
            pltpu.SemaphoreType.DMA((5,)),
        ],
        compiler_params=small,
        name="edges",
    )(right_hbm, weight_hbm, near_hbm)

    odd_side = lax.ppermute(odd, "fcol", swaps[1])
    even_side = lax.ppermute(even, "fcol", swaps[0])
    if pairs == 2:
        moves = [[(0, 1), (1, 0)]]
    else:
        moves = [
            [(i, i + 1) for i in range(pairs - 1)],
            [(i + 1, i) for i in range(pairs - 1)],
        ]
    ends = len(moves)

    def block_types(count):
        return (
            pltpu.VMEM((slots, count, cols, LANES), BF16),
            pltpu.VMEM((count, cols, pixels), F32),
            pltpu.VMEM((count, cols, pixels), F32),
        )

    whole, stencil, *own_block = pl.pallas_call(
        functools.partial(own_kernel, ends),
        out_shape=(
            pltpu.VMEM((rows + 1, 2 * cols, pixels), BF16),
            pltpu.VMEM(stencils.shape, stencils.dtype),
        )
        + block_types(rows),
        in_specs=[HBM_SPEC] * 3 + [VMEM_SPEC],
        out_specs=(VMEM_SPEC,) * 5,
        scratch_shapes=[pltpu.SemaphoreType.DMA((3 + 2 * rows,))],
        compiler_params=small,
        cost_estimate=pl.CostEstimate(flops=0, bytes_accessed=6000000, transcendentals=0),
        name="own",
    )(stencil_hbm, right_hbm, weight_hbm, held)

    wholes = [lax.ppermute(whole, "frow", move) for move in moves]
    sides = jnp.stack([odd_side, even_side])
    sides_held = [lax.ppermute(sides, "frow", move) for move in moves]
    far_rows = rows if ends == 1 else STEPS
    halo_blocks = pl.pallas_call(
        functools.partial(rows_kernel, ends),
        out_shape=block_types(far_rows) * ends,
        in_specs=[VMEM_SPEC] * ends,
        out_specs=(VMEM_SPEC,) * (3 * ends),
        compiler_params=small,
        cost_estimate=pl.CostEstimate(flops=0, bytes_accessed=4000000, transcendentals=0),
        name="rows",
    )(*wholes)

    cols_held = cols + 2 * SIDE
    rows_held = rows + ends * far_rows
    solution, coarse = pl.pallas_call(
        functools.partial(smooth_kernel, ends),
        out_shape=(
            jax.ShapeDtypeStruct((rows, cols, pixels), F32),
            pltpu.VMEM((rows // 2, cols // 2, pixels), BF16),
        ),
        in_specs=[VMEM_SPEC] * (6 + 4 * ends),
        out_specs=(VMEM_SPEC,) * 2,
        scratch_shapes=[
            pltpu.VMEM((rows_held, cols_held, pixels), F32),
            pltpu.VMEM((rows_held, cols_held, pixels), F32),
            pltpu.VMEM((rows_held, cols_held, pixels), F32),
            pltpu.VMEM((2, 3, rows_held + 2, cols_held, pixels), BF16),
            pltpu.VMEM((slots, rows_held, 2 * SIDE, LANES), BF16),
            pltpu.VMEM((rows, cols, pixels), F32),
            pltpu.VMEM((rows, cols, LANES), F32),
        ],
        compiler_params=pltpu.CompilerParams(vmem_limit_bytes=24 * 1024 * 1024),
        name="smooth",
    )(stencil, odd_side, even_side, *sides_held, *own_block, *halo_blocks)

    half = ring // 2
    across = [(i, (i + half) % ring) for i in range(ring)]
    pair = jnp.stack([coarse, lax.ppermute(coarse, "fcol", across)])
    halves = [list(range(half)), list(range(half, ring))]
    spread = jnp.broadcast_to(pair[None], (half,) + pair.shape)
    block = lax.all_to_all(spread, "fcol", 0, 0, axis_index_groups=halves)
    widened = (rows // 2, ring, cols // 2, pixels)
    gathered = pl.pallas_call(
        widen_kernel,
        out_shape=jax.ShapeDtypeStruct(widened, F32),
        in_specs=[VMEM_SPEC],
        out_specs=HBM_SPEC,
        scratch_shapes=[pltpu.VMEM(widened, F32), pltpu.SemaphoreType.DMA((rows // 2,))],
        compiler_params=small,
        name="widen",
    )(block)
    return solution, gathered.reshape(rows // 2, ring * (cols // 2), pixels)


def solution(mesh):
    placed = (P("frow", "fcol", None), P("frow", "fcol", None), P(), P("frow", "fcol", None))
    return jax.shard_map(
        body,
        mesh=mesh,
        in_specs=placed,
        out_specs=(P("frow", "fcol", None), P("frow", None, None)),
        check_vma=False,
    )
```

```python
import functools

import jax
import jax.numpy as jnp
from jax import lax
from jax.experimental import pallas as pl
from jax.experimental.pallas import tpu as pltpu
from jax.sharding import PartitionSpec as P

DEG = 3
SWEEPS = 2
STEPS = DEG * SWEEPS
SIDE = 8
LANES = 128
PIECE_ROWS = 4

lower_edge = 1.5
upper_edge = 6.0
center = 0.5 * (upper_edge + lower_edge)
half_width = 0.5 * (upper_edge - lower_edge)
weight_middle = 3.75

F32 = jnp.float32
BF16 = jnp.bfloat16
HBM_SPEC = pl.BlockSpec(memory_space=pl.ANY)
VMEM_SPEC = pl.BlockSpec(memory_space=pltpu.VMEM)


def step_factors():
    spread_ratio = center / half_width
    factors = []
    for sweep in range(SWEEPS):
        ratio = 1.0 / spread_ratio
        for step in range(DEG):
            if step < DEG - 1:
                ratio_next = 1.0 / (2.0 * spread_ratio - ratio)
                factors.append((ratio_next * ratio, 2.0 * ratio_next / half_width))
                ratio = ratio_next
            else:
                factors.append((0.0, 1.0 / center))
    return factors


def row_places(ends, own_rows):
    if ends == 1:
        flip = lax.axis_index("frow")
        place = [row + flip * (own_rows - 1 - 2 * row) for row in range(own_rows)]
        return place, [list(enumerate(place))], 0
    above = [(own_rows - STEPS + row, row) for row in range(STEPS)]
    below = [(row, row) for row in range(STEPS)]
    return list(range(own_rows)), [above, below], 1


def slot_places(ends, slots):
    if ends == 1:
        flip = lax.axis_index("frow")
        return [(slot // 3 + flip * (2 - 2 * (slot // 3))) * 3 + slot % 3 for slot in range(slots)]
    return list(range(slots))


def spread_flags(ends, mask, flags, own_rows, places):
    slots, _, cols, _ = mask.shape
    slot_place = slot_places(ends, slots)
    for slot in range(slots):
        for row, at in places:
            lane = slot * own_rows + row
            column = jnp.broadcast_to(flags[:, lane : lane + 1], (cols, LANES))
            mask[slot_place[slot], at] = column.astype(BF16)


def edge_kernel(right_hbm, weight_hbm, near_hbm, *refs):
    odd_ref, even_ref, held_ref, strips, near_ref, arrived = refs
    slots, rows, cols = near_ref.shape
    copies = [pltpu.make_async_copy(near_hbm, near_ref, arrived.at[4])]
    for end, start in enumerate((0, cols - SIDE)):
        for kind, source in enumerate((right_hbm, weight_hbm)):
            copies.append(
                pltpu.make_async_copy(
                    source.at[:, pl.ds(start, SIDE)],
                    strips.at[end, kind],
                    arrived.at[2 * end + kind],
                )
            )
    for copy in copies:
        copy.start()
    copies[0].wait()
    flags = jnp.where(near_ref[...] >= 0, 1.0, 0.0).astype(F32).reshape(slots * rows, cols)
    flags = jnp.concatenate([flags, jnp.zeros((slots * rows, LANES - cols), F32)], 1)
    flags = jnp.concatenate([flags, jnp.zeros((LANES - slots * rows, LANES), F32)], 0)
    turned = jnp.transpose(flags)[:cols]
    held_ref[...] = turned
    for copy in copies[1:]:
        copy.wait()
    parity = lax.rem(lax.axis_index("fcol"), 2)
    flags = [turned[:SIDE], turned[cols - SIDE :]]
    for ref, end in ((odd_ref, parity), (even_ref, 1 - parity)):
        ref[:rows] = jnp.concatenate([strips[end, 0], strips[end, 1] - weight_middle], 1).astype(
            BF16
        )
        strip = jnp.where(end == 0, flags[0], flags[1])
        strip = jnp.concatenate([strip, jnp.zeros((SIDE, LANES), F32)], 0)
        ref[rows, :, :LANES] = strip.astype(BF16)


def own_kernel(ends, stencil_hbm, right_hbm, weight_hbm, held_ref, *refs):
    whole_ref, stencil_ref, mask, residual, weight, arrived = refs
    slots = mask.shape[0]
    own_rows, own_cols, _ = residual.shape
    place, _, _ = row_places(ends, own_rows)
    slot_place = slot_places(ends, slots)
    copies = []
    for row in range(own_rows):
        for source, target in ((right_hbm, residual), (weight_hbm, weight)):
            copies.append(
                pltpu.make_async_copy(
                    source.at[row], target.at[place[row]], arrived.at[3 + len(copies)]
                )
            )
    stencil_copies = [
        pltpu.make_async_copy(
            stencil_hbm.at[pl.ds(slot, 3)],
            stencil_ref.at[pl.ds(slot_place[slot], 3)],
            arrived.at[slot // 3],
        )
        for slot in range(0, slots, 3)
    ]
    for copy in copies + stencil_copies:
        copy.start()
    flags = held_ref[...]
    spread_flags(ends, mask, flags, own_rows, list(enumerate(place)))
    whole_ref[own_rows, :own_cols, :LANES] = flags.astype(BF16)
    for copy in copies:
        copy.wait()
    for row, at in enumerate(place):
        whole_ref[row, :own_cols] = residual[at].astype(BF16)
        whole_ref[row, own_cols:] = (weight[at] - weight_middle).astype(BF16)
    for copy in stencil_copies:
        copy.wait()


def rows_kernel(ends, *refs):
    for index in range(ends):
        whole_ref = refs[index]
        mask, residual, weight = refs[ends + 3 * index : ends + 3 * index + 3]
        own_rows = whole_ref.shape[0] - 1
        own_cols = residual.shape[1]
        places = row_places(ends, own_rows)[1][index]
        for row, at in places:
            strip = whole_ref[row].astype(F32)
            residual[at] = strip[:own_cols]
            weight[at] = strip[own_cols:] + weight_middle
        flags = whole_ref[own_rows, :own_cols, :LANES].astype(F32)
        spread_flags(ends, mask, flags, own_rows, places)


def smooth_kernel(ends, *refs):
    stencil_ref, odd_ref, even_ref = refs[:3]
    sides = refs[3 : 3 + ends]
    own_block = refs[3 + ends : 6 + ends]
    halo_blocks = [refs[6 + ends + 3 * i : 9 + ends + 3 * i] for i in range(ends)]
    solution_ref, coarse_ref = refs[6 + 4 * ends : 8 + 4 * ends]
    residual, weight, direction, shifted, side_mask, smoothed, summed = refs[8 + 4 * ends :]
    own_rows, own_cols, pixels = solution_ref.shape
    slots = side_mask.shape[0]
    rows, cols, _ = residual.shape
    place, halos, ahead = row_places(ends, own_rows)
    blocks = halo_blocks[:ahead] + [own_block] + halo_blocks[ahead:]
    bases = [0]
    for block in blocks:
        bases.append(bases[-1] + block[1].shape[0])
    own_start = bases[ahead]

    def flags_of(slot, first, last):
        pieces = []
        for base, block in zip(bases, blocks):
            low, high = max(first - base, 0), min(last - base, block[1].shape[0])
            if low < high:
                pieces.append(block[0][slot, low:high])
        return pieces[0] if len(pieces) == 1 else jnp.concatenate(pieces, 0)

    first_of_even = lax.rem(lax.axis_index("fcol"), 2) == 0

    def fill(base, block, odd, even, places):
        here = slice(base, base + block[1].shape[0])
        residual[here, :own_cols, :] = block[1][...]
        weight[here, :own_cols, :] = block[2][...]

        def in_order(odd_piece, even_piece):
            after = jnp.where(first_of_even, even_piece, odd_piece)
            before = jnp.where(first_of_even, odd_piece, even_piece)
            return after, before

        flags = in_order(*(piece[own_rows, :, :LANES].astype(F32)[:SIDE] for piece in (odd, even)))
        places = [(row, base + at) for row, at in places]
        spread_flags(ends, side_mask, jnp.concatenate(flags, 0), own_rows, places)
        for row, at in places:
            after, before = in_order(odd[row].astype(F32), even[row].astype(F32))
            residual[at, own_cols : own_cols + SIDE, :] = after[:SIDE]
            residual[at, own_cols + SIDE :, :] = before[:SIDE]
            weight[at, own_cols : own_cols + SIDE, :] = after[SIDE:] + weight_middle
            weight[at, own_cols + SIDE :, :] = before[SIDE:] + weight_middle

    fill(own_start, own_block, odd_ref, even_ref, list(enumerate(place)))
    halo_bases = bases[:ahead] + bases[ahead + 1 : -1]
    for base, block, sides_ref, places in zip(halo_bases, halo_blocks, sides, halos):
        fill(base, block, sides_ref.at[0], sides_ref.at[1], places)

    def put_direction(slot, start, count, value):
        here = slice(start + 1, start + 1 + count)
        shifted[slot, 1, here] = value.astype(BF16)
        shifted[slot, 0, here] = pltpu.roll(value, 1, 1).astype(BF16)
        shifted[slot, 2, here] = pltpu.roll(value, cols - 1, 1).astype(BF16)

    edge = jnp.zeros((cols, pixels), BF16)
    for slot in range(2):
        for move in range(3):
            shifted[slot, move, 0] = edge
            shifted[slot, move, rows + 1] = edge
    value = residual[...] * (1.0 / center)
    direction[...] = value
    put_direction(0, 0, rows, value)

    own = slice(own_start, own_start + own_rows)
    stencil = stencil_ref[...].reshape(slots * pixels, pixels)
    factors = step_factors()
    for step in range(STEPS):
        now, later = step % 2, 1 - step % 2
        last = step == STEPS - 1
        moved = direction[own, :own_cols, :]
        smoothed[...] = moved if step == 0 else smoothed[...] + moved
        margin = STEPS - 1 - step
        count = own_rows + ends * margin
        start = own_start - (ends - 1) * margin
        width = own_cols if last else cols
        pieces = -(-count // PIECE_ROWS)
        cuts = [start + count * i // pieces for i in range(pieces + 1)]
        for base, size in zip(cuts, (high - low for low, high in zip(cuts, cuts[1:]))):
            here = slice(base, base + size)
            picked = []
            for slot in range(slots):
                across, along = slot // 3, slot % 3
                keep = flags_of(slot, base, base + size)
                if not last:
                    keep = jnp.concatenate([keep, side_mask[slot, here]], 1)
                source = shifted[now, along, base + across : base + across + size, :width, :]
                picked.append(source[:, :, :LANES] * keep)
                picked.append(source[:, :, LANES:] * keep)
            picked = jnp.concatenate(picked, 2).reshape(size * width, slots * pixels)
            coupled = jnp.dot(picked, stencil, preferred_element_type=F32)
            coupled = coupled.reshape(size, width, pixels)
            moved = direction[here, :width, :]
            left = residual[here, :width, :] - (weight[here, :width, :] * moved + coupled)
            residual[here, :width, :] = left
            if not last:
                a, b = factors[step]
                value = b * left if a == 0.0 else a * moved + b * left
                direction[here, :width, :] = value
                put_direction(later, base, size, value)

    fine = residual[own, :own_cols, :].reshape(own_rows * own_cols, pixels)
    high = fine.astype(BF16)
    low = (fine - high.astype(F32)).astype(BF16)
    quarter = pixels // 4
    from_pixel = lax.broadcasted_iota(jnp.int32, (pixels, LANES), 0) // 4
    to_pixel = lax.broadcasted_iota(jnp.int32, (pixels, LANES), 1)
    adder = jnp.where(from_pixel == to_pixel, 1.0, 0.0).astype(BF16)
    total = jnp.dot(high, adder, preferred_element_type=F32) + jnp.dot(
        low, adder, preferred_element_type=F32
    )
    summed[...] = total.reshape(own_rows, own_cols, LANES)
    for row in range(own_rows // 2):
        pieces = []
        for across in range(2):
            for along in range(2):
                at = place[2 * row + across]
                piece = summed[at, pl.ds(along, own_cols // 2, stride=2), :]
                pieces.append(piece[:, :quarter])
        coarse_ref[row] = jnp.concatenate(pieces, 1).astype(BF16)
    for row, at in enumerate(place):
        solution_ref[row] = smoothed[at]


def widen_kernel(block_ref, out_hbm, wide, sent):
    rows, ring, _, _ = wide.shape
    half = ring // 2
    own_half = lax.axis_index("fcol") // half
    copies = []
    for row in range(rows):
        for i in range(half):
            wide[row, own_half * half + i] = block_ref[i, 0, row].astype(F32)
            wide[row, (1 - own_half) * half + i] = block_ref[i, 1, row].astype(F32)
        copies.append(pltpu.make_async_copy(wide.at[row], out_hbm.at[row], sent.at[row]))
        copies[-1].start()
    for copy in copies:
        copy.wait()


def body(right_side, noise_weight, stencils, neighbours):
    rows, cols, pixels = right_side.shape
    slots = stencils.shape[0]
    pairs, ring = lax.axis_size("frow"), lax.axis_size("fcol")
    swaps = [
        [(i, j) for low in range(first, ring - 1, 2) for i, j in ((low, low + 1), (low + 1, low))]
        for first in (0, 1)
    ]
    near = jnp.transpose(neighbours, (2, 0, 1))
    right_hbm, weight_hbm, near_hbm, stencil_hbm = [
        pltpu.with_memory_space_constraint(array, pltpu.HBM)
        for array in (right_side, noise_weight, near, stencils)
    ]
    small = pltpu.CompilerParams(vmem_limit_bytes=8 * 1024 * 1024)

    side = pltpu.VMEM((rows + 1, 2 * SIDE, pixels), BF16)
    odd, even, held = pl.pallas_call(
        edge_kernel,
        out_shape=(side, side, pltpu.VMEM((cols, LANES), F32)),
        in_specs=[HBM_SPEC] * 3,
        out_specs=(VMEM_SPEC,) * 3,
        scratch_shapes=[
            pltpu.VMEM((2, 2, rows, SIDE, pixels), F32),
            pltpu.VMEM((slots, rows, cols), jnp.int32),
            pltpu.SemaphoreType.DMA((5,)),
        ],
        compiler_params=small,
        name="edges",
    )(right_hbm, weight_hbm, near_hbm)

    odd_side = lax.ppermute(odd, "fcol", swaps[1])
    even_side = lax.ppermute(even, "fcol", swaps[0])
    if pairs == 2:
        moves = [[(0, 1), (1, 0)]]
    else:
        moves = [
            [(i, i + 1) for i in range(pairs - 1)],
            [(i + 1, i) for i in range(pairs - 1)],
        ]
    ends = len(moves)

    def block_types(count):
        return (
            pltpu.VMEM((slots, count, cols, LANES), BF16),
            pltpu.VMEM((count, cols, pixels), F32),
            pltpu.VMEM((count, cols, pixels), F32),
        )

    whole, stencil, *own_block = pl.pallas_call(
        functools.partial(own_kernel, ends),
        out_shape=(
            pltpu.VMEM((rows + 1, 2 * cols, pixels), BF16),
            pltpu.VMEM(stencils.shape, stencils.dtype),
        )
        + block_types(rows),
        in_specs=[HBM_SPEC] * 3 + [VMEM_SPEC],
        out_specs=(VMEM_SPEC,) * 5,
        scratch_shapes=[pltpu.SemaphoreType.DMA((3 + 2 * rows,))],
        compiler_params=small,
        cost_estimate=pl.CostEstimate(flops=0, bytes_accessed=6000000, transcendentals=0),
        name="own",
    )(stencil_hbm, right_hbm, weight_hbm, held)

    wholes = [lax.ppermute(whole, "frow", move) for move in moves]
    sides = jnp.stack([odd_side, even_side])
    sides_held = [lax.ppermute(sides, "frow", move) for move in moves]
    far_rows = rows if ends == 1 else STEPS
    halo_blocks = pl.pallas_call(
        functools.partial(rows_kernel, ends),
        out_shape=block_types(far_rows) * ends,
        in_specs=[VMEM_SPEC] * ends,
        out_specs=(VMEM_SPEC,) * (3 * ends),
        compiler_params=small,
        cost_estimate=pl.CostEstimate(flops=0, bytes_accessed=4000000, transcendentals=0),
        name="rows",
    )(*wholes)

    cols_held = cols + 2 * SIDE
    rows_held = rows + ends * far_rows
    solution, coarse = pl.pallas_call(
        functools.partial(smooth_kernel, ends),
        out_shape=(
            jax.ShapeDtypeStruct((rows, cols, pixels), F32),
            pltpu.VMEM((rows // 2, cols // 2, pixels), BF16),
        ),
        in_specs=[VMEM_SPEC] * (6 + 4 * ends),
        out_specs=(VMEM_SPEC,) * 2,
        scratch_shapes=[
            pltpu.VMEM((rows_held, cols_held, pixels), F32),
            pltpu.VMEM((rows_held, cols_held, pixels), F32),
            pltpu.VMEM((rows_held, cols_held, pixels), F32),
            pltpu.VMEM((2, 3, rows_held + 2, cols_held, pixels), BF16),
            pltpu.VMEM((slots, rows_held, 2 * SIDE, LANES), BF16),
            pltpu.VMEM((rows, cols, pixels), F32),
            pltpu.VMEM((rows, cols, LANES), F32),
        ],
        compiler_params=pltpu.CompilerParams(vmem_limit_bytes=24 * 1024 * 1024),
        name="smooth",
    )(stencil, odd_side, even_side, *sides_held, *own_block, *halo_blocks)

    half = ring // 2
    across = [(i, (i + half) % ring) for i in range(ring)]
    pair = jnp.stack([coarse, lax.ppermute(coarse, "fcol", across)])
    halves = [list(range(half)), list(range(half, ring))]
    spread = jnp.broadcast_to(pair[None], (half,) + pair.shape)
    block = lax.all_to_all(spread, "fcol", 0, 0, axis_index_groups=halves)
    widened = (rows // 2, ring, cols // 2, pixels)
    gathered = pl.pallas_call(
        widen_kernel,
        out_shape=jax.ShapeDtypeStruct(widened, F32),
        in_specs=[VMEM_SPEC],
        out_specs=HBM_SPEC,
        scratch_shapes=[pltpu.VMEM(widened, F32), pltpu.SemaphoreType.DMA((rows // 2,))],
        compiler_params=small,
        name="widen",
    )(block)
    return solution, gathered.reshape(rows // 2, ring * (cols // 2), pixels)


def solution(mesh):
    placed = (P("frow", "fcol", None), P("frow", "fcol", None), P(), P("frow", "fcol", None))
    return jax.shard_map(
        body,
        mesh=mesh,
        in_specs=placed,
        out_specs=(P("frow", "fcol", None), P("frow", None, None)),
        check_vma=False,
    )
```

```python
import functools

import jax
import jax.numpy as jnp
from jax import lax
from jax.experimental import pallas as pl
from jax.experimental.pallas import tpu as pltpu
from jax.sharding import PartitionSpec as P

DEG = 3
SWEEPS = 2
STEPS = DEG * SWEEPS
SIDE = 8
LANES = 128
STRIPS = ((0, STEPS - 1), (SIDE - STEPS, 0))
PIECE_ROWS = 4

lower_edge = 1.5
upper_edge = 6.0
center = 0.5 * (upper_edge + lower_edge)
half_width = 0.5 * (upper_edge - lower_edge)
weight_middle = 3.75

F32 = jnp.float32
BF16 = jnp.bfloat16
HBM_SPEC = pl.BlockSpec(memory_space=pl.ANY)
VMEM_SPEC = pl.BlockSpec(memory_space=pltpu.VMEM)


def step_factors():
    spread_ratio = center / half_width
    factors = []
    for sweep in range(SWEEPS):
        ratio = 1.0 / spread_ratio
        for step in range(DEG):
            if step < DEG - 1:
                ratio_next = 1.0 / (2.0 * spread_ratio - ratio)
                factors.append((ratio_next * ratio, 2.0 * ratio_next / half_width))
                ratio = ratio_next
            else:
                factors.append((0.0, 1.0 / center))
    return factors


def row_places(ends, own_rows):
    if ends == 1:
        flip = lax.axis_index("frow")
        place = [row + flip * (own_rows - 1 - 2 * row) for row in range(own_rows)]
        return place, [list(enumerate(place))], 0
    above = [(own_rows - STEPS + row, row) for row in range(STEPS)]
    below = [(row, row) for row in range(STEPS)]
    return list(range(own_rows)), [above, below], 1


def slot_places(ends, slots):
    if ends == 1:
        flip = lax.axis_index("frow")
        return [(slot // 3 + flip * (2 - 2 * (slot // 3))) * 3 + slot % 3 for slot in range(slots)]
    return list(range(slots))


def spread_flags(ends, mask, flags, own_rows, places):
    slots, _, cols, _ = mask.shape
    slot_place = slot_places(ends, slots)
    for slot in range(slots):
        for row, at in places:
            lane = slot * own_rows + row
            column = jnp.broadcast_to(flags[:, lane : lane + 1], (cols, LANES))
            mask[slot_place[slot], at] = column.astype(BF16)


def edge_kernel(right_hbm, weight_hbm, near_hbm, *refs):
    odd_ref, even_ref, held_ref, strips, flat, near_ref, arrived = refs
    slots, rows, cols = near_ref.shape
    copies = [pltpu.make_async_copy(near_hbm, near_ref, arrived.at[4])]
    for end, start in enumerate((0, cols - SIDE)):
        for kind, source in enumerate((right_hbm, weight_hbm)):
            copies.append(
                pltpu.make_async_copy(
                    source.at[:, pl.ds(start, SIDE)],
                    strips.at[end, kind],
                    arrived.at[2 * end + kind],
                )
            )
    for copy in copies:
        copy.start()
    copies[0].wait()
    flags = jnp.where(near_ref[...] >= 0, 1.0, 0.0).astype(F32).reshape(slots * rows, cols)
    flags = jnp.concatenate([flags, jnp.zeros((slots * rows, LANES - cols), F32)], 1)
    flags = jnp.concatenate([flags, jnp.zeros((LANES - slots * rows, LANES), F32)], 0)
    turned = jnp.transpose(flags)[:cols]
    held_ref[...] = turned
    for copy in copies[1:]:
        copy.wait()
    for end, (low, far) in enumerate(STRIPS):
        for row in range(rows):
            base = 2 * STEPS * row
            flat[end, base : base + STEPS] = strips[end, 0, row, low : low + STEPS]
            weight = strips[end, 1, row, low : low + STEPS] - weight_middle
            flat[end, base + STEPS : base + 2 * STEPS] = weight
            column = row + end * (cols - SIDE)
            flat[end, base + STEPS + far, :LANES] = turned[column]
    parity = lax.rem(lax.axis_index("fcol"), 2)
    odd_ref[...] = flat[parity].astype(BF16)
    even_ref[...] = flat[1 - parity].astype(BF16)


def own_kernel(ends, stencil_hbm, right_hbm, weight_hbm, held_ref, *refs):
    whole_ref, stencil_ref, mask, residual, weight, arrived = refs
    slots = mask.shape[0]
    own_rows, own_cols, _ = residual.shape
    place, _, _ = row_places(ends, own_rows)
    slot_place = slot_places(ends, slots)
    copies = []
    for row in range(own_rows):
        for source, target in ((right_hbm, residual), (weight_hbm, weight)):
            copies.append(
                pltpu.make_async_copy(
                    source.at[row], target.at[place[row]], arrived.at[3 + len(copies)]
                )
            )
    stencil_copies = [
        pltpu.make_async_copy(
            stencil_hbm.at[pl.ds(slot, 3)],
            stencil_ref.at[pl.ds(slot_place[slot], 3)],
            arrived.at[slot // 3],
        )
        for slot in range(0, slots, 3)
    ]
    for copy in copies + stencil_copies:
        copy.start()
    flags = held_ref[...]
    spread_flags(ends, mask, flags, own_rows, list(enumerate(place)))
    whole_ref[own_rows, :own_cols, :LANES] = flags.astype(BF16)
    for copy in copies:
        copy.wait()
    for row, at in enumerate(place):
        whole_ref[row, :own_cols] = residual[at].astype(BF16)
        whole_ref[row, own_cols:] = (weight[at] - weight_middle).astype(BF16)
    for copy in stencil_copies:
        copy.wait()


def rows_kernel(ends, *refs):
    for index in range(ends):
        whole_ref = refs[index]
        mask, residual, weight = refs[ends + 3 * index : ends + 3 * index + 3]
        own_rows = whole_ref.shape[0] - 1
        own_cols = residual.shape[1]
        places = row_places(ends, own_rows)[1][index]
        for row, at in places:
            strip = whole_ref[row].astype(F32)
            residual[at] = strip[:own_cols]
            weight[at] = strip[own_cols:] + weight_middle
        flags = whole_ref[own_rows, :own_cols, :LANES].astype(F32)
        spread_flags(ends, mask, flags, own_rows, places)


def smooth_kernel(ends, *refs):
    stencil_ref, odd_ref, even_ref = refs[:3]
    sides = refs[3 : 3 + ends]
    own_block = refs[3 + ends : 6 + ends]
    halo_blocks = [refs[6 + ends + 3 * i : 9 + ends + 3 * i] for i in range(ends)]
    solution_ref, coarse_ref = refs[6 + 4 * ends : 8 + 4 * ends]
    residual, weight, direction, shifted, side_mask, strips, turned, smoothed, summed = refs[
        8 + 4 * ends :
    ]
    own_rows, own_cols, pixels = solution_ref.shape
    slots = side_mask.shape[0]
    rows, cols, _ = residual.shape
    place, halos, ahead = row_places(ends, own_rows)
    blocks = halo_blocks[:ahead] + [own_block] + halo_blocks[ahead:]
    bases = [0]
    for block in blocks:
        bases.append(bases[-1] + block[1].shape[0])
    own_start = bases[ahead]

    def flags_of(slot, first, last):
        pieces = []
        for base, block in zip(bases, blocks):
            low, high = max(first - base, 0), min(last - base, block[1].shape[0])
            if low < high:
                pieces.append(block[0][slot, low:high])
        return pieces[0] if len(pieces) == 1 else jnp.concatenate(pieces, 0)

    first_of_even = lax.rem(lax.axis_index("fcol"), 2) == 0

    def fill(index, base, block, odd, even, places):
        here = slice(base, base + block[1].shape[0])
        residual[here, :own_cols, :] = block[1][...]
        weight[here, :own_cols, :] = block[2][...]
        unused = jnp.zeros((block[1].shape[0], cols - own_cols, pixels), F32)
        residual[here, own_cols:, :] = unused
        weight[here, own_cols:, :] = unused
        strips[index, 0] = jnp.where(first_of_even, even[...], odd[...]).astype(F32)
        strips[index, 1] = jnp.where(first_of_even, odd[...], even[...]).astype(F32)
        places = [(row, base + at) for row, at in places]
        for end, (low, far) in enumerate(STRIPS):
            side = slice(own_cols + end * SIDE + low, own_cols + end * SIDE + low + STEPS)
            for row, at in places:
                flat = 2 * STEPS * row
                residual[at, side, :] = strips[index, end, flat : flat + STEPS]
                moved = strips[index, end, flat + STEPS : flat + 2 * STEPS]
                weight[at, side, :] = moved + weight_middle
            for column in range(SIDE):
                flat = 2 * STEPS * column + STEPS + far
                turned[index, end * SIDE + column] = strips[index, end, flat, :LANES]
        spread_flags(ends, side_mask, turned[index], own_rows, places)

    fill(0, own_start, own_block, odd_ref, even_ref, list(enumerate(place)))
    halo_bases = bases[:ahead] + bases[ahead + 1 : -1]
    for index, (base, block, sides_ref, places) in enumerate(
        zip(halo_bases, halo_blocks, sides, halos)
    ):
        fill(1 + index, base, block, sides_ref.at[0], sides_ref.at[1], places)

    def put_direction(slot, start, count, value):
        here = slice(start + 1, start + 1 + count)
        shifted[slot, 1, here] = value.astype(BF16)
        shifted[slot, 0, here] = pltpu.roll(value, 1, 1).astype(BF16)
        shifted[slot, 2, here] = pltpu.roll(value, cols - 1, 1).astype(BF16)

    edge = jnp.zeros((cols, pixels), BF16)
    for slot in range(2):
        for move in range(3):
            shifted[slot, move, 0] = edge
            shifted[slot, move, rows + 1] = edge
    value = residual[...] * (1.0 / center)
    direction[...] = value
    put_direction(0, 0, rows, value)

    own = slice(own_start, own_start + own_rows)
    stencil = stencil_ref[...].reshape(slots * pixels, pixels)
    factors = step_factors()
    for step in range(STEPS):
        now, later = step % 2, 1 - step % 2
        last = step == STEPS - 1
        moved = direction[own, :own_cols, :]
        smoothed[...] = moved if step == 0 else smoothed[...] + moved
        margin = STEPS - 1 - step
        count = own_rows + ends * margin
        start = own_start - (ends - 1) * margin
        width = own_cols if last else cols
        pieces = -(-count // PIECE_ROWS)
        cuts = [start + count * i // pieces for i in range(pieces + 1)]
        for base, size in zip(cuts, (high - low for low, high in zip(cuts, cuts[1:]))):
            here = slice(base, base + size)
            picked = []
            for slot in range(slots):
                across, along = slot // 3, slot % 3
                keep = flags_of(slot, base, base + size)
                if not last:
                    keep = jnp.concatenate([keep, side_mask[slot, here]], 1)
                source = shifted[now, along, base + across : base + across + size, :width, :]
                picked.append(source[:, :, :LANES] * keep)
                picked.append(source[:, :, LANES:] * keep)
            picked = jnp.concatenate(picked, 2).reshape(size * width, slots * pixels)
            coupled = jnp.dot(picked, stencil, preferred_element_type=F32)
            coupled = coupled.reshape(size, width, pixels)
            moved = direction[here, :width, :]
            left = residual[here, :width, :] - (weight[here, :width, :] * moved + coupled)
            residual[here, :width, :] = left
            if not last:
                a, b = factors[step]
                value = b * left if a == 0.0 else a * moved + b * left
                direction[here, :width, :] = value
                put_direction(later, base, size, value)

    fine = residual[own, :own_cols, :].reshape(own_rows * own_cols, pixels)
    high = fine.astype(BF16)
    low = (fine - high.astype(F32)).astype(BF16)
    quarter = pixels // 4
    from_pixel = lax.broadcasted_iota(jnp.int32, (pixels, LANES), 0) // 4
    to_pixel = lax.broadcasted_iota(jnp.int32, (pixels, LANES), 1)
    adder = jnp.where(from_pixel == to_pixel, 1.0, 0.0).astype(BF16)
    total = jnp.dot(high, adder, preferred_element_type=F32) + jnp.dot(
        low, adder, preferred_element_type=F32
    )
    summed[...] = total.reshape(own_rows, own_cols, LANES)
    for row in range(own_rows // 2):
        pieces = []
        for across in range(2):
            for along in range(2):
                at = place[2 * row + across]
                piece = summed[at, pl.ds(along, own_cols // 2, stride=2), :]
                pieces.append(piece[:, :quarter])
        coarse_ref[row] = jnp.concatenate(pieces, 1).astype(BF16)
    for row, at in enumerate(place):
        solution_ref[row] = smoothed[at]


def widen_kernel(block_ref, out_hbm, wide, sent):
    rows, ring, _, _ = wide.shape
    half = ring // 2
    own_half = lax.axis_index("fcol") // half
    copies = []
    for row in range(rows):
        for i in range(half):
            wide[row, own_half * half + i] = block_ref[i, 0, row].astype(F32)
            wide[row, (1 - own_half) * half + i] = block_ref[i, 1, row].astype(F32)
        copies.append(pltpu.make_async_copy(wide.at[row], out_hbm.at[row], sent.at[row]))
        copies[-1].start()
    for copy in copies:
        copy.wait()


def body(right_side, noise_weight, stencils, neighbours):
    rows, cols, pixels = right_side.shape
    slots = stencils.shape[0]
    pairs, ring = lax.axis_size("frow"), lax.axis_size("fcol")
    swaps = [
        [(i, j) for low in range(first, ring - 1, 2) for i, j in ((low, low + 1), (low + 1, low))]
        for first in (0, 1)
    ]
    near = jnp.transpose(neighbours, (2, 0, 1))
    right_hbm, weight_hbm, near_hbm, stencil_hbm = [
        pltpu.with_memory_space_constraint(array, pltpu.HBM)
        for array in (right_side, noise_weight, near, stencils)
    ]
    small = pltpu.CompilerParams(vmem_limit_bytes=8 * 1024 * 1024)

    side = pltpu.VMEM((2 * STEPS * rows, pixels), BF16)
    odd, even, held = pl.pallas_call(
        edge_kernel,
        out_shape=(side, side, pltpu.VMEM((cols, LANES), F32)),
        in_specs=[HBM_SPEC] * 3,
        out_specs=(VMEM_SPEC,) * 3,
        scratch_shapes=[
            pltpu.VMEM((2, 2, rows, SIDE, pixels), F32),
            pltpu.VMEM((2, 2 * STEPS * rows, pixels), F32),
            pltpu.VMEM((slots, rows, cols), jnp.int32),
            pltpu.SemaphoreType.DMA((5,)),
        ],
        compiler_params=small,
        name="edges",
    )(right_hbm, weight_hbm, near_hbm)

    odd_side = lax.ppermute(odd, "fcol", swaps[1])
    even_side = lax.ppermute(even, "fcol", swaps[0])
    if pairs == 2:
        moves = [[(0, 1), (1, 0)]]
    else:
        moves = [
            [(i, i + 1) for i in range(pairs - 1)],
            [(i + 1, i) for i in range(pairs - 1)],
        ]
    ends = len(moves)

    def block_types(count):
        return (
            pltpu.VMEM((slots, count, cols, LANES), BF16),
            pltpu.VMEM((count, cols, pixels), F32),
            pltpu.VMEM((count, cols, pixels), F32),
        )

    whole, stencil, *own_block = pl.pallas_call(
        functools.partial(own_kernel, ends),
        out_shape=(
            pltpu.VMEM((rows + 1, 2 * cols, pixels), BF16),
            pltpu.VMEM(stencils.shape, stencils.dtype),
        )
        + block_types(rows),
        in_specs=[HBM_SPEC] * 3 + [VMEM_SPEC],
        out_specs=(VMEM_SPEC,) * 5,
        scratch_shapes=[pltpu.SemaphoreType.DMA((3 + 2 * rows,))],
        compiler_params=small,
        cost_estimate=pl.CostEstimate(flops=0, bytes_accessed=6000000, transcendentals=0),
        name="own",
    )(stencil_hbm, right_hbm, weight_hbm, held)

    wholes = [lax.ppermute(whole, "frow", move) for move in moves]
    sides = jnp.stack([odd_side, even_side])
    sides_held = [lax.ppermute(sides, "frow", move) for move in moves]
    far_rows = rows if ends == 1 else STEPS
    halo_blocks = pl.pallas_call(
        functools.partial(rows_kernel, ends),
        out_shape=block_types(far_rows) * ends,
        in_specs=[VMEM_SPEC] * ends,
        out_specs=(VMEM_SPEC,) * (3 * ends),
        compiler_params=small,
        cost_estimate=pl.CostEstimate(flops=0, bytes_accessed=4000000, transcendentals=0),
        name="rows",
    )(*wholes)

    cols_held = cols + 2 * SIDE
    rows_held = rows + ends * far_rows
    solution, coarse = pl.pallas_call(
        functools.partial(smooth_kernel, ends),
        out_shape=(
            jax.ShapeDtypeStruct((rows, cols, pixels), F32),
            pltpu.VMEM((rows // 2, cols // 2, pixels), BF16),
        ),
        in_specs=[VMEM_SPEC] * (6 + 4 * ends),
        out_specs=(VMEM_SPEC,) * 2,
        scratch_shapes=[
            pltpu.VMEM((rows_held, cols_held, pixels), F32),
            pltpu.VMEM((rows_held, cols_held, pixels), F32),
            pltpu.VMEM((rows_held, cols_held, pixels), F32),
            pltpu.VMEM((2, 3, rows_held + 2, cols_held, pixels), BF16),
            pltpu.VMEM((slots, rows_held, 2 * SIDE, LANES), BF16),
            pltpu.VMEM((1 + ends, 2, 2 * STEPS * rows, pixels), F32),
            pltpu.VMEM((1 + ends, 2 * SIDE, LANES), F32),
            pltpu.VMEM((rows, cols, pixels), F32),
            pltpu.VMEM((rows, cols, LANES), F32),
        ],
        compiler_params=pltpu.CompilerParams(vmem_limit_bytes=24 * 1024 * 1024),
        name="smooth",
    )(stencil, odd_side, even_side, *sides_held, *own_block, *halo_blocks)

    half = ring // 2
    across = [(i, (i + half) % ring) for i in range(ring)]
    pair = jnp.stack([coarse, lax.ppermute(coarse, "fcol", across)])
    halves = [list(range(half)), list(range(half, ring))]
    spread = jnp.broadcast_to(pair[None], (half,) + pair.shape)
    block = lax.all_to_all(spread, "fcol", 0, 0, axis_index_groups=halves)
    widened = (rows // 2, ring, cols // 2, pixels)
    gathered = pl.pallas_call(
        widen_kernel,
        out_shape=jax.ShapeDtypeStruct(widened, F32),
        in_specs=[VMEM_SPEC],
        out_specs=HBM_SPEC,
        scratch_shapes=[pltpu.VMEM(widened, F32), pltpu.SemaphoreType.DMA((rows // 2,))],
        compiler_params=small,
        name="widen",
    )(block)
    return solution, gathered.reshape(rows // 2, ring * (cols // 2), pixels)


def solution(mesh):
    placed = (P("frow", "fcol", None), P("frow", "fcol", None), P(), P("frow", "fcol", None))
    return jax.shard_map(
        body,
        mesh=mesh,
        in_specs=placed,
        out_specs=(P("frow", "fcol", None), P("frow", None, None)),
        check_vma=False,
    )
```

```python
import functools

import jax
import jax.numpy as jnp
from jax import lax
from jax.experimental import pallas as pl
from jax.experimental.pallas import tpu as pltpu
from jax.sharding import PartitionSpec as P

DEG = 3
SWEEPS = 2
STEPS = DEG * SWEEPS
SIDE = 8
LANES = 128
STRIPS = ((0, STEPS - 1), (SIDE - STEPS, 0))
PIECE_ROWS = 4

lower_edge = 1.5
upper_edge = 6.0
center = 0.5 * (upper_edge + lower_edge)
half_width = 0.5 * (upper_edge - lower_edge)
weight_middle = 3.75

F32 = jnp.float32
BF16 = jnp.bfloat16
HBM_SPEC = pl.BlockSpec(memory_space=pl.ANY)
VMEM_SPEC = pl.BlockSpec(memory_space=pltpu.VMEM)


def step_factors():
    spread_ratio = center / half_width
    factors = []
    for sweep in range(SWEEPS):
        ratio = 1.0 / spread_ratio
        for step in range(DEG):
            if step < DEG - 1:
                ratio_next = 1.0 / (2.0 * spread_ratio - ratio)
                factors.append((ratio_next * ratio, 2.0 * ratio_next / half_width))
                ratio = ratio_next
            else:
                factors.append((0.0, 1.0 / center))
    return factors


def row_places(ends, own_rows):
    if ends == 1:
        flip = lax.axis_index("frow")
        place = [row + flip * (own_rows - 1 - 2 * row) for row in range(own_rows)]
        return place, [list(enumerate(place))], 0
    above = [(own_rows - STEPS + row, row) for row in range(STEPS)]
    below = [(row, row) for row in range(STEPS)]
    return list(range(own_rows)), [above, below], 1


def rows_sent(ends, own_rows):
    if ends == 1:
        return [([own_rows - 1 - row for row in range(STEPS)], STEPS - 1)]
    return [
        ([own_rows - STEPS + row for row in range(STEPS)], 0),
        (list(range(STEPS)), STEPS - 1),
    ]


def slot_places(ends, slots):
    if ends == 1:
        flip = lax.axis_index("frow")
        return [(slot // 3 + flip * (2 - 2 * (slot // 3))) * 3 + slot % 3 for slot in range(slots)]
    return list(range(slots))


def spread_flags(ends, mask, flags, own_rows, places):
    slots, _, cols, _ = mask.shape
    slot_place = slot_places(ends, slots)
    for slot in range(slots):
        for row, at in places:
            lane = slot * own_rows + row
            column = jnp.broadcast_to(flags[:, lane : lane + 1], (cols, LANES))
            mask[slot_place[slot], at] = column.astype(BF16)


def edge_kernel(right_hbm, weight_hbm, near_hbm, *refs):
    odd_ref, even_ref, held_ref, strips, flat, near_ref, arrived = refs
    slots, rows, cols = near_ref.shape
    copies = [pltpu.make_async_copy(near_hbm, near_ref, arrived.at[4])]
    for end, start in enumerate((0, cols - SIDE)):
        for kind, source in enumerate((right_hbm, weight_hbm)):
            copies.append(
                pltpu.make_async_copy(
                    source.at[:, pl.ds(start, SIDE)],
                    strips.at[end, kind],
                    arrived.at[2 * end + kind],
                )
            )
    for copy in copies:
        copy.start()
    copies[0].wait()
    flags = jnp.where(near_ref[...] >= 0, 1.0, 0.0).astype(F32).reshape(slots * rows, cols)
    flags = jnp.concatenate([flags, jnp.zeros((slots * rows, LANES - cols), F32)], 1)
    flags = jnp.concatenate([flags, jnp.zeros((LANES - slots * rows, LANES), F32)], 0)
    turned = jnp.transpose(flags)[:cols]
    held_ref[...] = turned
    for copy in copies[1:]:
        copy.wait()
    for end, (low, far) in enumerate(STRIPS):
        for row in range(rows):
            base = 2 * STEPS * row
            flat[end, base : base + STEPS] = strips[end, 0, row, low : low + STEPS]
            weight = strips[end, 1, row, low : low + STEPS] - weight_middle
            flat[end, base + STEPS : base + 2 * STEPS] = weight
            column = row + end * (cols - SIDE)
            flat[end, base + STEPS + far, :LANES] = turned[column]
    parity = lax.rem(lax.axis_index("fcol"), 2)
    odd_ref[...] = flat[parity].astype(BF16)
    even_ref[...] = flat[1 - parity].astype(BF16)


def own_kernel(ends, stencil_hbm, right_hbm, weight_hbm, held_ref, *refs):
    whole_refs = refs[:ends]
    stencil_ref, mask, residual, weight, arrived = refs[ends:]
    slots = mask.shape[0]
    own_rows, own_cols, _ = residual.shape
    place, _, _ = row_places(ends, own_rows)
    slot_place = slot_places(ends, slots)
    copies = []
    for row in range(own_rows):
        for source, target in ((right_hbm, residual), (weight_hbm, weight)):
            copies.append(
                pltpu.make_async_copy(
                    source.at[row], target.at[place[row]], arrived.at[3 + len(copies)]
                )
            )
    stencil_copies = [
        pltpu.make_async_copy(
            stencil_hbm.at[pl.ds(slot, 3)],
            stencil_ref.at[pl.ds(slot_place[slot], 3)],
            arrived.at[slot // 3],
        )
        for slot in range(0, slots, 3)
    ]
    for copy in copies + stencil_copies:
        copy.start()
    flags = held_ref[...]
    spread_flags(ends, mask, flags, own_rows, list(enumerate(place)))
    for copy in copies:
        copy.wait()
    for whole_ref, (sent, far) in zip(whole_refs, rows_sent(ends, own_rows)):
        for row, at in enumerate(sent):
            whole_ref[row, :own_cols] = residual[at].astype(BF16)
            if row == far:
                whole_ref[row, own_cols:, :LANES] = flags.astype(BF16)
                whole_ref[row, own_cols:, LANES:] = flags.astype(BF16)
            else:
                whole_ref[row, own_cols:] = (weight[at] - weight_middle).astype(BF16)
    for copy in stencil_copies:
        copy.wait()


def rows_kernel(ends, *refs):
    for index in range(ends):
        whole_ref = refs[index]
        mask, residual, weight = refs[ends + 3 * index : ends + 3 * index + 3]
        own_rows, own_cols = mask.shape[1], residual.shape[1]
        for row in range(STEPS):
            strip = whole_ref[row].astype(F32)
            residual[row] = strip[:own_cols]
            weight[row] = strip[own_cols:] + weight_middle
        far = rows_sent(ends, own_rows)[index][1]
        flags = whole_ref[far, own_cols:, :LANES].astype(F32)
        places = row_places(ends, own_rows)[1][index]
        spread_flags(ends, mask, flags, own_rows, places)


def smooth_kernel(ends, *refs):
    stencil_ref, odd_ref, even_ref = refs[:3]
    sides = refs[3 : 3 + ends]
    own_block = refs[3 + ends : 6 + ends]
    halo_blocks = [refs[6 + ends + 3 * i : 9 + ends + 3 * i] for i in range(ends)]
    solution_ref, coarse_ref = refs[6 + 4 * ends : 8 + 4 * ends]
    residual, weight, direction, shifted, side_mask, strips, turned, smoothed, summed = refs[
        8 + 4 * ends :
    ]
    own_rows, own_cols, pixels = solution_ref.shape
    slots = side_mask.shape[0]
    rows, cols, _ = residual.shape
    place, halos, ahead = row_places(ends, own_rows)
    blocks = halo_blocks[:ahead] + [own_block] + halo_blocks[ahead:]
    bases = [0]
    for block in blocks:
        bases.append(bases[-1] + block[1].shape[0])
    if bases[-1] < rows:
        unused = jnp.zeros((rows - bases[-1], cols, pixels), F32)
        residual[bases[-1] :] = unused
        weight[bases[-1] :] = unused
    own_start = bases[ahead]

    def flags_of(slot, first, last):
        pieces = []
        for base, block in zip(bases, blocks):
            low, high = max(first - base, 0), min(last - base, block[1].shape[0])
            if low < high:
                pieces.append(block[0][slot, low:high])
        return pieces[0] if len(pieces) == 1 else jnp.concatenate(pieces, 0)

    first_of_even = lax.rem(lax.axis_index("fcol"), 2) == 0

    def fill(index, base, block, odd, even, places):
        here = slice(base, base + block[1].shape[0])
        residual[here, :own_cols, :] = block[1][...]
        weight[here, :own_cols, :] = block[2][...]
        unused = jnp.zeros((block[1].shape[0], cols - own_cols, pixels), F32)
        residual[here, own_cols:, :] = unused
        weight[here, own_cols:, :] = unused
        strips[index, 0] = jnp.where(first_of_even, even[...], odd[...]).astype(F32)
        strips[index, 1] = jnp.where(first_of_even, odd[...], even[...]).astype(F32)
        places = [(row, base + at) for row, at in places]
        for end, (low, far) in enumerate(STRIPS):
            side = slice(own_cols + end * SIDE + low, own_cols + end * SIDE + low + STEPS)
            for row, at in places:
                flat = 2 * STEPS * row
                residual[at, side, :] = strips[index, end, flat : flat + STEPS]
                moved = strips[index, end, flat + STEPS : flat + 2 * STEPS]
                weight[at, side, :] = moved + weight_middle
            for column in range(SIDE):
                flat = 2 * STEPS * column + STEPS + far
                turned[index, end * SIDE + column] = strips[index, end, flat, :LANES]
        spread_flags(ends, side_mask, turned[index], own_rows, places)

    fill(0, own_start, own_block, odd_ref, even_ref, list(enumerate(place)))
    halo_bases = bases[:ahead] + bases[ahead + 1 : -1]
    for index, (base, block, sides_ref, places) in enumerate(
        zip(halo_bases, halo_blocks, sides, halos)
    ):
        fill(1 + index, base, block, sides_ref.at[0], sides_ref.at[1], places)

    def put_direction(slot, start, count, value):
        here = slice(start + 1, start + 1 + count)
        shifted[slot, 1, here] = value.astype(BF16)
        shifted[slot, 0, here] = pltpu.roll(value, 1, 1).astype(BF16)
        shifted[slot, 2, here] = pltpu.roll(value, cols - 1, 1).astype(BF16)

    edge = jnp.zeros((cols, pixels), BF16)
    for slot in range(2):
        for move in range(3):
            shifted[slot, move, 0] = edge
            shifted[slot, move, rows + 1] = edge
    value = residual[...] * (1.0 / center)
    direction[...] = value
    put_direction(0, 0, rows, value)

    own = slice(own_start, own_start + own_rows)
    stencil = stencil_ref[...].reshape(slots * pixels, pixels)
    factors = step_factors()
    for step in range(STEPS):
        now, later = step % 2, 1 - step % 2
        last = step == STEPS - 1
        moved = direction[own, :own_cols, :]
        smoothed[...] = moved if step == 0 else smoothed[...] + moved
        margin = STEPS - 1 - step
        count = own_rows + ends * margin
        start = own_start - (ends - 1) * margin
        width = own_cols if last else cols
        pieces = -(-count // PIECE_ROWS)
        cuts = [start + count * i // pieces for i in range(pieces + 1)]
        for base, size in zip(cuts, (high - low for low, high in zip(cuts, cuts[1:]))):
            here = slice(base, base + size)
            picked = []
            for slot in range(slots):
                across, along = slot // 3, slot % 3
                keep = flags_of(slot, base, base + size)
                if not last:
                    keep = jnp.concatenate([keep, side_mask[slot, here]], 1)
                source = shifted[now, along, base + across : base + across + size, :width, :]
                picked.append(source[:, :, :LANES] * keep)
                picked.append(source[:, :, LANES:] * keep)
            picked = jnp.concatenate(picked, 2).reshape(size * width, slots * pixels)
            coupled = jnp.dot(picked, stencil, preferred_element_type=F32)
            coupled = coupled.reshape(size, width, pixels)
            moved = direction[here, :width, :]
            left = residual[here, :width, :] - (weight[here, :width, :] * moved + coupled)
            residual[here, :width, :] = left
            if not last:
                a, b = factors[step]
                value = b * left if a == 0.0 else a * moved + b * left
                direction[here, :width, :] = value
                put_direction(later, base, size, value)

    fine = residual[own, :own_cols, :].reshape(own_rows * own_cols, pixels)
    high = fine.astype(BF16)
    low = (fine - high.astype(F32)).astype(BF16)
    quarter = pixels // 4
    from_pixel = lax.broadcasted_iota(jnp.int32, (pixels, LANES), 0) // 4
    to_pixel = lax.broadcasted_iota(jnp.int32, (pixels, LANES), 1)
    adder = jnp.where(from_pixel == to_pixel, 1.0, 0.0).astype(BF16)
    total = jnp.dot(high, adder, preferred_element_type=F32) + jnp.dot(
        low, adder, preferred_element_type=F32
    )
    summed[...] = total.reshape(own_rows, own_cols, LANES)
    for row in range(own_rows // 2):
        pieces = []
        for across in range(2):
            for along in range(2):
                at = place[2 * row + across]
                piece = summed[at, pl.ds(along, own_cols // 2, stride=2), :]
                pieces.append(piece[:, :quarter])
        coarse_ref[row] = jnp.concatenate(pieces, 1).astype(BF16)
    for row, at in enumerate(place):
        solution_ref[row] = smoothed[at]


def widen_kernel(block_ref, out_hbm, wide, sent):
    rows, ring, _, _ = wide.shape
    half = ring // 2
    own_half = lax.axis_index("fcol") // half
    copies = []
    for row in range(rows):
        for i in range(half):
            wide[row, own_half * half + i] = block_ref[i, 0, row].astype(F32)
            wide[row, (1 - own_half) * half + i] = block_ref[i, 1, row].astype(F32)
        copies.append(pltpu.make_async_copy(wide.at[row], out_hbm.at[row], sent.at[row]))
        copies[-1].start()
    for copy in copies:
        copy.wait()


def body(right_side, noise_weight, stencils, neighbours):
    rows, cols, pixels = right_side.shape
    slots = stencils.shape[0]
    pairs, ring = lax.axis_size("frow"), lax.axis_size("fcol")
    swaps = [
        [(i, j) for low in range(first, ring - 1, 2) for i, j in ((low, low + 1), (low + 1, low))]
        for first in (0, 1)
    ]
    near = jnp.transpose(neighbours, (2, 0, 1))
    right_hbm, weight_hbm, near_hbm, stencil_hbm = [
        pltpu.with_memory_space_constraint(array, pltpu.HBM)
        for array in (right_side, noise_weight, near, stencils)
    ]
    small = pltpu.CompilerParams(vmem_limit_bytes=8 * 1024 * 1024)

    side = pltpu.VMEM((2 * STEPS * rows, pixels), BF16)
    odd, even, held = pl.pallas_call(
        edge_kernel,
        out_shape=(side, side, pltpu.VMEM((cols, LANES), F32)),
        in_specs=[HBM_SPEC] * 3,
        out_specs=(VMEM_SPEC,) * 3,
        scratch_shapes=[
            pltpu.VMEM((2, 2, rows, SIDE, pixels), F32),
            pltpu.VMEM((2, 2 * STEPS * rows, pixels), F32),
            pltpu.VMEM((slots, rows, cols), jnp.int32),
            pltpu.SemaphoreType.DMA((5,)),
        ],
        compiler_params=small,
        name="edges",
    )(right_hbm, weight_hbm, near_hbm)

    odd_side = lax.ppermute(odd, "fcol", swaps[1])
    even_side = lax.ppermute(even, "fcol", swaps[0])
    if pairs == 2:
        moves = [[(0, 1), (1, 0)]]
    else:
        moves = [
            [(i, i + 1) for i in range(pairs - 1)],
            [(i + 1, i) for i in range(pairs - 1)],
        ]
    ends = len(moves)

    def block_types(count):
        return (
            pltpu.VMEM((slots, rows, cols, LANES), BF16),
            pltpu.VMEM((count, cols, pixels), F32),
            pltpu.VMEM((count, cols, pixels), F32),
        )

    *sent, stencil, mask, right, weight = pl.pallas_call(
        functools.partial(own_kernel, ends),
        out_shape=(pltpu.VMEM((STEPS, 2 * cols, pixels), BF16),) * ends
        + (pltpu.VMEM(stencils.shape, stencils.dtype),)
        + block_types(rows),
        in_specs=[HBM_SPEC] * 3 + [VMEM_SPEC],
        out_specs=(VMEM_SPEC,) * (4 + ends),
        scratch_shapes=[pltpu.SemaphoreType.DMA((3 + 2 * rows,))],
        compiler_params=small,
        cost_estimate=pl.CostEstimate(flops=0, bytes_accessed=6000000, transcendentals=0),
        name="own",
    )(stencil_hbm, right_hbm, weight_hbm, held)

    wholes = [lax.ppermute(whole, "frow", move) for whole, move in zip(sent, moves)]
    sides = jnp.stack([odd_side, even_side])
    sides_held = [lax.ppermute(sides, "frow", move) for move in moves]
    halo_blocks = pl.pallas_call(
        functools.partial(rows_kernel, ends),
        out_shape=block_types(STEPS) * ends,
        in_specs=[VMEM_SPEC] * ends,
        out_specs=(VMEM_SPEC,) * (3 * ends),
        compiler_params=small,
        cost_estimate=pl.CostEstimate(flops=0, bytes_accessed=4000000, transcendentals=0),
        name="rows",
    )(*wholes)

    cols_held = cols + 2 * SIDE
    rows_held = 2 * rows if ends == 1 else rows + 2 * STEPS
    solution, coarse = pl.pallas_call(
        functools.partial(smooth_kernel, ends),
        out_shape=(
            jax.ShapeDtypeStruct((rows, cols, pixels), F32),
            pltpu.VMEM((rows // 2, cols // 2, pixels), BF16),
        ),
        in_specs=[VMEM_SPEC] * (6 + 4 * ends),
        out_specs=(VMEM_SPEC,) * 2,
        scratch_shapes=[
            pltpu.VMEM((rows_held, cols_held, pixels), F32),
            pltpu.VMEM((rows_held, cols_held, pixels), F32),
            pltpu.VMEM((rows_held, cols_held, pixels), F32),
            pltpu.VMEM((2, 3, rows_held + 2, cols_held, pixels), BF16),
            pltpu.VMEM((slots, rows_held, 2 * SIDE, LANES), BF16),
            pltpu.VMEM((1 + ends, 2, 2 * STEPS * rows, pixels), F32),
            pltpu.VMEM((1 + ends, 2 * SIDE, LANES), F32),
            pltpu.VMEM((rows, cols, pixels), F32),
            pltpu.VMEM((rows, cols, LANES), F32),
        ],
        compiler_params=pltpu.CompilerParams(vmem_limit_bytes=24 * 1024 * 1024),
        name="smooth",
    )(stencil, odd_side, even_side, *sides_held, mask, right, weight, *halo_blocks)

    half = ring // 2
    across = [(i, (i + half) % ring) for i in range(ring)]
    pair = jnp.stack([coarse, lax.ppermute(coarse, "fcol", across)])
    halves = [list(range(half)), list(range(half, ring))]
    spread = jnp.broadcast_to(pair[None], (half,) + pair.shape)
    block = lax.all_to_all(spread, "fcol", 0, 0, axis_index_groups=halves)
    widened = (rows // 2, ring, cols // 2, pixels)
    gathered = pl.pallas_call(
        widen_kernel,
        out_shape=jax.ShapeDtypeStruct(widened, F32),
        in_specs=[VMEM_SPEC],
        out_specs=HBM_SPEC,
        scratch_shapes=[pltpu.VMEM(widened, F32), pltpu.SemaphoreType.DMA((rows // 2,))],
        compiler_params=small,
        name="widen",
    )(block)
    return solution, gathered.reshape(rows // 2, ring * (cols // 2), pixels)


def solution(mesh):
    placed = (P("frow", "fcol", None), P("frow", "fcol", None), P(), P("frow", "fcol", None))
    return jax.shard_map(
        body,
        mesh=mesh,
        in_specs=placed,
        out_specs=(P("frow", "fcol", None), P("frow", None, None)),
        check_vma=False,
    )
```

```python
import functools

import jax
import jax.numpy as jnp
from jax import lax
from jax.experimental import pallas as pl
from jax.experimental.pallas import tpu as pltpu
from jax.sharding import PartitionSpec as P

DEG = 3
SWEEPS = 2
STEPS = DEG * SWEEPS
SIDE = 8
LANES = 128
STRIPS = ((0, STEPS - 1), (SIDE - STEPS, 0))
PIECE_ROWS = 4

lower_edge = 1.5
upper_edge = 6.0
center = 0.5 * (upper_edge + lower_edge)
half_width = 0.5 * (upper_edge - lower_edge)
weight_middle = 3.75

F32 = jnp.float32
BF16 = jnp.bfloat16
HBM_SPEC = pl.BlockSpec(memory_space=pl.ANY)
VMEM_SPEC = pl.BlockSpec(memory_space=pltpu.VMEM)


def step_factors():
    spread_ratio = center / half_width
    factors = []
    for sweep in range(SWEEPS):
        ratio = 1.0 / spread_ratio
        for step in range(DEG):
            if step < DEG - 1:
                ratio_next = 1.0 / (2.0 * spread_ratio - ratio)
                factors.append((ratio_next * ratio, 2.0 * ratio_next / half_width))
                ratio = ratio_next
            else:
                factors.append((0.0, 1.0 / center))
    return factors


def row_places(ends, own_rows):
    if ends == 1:
        flip = lax.axis_index("frow")
        place = [row + flip * (own_rows - 1 - 2 * row) for row in range(own_rows)]
        return place, [list(enumerate(place))], 0
    above = [(own_rows - STEPS + row, row) for row in range(STEPS)]
    below = [(row, row) for row in range(STEPS)]
    return list(range(own_rows)), [above, below], 1


def rows_sent(ends, own_rows):
    if ends == 1:
        return [([own_rows - 1 - row for row in range(STEPS)], STEPS - 1)]
    return [
        ([own_rows - STEPS + row for row in range(STEPS)], 0),
        (list(range(STEPS)), STEPS - 1),
    ]


def slot_places(ends, slots):
    if ends == 1:
        flip = lax.axis_index("frow")
        return [(slot // 3 + flip * (2 - 2 * (slot // 3))) * 3 + slot % 3 for slot in range(slots)]
    return list(range(slots))


def spread_flags(ends, mask, flags, own_rows, places):
    slots, _, cols, _ = mask.shape
    slot_place = slot_places(ends, slots)
    for slot in range(slots):
        if slot == slots // 2:
            continue
        for row, at in places:
            lane = slot * own_rows + row
            column = jnp.broadcast_to(flags[:, lane : lane + 1], (cols, LANES))
            mask[slot_place[slot], at] = column.astype(BF16)


def edge_kernel(right_hbm, weight_hbm, near_hbm, *refs):
    odd_ref, even_ref, held_ref, strips, flat, near_ref, arrived = refs
    slots, rows, cols = near_ref.shape
    copies = [pltpu.make_async_copy(near_hbm, near_ref, arrived.at[4])]
    for end, start in enumerate((0, cols - SIDE)):
        for kind, source in enumerate((right_hbm, weight_hbm)):
            copies.append(
                pltpu.make_async_copy(
                    source.at[:, pl.ds(start, SIDE)],
                    strips.at[end, kind],
                    arrived.at[2 * end + kind],
                )
            )
    for copy in copies:
        copy.start()
    copies[0].wait()
    flags = jnp.where(near_ref[...] >= 0, 1.0, 0.0).astype(F32).reshape(slots * rows, cols)
    flags = jnp.concatenate([flags, jnp.zeros((slots * rows, LANES - cols), F32)], 1)
    flags = jnp.concatenate([flags, jnp.zeros((LANES - slots * rows, LANES), F32)], 0)
    turned = jnp.transpose(flags)[:cols]
    held_ref[...] = turned
    for copy in copies[1:]:
        copy.wait()
    for end, (low, far) in enumerate(STRIPS):
        for row in range(rows):
            base = 2 * STEPS * row
            flat[end, base : base + STEPS] = strips[end, 0, row, low : low + STEPS]
            weight = strips[end, 1, row, low : low + STEPS] - weight_middle
            flat[end, base + STEPS : base + 2 * STEPS] = weight
            column = row + end * (cols - SIDE)
            flat[end, base + STEPS + far, :LANES] = turned[column]
    parity = lax.rem(lax.axis_index("fcol"), 2)
    odd_ref[...] = flat[parity].astype(BF16)
    even_ref[...] = flat[1 - parity].astype(BF16)


def own_kernel(ends, stencil_hbm, right_hbm, weight_hbm, held_ref, *refs):
    whole_refs = refs[:ends]
    stencil_ref, mask, residual, weight, arrived = refs[ends:]
    slots = mask.shape[0]
    own_rows, own_cols, _ = residual.shape
    place, _, _ = row_places(ends, own_rows)
    slot_place = slot_places(ends, slots)
    copies = []
    for row in range(own_rows):
        for source, target in ((right_hbm, residual), (weight_hbm, weight)):
            copies.append(
                pltpu.make_async_copy(
                    source.at[row], target.at[place[row]], arrived.at[3 + len(copies)]
                )
            )
    stencil_copies = [
        pltpu.make_async_copy(
            stencil_hbm.at[pl.ds(slot, 3)],
            stencil_ref.at[pl.ds(slot_place[slot], 3)],
            arrived.at[slot // 3],
        )
        for slot in range(0, slots, 3)
    ]
    for copy in copies + stencil_copies:
        copy.start()
    flags = held_ref[...]
    spread_flags(ends, mask, flags, own_rows, list(enumerate(place)))
    for copy in copies:
        copy.wait()
    for whole_ref, (sent, far) in zip(whole_refs, rows_sent(ends, own_rows)):
        for row, at in enumerate(sent):
            whole_ref[row, :own_cols] = residual[at].astype(BF16)
            if row == far:
                whole_ref[row, own_cols:, :LANES] = flags.astype(BF16)
                whole_ref[row, own_cols:, LANES:] = flags.astype(BF16)
            else:
                whole_ref[row, own_cols:] = (weight[at] - weight_middle).astype(BF16)
    for copy in stencil_copies:
        copy.wait()


def rows_kernel(ends, *refs):
    for index in range(ends):
        whole_ref = refs[index]
        mask, residual, weight = refs[ends + 3 * index : ends + 3 * index + 3]
        own_rows, own_cols = mask.shape[1], residual.shape[1]
        for row in range(STEPS):
            strip = whole_ref[row].astype(F32)
            residual[row] = strip[:own_cols]
            weight[row] = strip[own_cols:] + weight_middle
        far = rows_sent(ends, own_rows)[index][1]
        flags = whole_ref[far, own_cols:, :LANES].astype(F32)
        places = row_places(ends, own_rows)[1][index]
        spread_flags(ends, mask, flags, own_rows, places)


def lay_sides(ends, odd_ref, even_ref, places, own_rows, mask, right, weight, strips, turned):
    first_of_even = lax.rem(lax.axis_index("fcol"), 2) == 0
    strips[0] = jnp.where(first_of_even, even_ref[...], odd_ref[...]).astype(F32)
    strips[1] = jnp.where(first_of_even, odd_ref[...], even_ref[...]).astype(F32)
    right[...] = jnp.zeros(right.shape, F32)
    weight[...] = jnp.zeros(weight.shape, F32)
    for end, (low, far) in enumerate(STRIPS):
        side = slice(end * SIDE + low, end * SIDE + low + STEPS)
        for row, at in places:
            flat = 2 * STEPS * row
            right[at, side, :] = strips[end, flat : flat + STEPS]
            weight[at, side, :] = strips[end, flat + STEPS : flat + 2 * STEPS] + weight_middle
        for column in range(SIDE):
            flat = 2 * STEPS * column + STEPS + far
            turned[end * SIDE + column] = strips[end, flat, :LANES]
    spread_flags(ends, mask, turned[...], own_rows, places)


def sides_kernel(ends, odd_ref, even_ref, mask, right, weight, strips, turned):
    own_rows = right.shape[0]
    places = list(enumerate(row_places(ends, own_rows)[0]))
    lay_sides(ends, odd_ref, even_ref, places, own_rows, mask, right, weight, strips, turned)


def smooth_kernel(ends, *refs):
    stencil_ref, *beside = refs[:4]
    sides = refs[4 : 4 + ends]
    own_block = refs[4 + ends : 7 + ends]
    halo_blocks = [refs[7 + ends + 3 * i : 10 + ends + 3 * i] for i in range(ends)]
    solution_ref, coarse_ref, residual, weight, direction, shifted = refs[7 + 4 * ends :][:6]
    far_masks, far_right, far_weight, strips, turned, smoothed, summed = refs[13 + 4 * ends :]
    own_rows, own_cols, pixels = solution_ref.shape
    slots = beside[0].shape[0]
    rows, cols, _ = residual.shape
    place, halos, ahead = row_places(ends, own_rows)
    blocks = halo_blocks[:ahead] + [own_block] + halo_blocks[ahead:]
    bases = [0]
    for block in blocks:
        bases.append(bases[-1] + block[1].shape[0])
    if bases[-1] < rows:
        unused = jnp.zeros((rows - bases[-1], cols, pixels), F32)
        residual[bases[-1] :] = unused
        weight[bases[-1] :] = unused
    own_start = bases[ahead]

    def flags_of(masks, slot, first, last):
        pieces = []
        for base, block, flags in zip(bases, blocks, masks):
            low, high = max(first - base, 0), min(last - base, block[1].shape[0])
            if low < high:
                pieces.append(flags[slot, low:high])
        return pieces[0] if len(pieces) == 1 else jnp.concatenate(pieces, 0)

    for base, block in zip(bases, blocks):
        here = slice(base, base + block[1].shape[0])
        residual[here, :own_cols, :] = block[1][...]
        weight[here, :own_cols, :] = block[2][...]
    here = slice(own_start, own_start + own_rows)
    residual[here, own_cols:, :] = beside[1][...]
    weight[here, own_cols:, :] = beside[2][...]
    halo_bases = bases[:ahead] + bases[ahead + 1 : -1]
    for index, (base, sides_ref, places) in enumerate(zip(halo_bases, sides, halos)):
        lay_sides(
            ends, sides_ref.at[0], sides_ref.at[1], places, own_rows, far_masks.at[index],
            far_right.at[index], far_weight.at[index], strips.at[index], turned,
        )
        count = halo_blocks[index][1].shape[0]
        residual[base : base + count, own_cols:, :] = far_right[index, :count]
        weight[base : base + count, own_cols:, :] = far_weight[index, :count]
    side_masks = [far_masks.at[index] for index in range(ends)]
    side_masks = side_masks[:ahead] + [beside[0]] + side_masks[ahead:]

    def put_direction(slot, start, count, value):
        here = slice(start + 1, start + 1 + count)
        shifted[slot, 1, here] = value.astype(BF16)
        shifted[slot, 0, here] = pltpu.roll(value, 1, 1).astype(BF16)
        shifted[slot, 2, here] = pltpu.roll(value, cols - 1, 1).astype(BF16)

    edge = jnp.zeros((cols, pixels), BF16)
    for slot in range(2):
        for move in range(3):
            shifted[slot, move, 0] = edge
            shifted[slot, move, rows + 1] = edge
    value = residual[...] * (1.0 / center)
    direction[...] = value
    put_direction(0, 0, rows, value)

    own = slice(own_start, own_start + own_rows)
    stencil = stencil_ref[...].reshape(slots * pixels, pixels)
    factors = step_factors()
    for step in range(STEPS):
        now, later = step % 2, 1 - step % 2
        last = step == STEPS - 1
        moved = direction[own, :own_cols, :]
        smoothed[...] = moved if step == 0 else smoothed[...] + moved
        margin = STEPS - 1 - step
        count = own_rows + ends * margin
        start = own_start - (ends - 1) * margin
        width = own_cols if last else cols
        pieces = -(-count // PIECE_ROWS)
        cuts = [start + count * i // pieces for i in range(pieces + 1)]
        for base, size in zip(cuts, (high - low for low, high in zip(cuts, cuts[1:]))):
            here = slice(base, base + size)
            picked = []
            for slot in range(slots):
                across, along = slot // 3, slot % 3
                source = shifted[now, along, base + across : base + across + size, :width, :]
                if slot == slots // 2:
                    picked.append(source)
                    continue
                keep = flags_of([block[0] for block in blocks], slot, base, base + size)
                if not last:
                    keep_sides = flags_of(side_masks, slot, base, base + size)
                    keep = jnp.concatenate([keep, keep_sides], 1)
                picked.append(source[:, :, :LANES] * keep)
                picked.append(source[:, :, LANES:] * keep)
            picked = jnp.concatenate(picked, 2).reshape(size * width, slots * pixels)
            coupled = jnp.dot(picked, stencil, preferred_element_type=F32)
            coupled = coupled.reshape(size, width, pixels)
            moved = direction[here, :width, :]
            left = residual[here, :width, :] - (weight[here, :width, :] * moved + coupled)
            residual[here, :width, :] = left
            if not last:
                a, b = factors[step]
                value = b * left if a == 0.0 else a * moved + b * left
                direction[here, :width, :] = value
                put_direction(later, base, size, value)

    fine = residual[own, :own_cols, :].reshape(own_rows * own_cols, pixels)
    high = fine.astype(BF16)
    low = (fine - high.astype(F32)).astype(BF16)
    quarter = pixels // 4
    from_pixel = lax.broadcasted_iota(jnp.int32, (pixels, LANES), 0) // 4
    to_pixel = lax.broadcasted_iota(jnp.int32, (pixels, LANES), 1)
    adder = jnp.where(from_pixel == to_pixel, 1.0, 0.0).astype(BF16)
    total = jnp.dot(high, adder, preferred_element_type=F32) + jnp.dot(
        low, adder, preferred_element_type=F32
    )
    summed[...] = total.reshape(own_rows, own_cols, LANES)
    for row in range(own_rows // 2):
        pieces = []
        for across in range(2):
            for along in range(2):
                at = place[2 * row + across]
                piece = summed[at, pl.ds(along, own_cols // 2, stride=2), :]
                pieces.append(piece[:, :quarter])
        coarse_ref[row] = jnp.concatenate(pieces, 1).astype(BF16)
    for row, at in enumerate(place):
        solution_ref[row] = smoothed[at]


def widen_kernel(block_ref, out_hbm, wide, sent):
    rows, ring, _, _ = wide.shape
    half = ring // 2
    own_half = lax.axis_index("fcol") // half
    copies = []
    for row in range(rows):
        for i in range(half):
            wide[row, own_half * half + i] = block_ref[i, 0, row].astype(F32)
            wide[row, (1 - own_half) * half + i] = block_ref[i, 1, row].astype(F32)
        copies.append(pltpu.make_async_copy(wide.at[row], out_hbm.at[row], sent.at[row]))
        copies[-1].start()
    for copy in copies:
        copy.wait()


def body(right_side, noise_weight, stencils, neighbours):
    rows, cols, pixels = right_side.shape
    slots = stencils.shape[0]
    pairs, ring = lax.axis_size("frow"), lax.axis_size("fcol")
    swaps = [
        [(i, j) for low in range(first, ring - 1, 2) for i, j in ((low, low + 1), (low + 1, low))]
        for first in (0, 1)
    ]
    near = jnp.transpose(neighbours, (2, 0, 1))
    right_hbm, weight_hbm, near_hbm, stencil_hbm = [
        pltpu.with_memory_space_constraint(array, pltpu.HBM)
        for array in (right_side, noise_weight, near, stencils)
    ]
    small = pltpu.CompilerParams(vmem_limit_bytes=8 * 1024 * 1024)

    side = pltpu.VMEM((2 * STEPS * rows, pixels), BF16)
    odd, even, held = pl.pallas_call(
        edge_kernel,
        out_shape=(side, side, pltpu.VMEM((cols, LANES), F32)),
        in_specs=[HBM_SPEC] * 3,
        out_specs=(VMEM_SPEC,) * 3,
        scratch_shapes=[
            pltpu.VMEM((2, 2, rows, SIDE, pixels), F32),
            pltpu.VMEM((2, 2 * STEPS * rows, pixels), F32),
            pltpu.VMEM((slots, rows, cols), jnp.int32),
            pltpu.SemaphoreType.DMA((5,)),
        ],
        compiler_params=small,
        name="edges",
    )(right_hbm, weight_hbm, near_hbm)

    odd_side = lax.ppermute(odd, "fcol", swaps[1])
    even_side = lax.ppermute(even, "fcol", swaps[0])
    if pairs == 2:
        moves = [[(0, 1), (1, 0)]]
    else:
        moves = [
            [(i, i + 1) for i in range(pairs - 1)],
            [(i + 1, i) for i in range(pairs - 1)],
        ]
    ends = len(moves)

    def block_types(count):
        return (
            pltpu.VMEM((slots, rows, cols, LANES), BF16),
            pltpu.VMEM((count, cols, pixels), F32),
            pltpu.VMEM((count, cols, pixels), F32),
        )

    *sent, stencil, mask, right, weight = pl.pallas_call(
        functools.partial(own_kernel, ends),
        out_shape=(pltpu.VMEM((STEPS, 2 * cols, pixels), BF16),) * ends
        + (pltpu.VMEM(stencils.shape, stencils.dtype),)
        + block_types(rows),
        in_specs=[HBM_SPEC] * 3 + [VMEM_SPEC],
        out_specs=(VMEM_SPEC,) * (4 + ends),
        scratch_shapes=[pltpu.SemaphoreType.DMA((3 + 2 * rows,))],
        compiler_params=small,
        cost_estimate=pl.CostEstimate(flops=0, bytes_accessed=6000000, transcendentals=0),
        name="own",
    )(stencil_hbm, right_hbm, weight_hbm, held)

    wholes = [lax.ppermute(whole, "frow", move) for whole, move in zip(sent, moves)]
    sides = jnp.stack([odd_side, even_side])
    sides_held = [lax.ppermute(sides, "frow", move) for move in moves]
    halo_blocks = pl.pallas_call(
        functools.partial(rows_kernel, ends),
        out_shape=block_types(STEPS) * ends,
        in_specs=[VMEM_SPEC] * ends,
        out_specs=(VMEM_SPEC,) * (3 * ends),
        compiler_params=small,
        cost_estimate=pl.CostEstimate(flops=0, bytes_accessed=4000000, transcendentals=0),
        name="rows",
    )(*wholes)

    side_types = (
        pltpu.VMEM((slots, rows, 2 * SIDE, LANES), BF16),
        pltpu.VMEM((rows, 2 * SIDE, pixels), F32),
        pltpu.VMEM((rows, 2 * SIDE, pixels), F32),
    )
    beside = pl.pallas_call(
        functools.partial(sides_kernel, ends),
        out_shape=side_types,
        in_specs=[VMEM_SPEC] * 2,
        out_specs=(VMEM_SPEC,) * 3,
        scratch_shapes=[
            pltpu.VMEM((2, 2 * STEPS * rows, pixels), F32),
            pltpu.VMEM((2 * SIDE, LANES), F32),
        ],
        compiler_params=small,
        cost_estimate=pl.CostEstimate(flops=0, bytes_accessed=1000000, transcendentals=0),
        name="sides",
    )(odd_side, even_side)

    cols_held = cols + 2 * SIDE
    rows_held = 2 * rows if ends == 1 else rows + 2 * STEPS
    solution, coarse = pl.pallas_call(
        functools.partial(smooth_kernel, ends),
        out_shape=(
            jax.ShapeDtypeStruct((rows, cols, pixels), F32),
            pltpu.VMEM((rows // 2, cols // 2, pixels), BF16),
        ),
        in_specs=[VMEM_SPEC] * (7 + 4 * ends),
        out_specs=(VMEM_SPEC,) * 2,
        scratch_shapes=[
            pltpu.VMEM((rows_held, cols_held, pixels), F32),
            pltpu.VMEM((rows_held, cols_held, pixels), F32),
            pltpu.VMEM((rows_held, cols_held, pixels), F32),
            pltpu.VMEM((2, 3, rows_held + 2, cols_held, pixels), BF16),
            pltpu.VMEM((ends, slots, rows, 2 * SIDE, LANES), BF16),
            pltpu.VMEM((ends, rows, 2 * SIDE, pixels), F32),
            pltpu.VMEM((ends, rows, 2 * SIDE, pixels), F32),
            pltpu.VMEM((ends, 2, 2 * STEPS * rows, pixels), F32),
            pltpu.VMEM((2 * SIDE, LANES), F32),
            pltpu.VMEM((rows, cols, pixels), F32),
            pltpu.VMEM((rows, cols, LANES), F32),
        ],
        compiler_params=pltpu.CompilerParams(vmem_limit_bytes=24 * 1024 * 1024),
        name="smooth",
    )(stencil, *beside, *sides_held, mask, right, weight, *halo_blocks)

    half = ring // 2
    across = [(i, (i + half) % ring) for i in range(ring)]
    pair = jnp.stack([coarse, lax.ppermute(coarse, "fcol", across)])
    halves = [list(range(half)), list(range(half, ring))]
    spread = jnp.broadcast_to(pair[None], (half,) + pair.shape)
    block = lax.all_to_all(spread, "fcol", 0, 0, axis_index_groups=halves)
    widened = (rows // 2, ring, cols // 2, pixels)
    gathered = pl.pallas_call(
        widen_kernel,
        out_shape=jax.ShapeDtypeStruct(widened, F32),
        in_specs=[VMEM_SPEC],
        out_specs=HBM_SPEC,
        scratch_shapes=[pltpu.VMEM(widened, F32), pltpu.SemaphoreType.DMA((rows // 2,))],
        compiler_params=small,
        name="widen",
    )(block)
    return solution, gathered.reshape(rows // 2, ring * (cols // 2), pixels)


def solution(mesh):
    placed = (P("frow", "fcol", None), P("frow", "fcol", None), P(), P("frow", "fcol", None))
    return jax.shard_map(
        body,
        mesh=mesh,
        in_specs=placed,
        out_specs=(P("frow", "fcol", None), P("frow", None, None)),
        check_vma=False,
    )
```

```python
import functools

import jax
import jax.numpy as jnp
from jax import lax
from jax.experimental import pallas as pl
from jax.experimental.pallas import tpu as pltpu
from jax.sharding import PartitionSpec as P

DEG = 3
SWEEPS = 2
STEPS = DEG * SWEEPS
SIDE = 8
LANES = 128
STRIPS = ((0, STEPS - 1), (SIDE - STEPS, 0))
PIECE_ROWS = 4

lower_edge = 1.5
upper_edge = 6.0
center = 0.5 * (upper_edge + lower_edge)
half_width = 0.5 * (upper_edge - lower_edge)
weight_middle = 3.75

F32 = jnp.float32
BF16 = jnp.bfloat16
HBM_SPEC = pl.BlockSpec(memory_space=pl.ANY)
VMEM_SPEC = pl.BlockSpec(memory_space=pltpu.VMEM)


def step_factors():
    spread_ratio = center / half_width
    factors = []
    for sweep in range(SWEEPS):
        ratio = 1.0 / spread_ratio
        for step in range(DEG):
            if step < DEG - 1:
                ratio_next = 1.0 / (2.0 * spread_ratio - ratio)
                factors.append((ratio_next * ratio, 2.0 * ratio_next / half_width))
                ratio = ratio_next
            else:
                factors.append((0.0, 1.0 / center))
    return factors


def row_places(ends, own_rows):
    if ends == 1:
        flip = lax.axis_index("frow")
        place = [row + flip * (own_rows - 1 - 2 * row) for row in range(own_rows)]
        return place, [list(enumerate(place))], 0
    above = [(own_rows - STEPS + row, row) for row in range(STEPS)]
    below = [(row, row) for row in range(STEPS)]
    return list(range(own_rows)), [above, below], 1


def rows_sent(ends, own_rows):
    if ends == 1:
        return [([own_rows - 1 - row for row in range(STEPS)], STEPS - 1)]
    return [
        ([own_rows - STEPS + row for row in range(STEPS)], 0),
        (list(range(STEPS)), STEPS - 1),
    ]


def slot_places(ends, slots):
    if ends == 1:
        flip = lax.axis_index("frow")
        return [(slot // 3 + flip * (2 - 2 * (slot // 3))) * 3 + slot % 3 for slot in range(slots)]
    return list(range(slots))


def spread_flags(ends, mask, flags, own_rows, places):
    slots, _, cols, _ = mask.shape
    slot_place = slot_places(ends, slots)
    for slot in range(slots):
        if slot == slots // 2:
            continue
        for row, at in places:
            lane = slot * own_rows + row
            column = jnp.broadcast_to(flags[:, lane : lane + 1], (cols, LANES))
            mask[slot_place[slot], at] = column.astype(BF16)


def edge_kernel(right_hbm, weight_hbm, near_hbm, *refs):
    odd_ref, even_ref, held_ref, strips, flat, near_ref, arrived = refs
    slots, rows, cols = near_ref.shape
    copies = [pltpu.make_async_copy(near_hbm, near_ref, arrived.at[4])]
    for end, start in enumerate((0, cols - SIDE)):
        for kind, source in enumerate((right_hbm, weight_hbm)):
            copies.append(
                pltpu.make_async_copy(
                    source.at[:, pl.ds(start, SIDE)],
                    strips.at[end, kind],
                    arrived.at[2 * end + kind],
                )
            )
    for copy in copies:
        copy.start()
    copies[0].wait()
    flags = jnp.where(near_ref[...] >= 0, 1.0, 0.0).astype(F32).reshape(slots * rows, cols)
    flags = jnp.concatenate([flags, jnp.zeros((slots * rows, LANES - cols), F32)], 1)
    flags = jnp.concatenate([flags, jnp.zeros((LANES - slots * rows, LANES), F32)], 0)
    turned = jnp.transpose(flags)[:cols]
    held_ref[...] = turned
    for copy in copies[1:]:
        copy.wait()
    for end, (low, far) in enumerate(STRIPS):
        for row in range(rows):
            base = 2 * STEPS * row
            flat[end, base : base + STEPS] = strips[end, 0, row, low : low + STEPS]
            weight = strips[end, 1, row, low : low + STEPS] - weight_middle
            flat[end, base + STEPS : base + 2 * STEPS] = weight
            column = row + end * (cols - SIDE)
            flat[end, base + STEPS + far, :LANES] = turned[column]
    parity = lax.rem(lax.axis_index("fcol"), 2)
    odd_ref[...] = flat[parity].astype(BF16)
    even_ref[...] = flat[1 - parity].astype(BF16)


def own_kernel(ends, stencil_hbm, right_hbm, weight_hbm, held_ref, *refs):
    whole_refs = refs[:ends]
    stencil_ref, mask, residual, weight, arrived = refs[ends:]
    slots = mask.shape[0]
    own_rows, own_cols, _ = residual.shape
    place, _, _ = row_places(ends, own_rows)
    slot_place = slot_places(ends, slots)
    copies = []
    for row in range(own_rows):
        for source, target in ((right_hbm, residual), (weight_hbm, weight)):
            copies.append(
                pltpu.make_async_copy(
                    source.at[row], target.at[place[row]], arrived.at[3 + len(copies)]
                )
            )
    stencil_copies = [
        pltpu.make_async_copy(
            stencil_hbm.at[pl.ds(slot, 3)],
            stencil_ref.at[pl.ds(slot_place[slot], 3)],
            arrived.at[slot // 3],
        )
        for slot in range(0, slots, 3)
    ]
    for copy in copies + stencil_copies:
        copy.start()
    flags = held_ref[...]
    spread_flags(ends, mask, flags, own_rows, list(enumerate(place)))
    for copy in copies:
        copy.wait()
    for whole_ref, (sent, far) in zip(whole_refs, rows_sent(ends, own_rows)):
        for row, at in enumerate(sent):
            whole_ref[row, :own_cols] = residual[at].astype(BF16)
            if row == far:
                whole_ref[row, own_cols:, :LANES] = flags.astype(BF16)
                whole_ref[row, own_cols:, LANES:] = flags.astype(BF16)
            else:
                whole_ref[row, own_cols:] = (weight[at] - weight_middle).astype(BF16)
    for copy in stencil_copies:
        copy.wait()


def rows_kernel(ends, *refs):
    for index in range(ends):
        whole_ref = refs[index]
        mask, residual, weight = refs[ends + 3 * index : ends + 3 * index + 3]
        own_rows, own_cols = mask.shape[1], residual.shape[1]
        for row in range(STEPS):
            strip = whole_ref[row].astype(F32)
            residual[row] = strip[:own_cols]
            weight[row] = strip[own_cols:] + weight_middle
        far = rows_sent(ends, own_rows)[index][1]
        flags = whole_ref[far, own_cols:, :LANES].astype(F32)
        places = row_places(ends, own_rows)[1][index]
        spread_flags(ends, mask, flags, own_rows, places)


def lay_sides(ends, odd_ref, even_ref, places, own_rows, mask, right, weight, strips, turned):
    first_of_even = lax.rem(lax.axis_index("fcol"), 2) == 0
    strips[0] = jnp.where(first_of_even, even_ref[...], odd_ref[...]).astype(F32)
    strips[1] = jnp.where(first_of_even, odd_ref[...], even_ref[...]).astype(F32)
    right[...] = jnp.zeros(right.shape, F32)
    weight[...] = jnp.zeros(weight.shape, F32)
    for end, (low, far) in enumerate(STRIPS):
        side = slice(end * SIDE + low, end * SIDE + low + STEPS)
        for row, at in places:
            flat = 2 * STEPS * row
            right[at, side, :] = strips[end, flat : flat + STEPS]
            weight[at, side, :] = strips[end, flat + STEPS : flat + 2 * STEPS] + weight_middle
        for column in range(SIDE):
            flat = 2 * STEPS * column + STEPS + far
            turned[end * SIDE + column] = strips[end, flat, :LANES]
    spread_flags(ends, mask, turned[...], own_rows, places)


def sides_kernel(ends, odd_ref, even_ref, mask, right, weight, strips, turned):
    own_rows = right.shape[0]
    places = list(enumerate(row_places(ends, own_rows)[0]))
    lay_sides(ends, odd_ref, even_ref, places, own_rows, mask, right, weight, strips, turned)


def smooth_kernel(ends, *refs):
    stencil_ref, *beside = refs[:4]
    sides = refs[4 : 4 + ends]
    own_block = refs[4 + ends : 7 + ends]
    halo_blocks = [refs[7 + ends + 3 * i : 10 + ends + 3 * i] for i in range(ends)]
    solution_ref, coarse_ref, residual, weight, direction, shifted = refs[7 + 4 * ends :][:6]
    far_masks, far_right, far_weight, strips, turned, smoothed, summed = refs[13 + 4 * ends :]
    own_rows, own_cols, pixels = solution_ref.shape
    slots = beside[0].shape[0]
    rows, cols, _ = residual.shape
    place, halos, ahead = row_places(ends, own_rows)
    blocks = halo_blocks[:ahead] + [own_block] + halo_blocks[ahead:]
    bases = [0]
    for block in blocks:
        bases.append(bases[-1] + block[1].shape[0])
    if bases[-1] < rows:
        unused = jnp.zeros((rows - bases[-1], cols, pixels), F32)
        residual[bases[-1] :] = unused
        weight[bases[-1] :] = unused
    own_start = bases[ahead]

    def flags_of(masks, slot, first, last):
        pieces = []
        for base, block, flags in zip(bases, blocks, masks):
            low, high = max(first - base, 0), min(last - base, block[1].shape[0])
            if low < high:
                pieces.append(flags[slot, low:high])
        return pieces[0] if len(pieces) == 1 else jnp.concatenate(pieces, 0)

    for base, block in zip(bases, blocks):
        here = slice(base, base + block[1].shape[0])
        residual[here, :own_cols, :] = block[1][...]
        weight[here, :own_cols, :] = block[2][...]
    here = slice(own_start, own_start + own_rows)
    residual[here, own_cols:, :] = beside[1][...]
    weight[here, own_cols:, :] = beside[2][...]
    halo_bases = bases[:ahead] + bases[ahead + 1 : -1]
    for index, (base, sides_ref, places) in enumerate(zip(halo_bases, sides, halos)):
        lay_sides(
            ends, sides_ref.at[0], sides_ref.at[1], places, own_rows, far_masks.at[index],
            far_right.at[index], far_weight.at[index], strips.at[index], turned,
        )
        count = halo_blocks[index][1].shape[0]
        residual[base : base + count, own_cols:, :] = far_right[index, :count]
        weight[base : base + count, own_cols:, :] = far_weight[index, :count]
    side_masks = [far_masks.at[index] for index in range(ends)]
    side_masks = side_masks[:ahead] + [beside[0]] + side_masks[ahead:]

    def put_direction(slot, start, count, value):
        here = slice(start + 1, start + 1 + count)
        shifted[slot, 1, here] = value.astype(BF16)
        shifted[slot, 0, here] = pltpu.roll(value, 1, 1).astype(BF16)
        shifted[slot, 2, here] = pltpu.roll(value, cols - 1, 1).astype(BF16)

    edge = jnp.zeros((cols, pixels), BF16)
    for slot in range(2):
        for move in range(3):
            shifted[slot, move, 0] = edge
            shifted[slot, move, rows + 1] = edge
    value = residual[...] * (1.0 / center)
    direction[...] = value
    put_direction(0, 0, rows, value)

    own = slice(own_start, own_start + own_rows)
    factors = step_factors()
    for step in range(STEPS):
        now, later = step % 2, 1 - step % 2
        last = step == STEPS - 1
        moved = direction[own, :own_cols, :]
        smoothed[...] = moved if step == 0 else smoothed[...] + moved
        margin = STEPS - 1 - step
        count = own_rows + ends * margin
        start = own_start - (ends - 1) * margin
        width = own_cols if last else cols
        pieces = -(-count // PIECE_ROWS)
        cuts = [start + count * i // pieces for i in range(pieces + 1)]
        for base, size in zip(cuts, (high - low for low, high in zip(cuts, cuts[1:]))):
            here = slice(base, base + size)
            coupled = jnp.zeros((size * width, pixels), F32)
            for slot in range(slots):
                across, along = slot // 3, slot % 3
                source = shifted[now, along, base + across : base + across + size, :width, :]
                if slot != slots // 2:
                    keep = flags_of([block[0] for block in blocks], slot, base, base + size)
                    if not last:
                        keep_sides = flags_of(side_masks, slot, base, base + size)
                        keep = jnp.concatenate([keep, keep_sides], 1)
                    source = jnp.concatenate(
                        [source[:, :, :LANES] * keep, source[:, :, LANES:] * keep], 2
                    )
                coupled += jnp.dot(
                    source.reshape(size * width, pixels),
                    stencil_ref[slot],
                    preferred_element_type=F32,
                )
            coupled = coupled.reshape(size, width, pixels)
            moved = direction[here, :width, :]
            left = residual[here, :width, :] - (weight[here, :width, :] * moved + coupled)
            residual[here, :width, :] = left
            if not last:
                a, b = factors[step]
                value = b * left if a == 0.0 else a * moved + b * left
                direction[here, :width, :] = value
                put_direction(later, base, size, value)

    fine = residual[own, :own_cols, :].reshape(own_rows * own_cols, pixels)
    high = fine.astype(BF16)
    low = (fine - high.astype(F32)).astype(BF16)
    quarter = pixels // 4
    from_pixel = lax.broadcasted_iota(jnp.int32, (pixels, LANES), 0) // 4
    to_pixel = lax.broadcasted_iota(jnp.int32, (pixels, LANES), 1)
    adder = jnp.where(from_pixel == to_pixel, 1.0, 0.0).astype(BF16)
    total = jnp.dot(high, adder, preferred_element_type=F32) + jnp.dot(
        low, adder, preferred_element_type=F32
    )
    summed[...] = total.reshape(own_rows, own_cols, LANES)
    for row in range(own_rows // 2):
        pieces = []
        for across in range(2):
            for along in range(2):
                at = place[2 * row + across]
                piece = summed[at, pl.ds(along, own_cols // 2, stride=2), :]
                pieces.append(piece[:, :quarter])
        coarse_ref[row] = jnp.concatenate(pieces, 1).astype(BF16)
    for row, at in enumerate(place):
        solution_ref[row] = smoothed[at]


def widen_kernel(block_ref, out_hbm, wide, sent):
    rows, ring, _, _ = wide.shape
    half = ring // 2
    own_half = lax.axis_index("fcol") // half
    copies = []
    for row in range(rows):
        for i in range(half):
            wide[row, own_half * half + i] = block_ref[i, 0, row].astype(F32)
            wide[row, (1 - own_half) * half + i] = block_ref[i, 1, row].astype(F32)
        copies.append(pltpu.make_async_copy(wide.at[row], out_hbm.at[row], sent.at[row]))
        copies[-1].start()
    for copy in copies:
        copy.wait()


def body(right_side, noise_weight, stencils, neighbours):
    rows, cols, pixels = right_side.shape
    slots = stencils.shape[0]
    pairs, ring = lax.axis_size("frow"), lax.axis_size("fcol")
    swaps = [
        [(i, j) for low in range(first, ring - 1, 2) for i, j in ((low, low + 1), (low + 1, low))]
        for first in (0, 1)
    ]
    near = jnp.transpose(neighbours, (2, 0, 1))
    right_hbm, weight_hbm, near_hbm, stencil_hbm = [
        pltpu.with_memory_space_constraint(array, pltpu.HBM)
        for array in (right_side, noise_weight, near, stencils)
    ]
    small = pltpu.CompilerParams(vmem_limit_bytes=8 * 1024 * 1024)

    side = pltpu.VMEM((2 * STEPS * rows, pixels), BF16)
    odd, even, held = pl.pallas_call(
        edge_kernel,
        out_shape=(side, side, pltpu.VMEM((cols, LANES), F32)),
        in_specs=[HBM_SPEC] * 3,
        out_specs=(VMEM_SPEC,) * 3,
        scratch_shapes=[
            pltpu.VMEM((2, 2, rows, SIDE, pixels), F32),
            pltpu.VMEM((2, 2 * STEPS * rows, pixels), F32),
            pltpu.VMEM((slots, rows, cols), jnp.int32),
            pltpu.SemaphoreType.DMA((5,)),
        ],
        compiler_params=small,
        name="edges",
    )(right_hbm, weight_hbm, near_hbm)

    odd_side = lax.ppermute(odd, "fcol", swaps[1])
    even_side = lax.ppermute(even, "fcol", swaps[0])
    if pairs == 2:
        moves = [[(0, 1), (1, 0)]]
    else:
        moves = [
            [(i, i + 1) for i in range(pairs - 1)],
            [(i + 1, i) for i in range(pairs - 1)],
        ]
    ends = len(moves)

    def block_types(count):
        return (
            pltpu.VMEM((slots, rows, cols, LANES), BF16),
            pltpu.VMEM((count, cols, pixels), F32),
            pltpu.VMEM((count, cols, pixels), F32),
        )

    *sent, stencil, mask, right, weight = pl.pallas_call(
        functools.partial(own_kernel, ends),
        out_shape=(pltpu.VMEM((STEPS, 2 * cols, pixels), BF16),) * ends
        + (pltpu.VMEM(stencils.shape, stencils.dtype),)
        + block_types(rows),
        in_specs=[HBM_SPEC] * 3 + [VMEM_SPEC],
        out_specs=(VMEM_SPEC,) * (4 + ends),
        scratch_shapes=[pltpu.SemaphoreType.DMA((3 + 2 * rows,))],
        compiler_params=small,
        cost_estimate=pl.CostEstimate(flops=0, bytes_accessed=6000000, transcendentals=0),
        name="own",
    )(stencil_hbm, right_hbm, weight_hbm, held)

    wholes = [lax.ppermute(whole, "frow", move) for whole, move in zip(sent, moves)]
    sides = jnp.stack([odd_side, even_side])
    sides_held = [lax.ppermute(sides, "frow", move) for move in moves]
    halo_blocks = pl.pallas_call(
        functools.partial(rows_kernel, ends),
        out_shape=block_types(STEPS) * ends,
        in_specs=[VMEM_SPEC] * ends,
        out_specs=(VMEM_SPEC,) * (3 * ends),
        compiler_params=small,
        cost_estimate=pl.CostEstimate(flops=0, bytes_accessed=4000000, transcendentals=0),
        name="rows",
    )(*wholes)

    side_types = (
        pltpu.VMEM((slots, rows, 2 * SIDE, LANES), BF16),
        pltpu.VMEM((rows, 2 * SIDE, pixels), F32),
        pltpu.VMEM((rows, 2 * SIDE, pixels), F32),
    )
    beside = pl.pallas_call(
        functools.partial(sides_kernel, ends),
        out_shape=side_types,
        in_specs=[VMEM_SPEC] * 2,
        out_specs=(VMEM_SPEC,) * 3,
        scratch_shapes=[
            pltpu.VMEM((2, 2 * STEPS * rows, pixels), F32),
            pltpu.VMEM((2 * SIDE, LANES), F32),
        ],
        compiler_params=small,
        cost_estimate=pl.CostEstimate(flops=0, bytes_accessed=1000000, transcendentals=0),
        name="sides",
    )(odd_side, even_side)

    cols_held = cols + 2 * SIDE
    rows_held = 2 * rows if ends == 1 else rows + 2 * STEPS
    solution, coarse = pl.pallas_call(
        functools.partial(smooth_kernel, ends),
        out_shape=(
            jax.ShapeDtypeStruct((rows, cols, pixels), F32),
            pltpu.VMEM((rows // 2, cols // 2, pixels), BF16),
        ),
        in_specs=[VMEM_SPEC] * (7 + 4 * ends),
        out_specs=(VMEM_SPEC,) * 2,
        scratch_shapes=[
            pltpu.VMEM((rows_held, cols_held, pixels), F32),
            pltpu.VMEM((rows_held, cols_held, pixels), F32),
            pltpu.VMEM((rows_held, cols_held, pixels), F32),
            pltpu.VMEM((2, 3, rows_held + 2, cols_held, pixels), BF16),
            pltpu.VMEM((ends, slots, rows, 2 * SIDE, LANES), BF16),
            pltpu.VMEM((ends, rows, 2 * SIDE, pixels), F32),
            pltpu.VMEM((ends, rows, 2 * SIDE, pixels), F32),
            pltpu.VMEM((ends, 2, 2 * STEPS * rows, pixels), F32),
            pltpu.VMEM((2 * SIDE, LANES), F32),
            pltpu.VMEM((rows, cols, pixels), F32),
            pltpu.VMEM((rows, cols, LANES), F32),
        ],
        compiler_params=pltpu.CompilerParams(vmem_limit_bytes=24 * 1024 * 1024),
        name="smooth",
    )(stencil, *beside, *sides_held, mask, right, weight, *halo_blocks)

    half = ring // 2
    across = [(i, (i + half) % ring) for i in range(ring)]
    pair = jnp.stack([coarse, lax.ppermute(coarse, "fcol", across)])
    halves = [list(range(half)), list(range(half, ring))]
    spread = jnp.broadcast_to(pair[None], (half,) + pair.shape)
    block = lax.all_to_all(spread, "fcol", 0, 0, axis_index_groups=halves)
    widened = (rows // 2, ring, cols // 2, pixels)
    gathered = pl.pallas_call(
        widen_kernel,
        out_shape=jax.ShapeDtypeStruct(widened, F32),
        in_specs=[VMEM_SPEC],
        out_specs=HBM_SPEC,
        scratch_shapes=[pltpu.VMEM(widened, F32), pltpu.SemaphoreType.DMA((rows // 2,))],
        compiler_params=small,
        name="widen",
    )(block)
    return solution, gathered.reshape(rows // 2, ring * (cols // 2), pixels)


def solution(mesh):
    placed = (P("frow", "fcol", None), P("frow", "fcol", None), P(), P("frow", "fcol", None))
    return jax.shard_map(
        body,
        mesh=mesh,
        in_specs=placed,
        out_specs=(P("frow", "fcol", None), P("frow", None, None)),
        check_vma=False,
    )
```

```python
import functools

import jax
import jax.numpy as jnp
from jax import lax
from jax.experimental import pallas as pl
from jax.experimental.pallas import tpu as pltpu
from jax.sharding import PartitionSpec as P

DEG = 3
SWEEPS = 2
STEPS = DEG * SWEEPS
SIDE = 8
LANES = 128
STRIPS = ((0, STEPS - 1), (SIDE - STEPS, 0))
PIECE_ROWS = 7

lower_edge = 1.5
upper_edge = 6.0
center = 0.5 * (upper_edge + lower_edge)
half_width = 0.5 * (upper_edge - lower_edge)
weight_middle = 3.75

F32 = jnp.float32
BF16 = jnp.bfloat16
HBM_SPEC = pl.BlockSpec(memory_space=pl.ANY)
VMEM_SPEC = pl.BlockSpec(memory_space=pltpu.VMEM)


def step_factors():
    spread_ratio = center / half_width
    factors = []
    for sweep in range(SWEEPS):
        ratio = 1.0 / spread_ratio
        for step in range(DEG):
            if step < DEG - 1:
                ratio_next = 1.0 / (2.0 * spread_ratio - ratio)
                factors.append((ratio_next * ratio, 2.0 * ratio_next / half_width))
                ratio = ratio_next
            else:
                factors.append((0.0, 1.0 / center))
    return factors


def row_places(ends, own_rows):
    if ends == 1:
        flip = lax.axis_index("frow")
        place = [row + flip * (own_rows - 1 - 2 * row) for row in range(own_rows)]
        return place, [list(enumerate(place))], 0
    above = [(own_rows - STEPS + row, row) for row in range(STEPS)]
    below = [(row, row) for row in range(STEPS)]
    return list(range(own_rows)), [above, below], 1


def rows_sent(ends, own_rows):
    if ends == 1:
        return [([own_rows - 1 - row for row in range(STEPS)], STEPS - 1)]
    return [
        ([own_rows - STEPS + row for row in range(STEPS)], 0),
        (list(range(STEPS)), STEPS - 1),
    ]


def slot_places(ends, slots):
    if ends == 1:
        flip = lax.axis_index("frow")
        return [(slot // 3 + flip * (2 - 2 * (slot // 3))) * 3 + slot % 3 for slot in range(slots)]
    return list(range(slots))


def spread_flags(ends, mask, flags, own_rows, places):
    slots, _, cols, _ = mask.shape
    slot_place = slot_places(ends, slots)
    for slot in range(slots):
        if slot == slots // 2:
            continue
        for row, at in places:
            lane = slot * own_rows + row
            column = jnp.broadcast_to(flags[:, lane : lane + 1], (cols, LANES))
            mask[slot_place[slot], at] = column.astype(BF16)


def edge_kernel(right_hbm, weight_hbm, near_hbm, *refs):
    odd_ref, even_ref, held_ref, strips, flat, near_ref, arrived = refs
    slots, rows, cols = near_ref.shape
    copies = [pltpu.make_async_copy(near_hbm, near_ref, arrived.at[4])]
    for end, start in enumerate((0, cols - SIDE)):
        for kind, source in enumerate((right_hbm, weight_hbm)):
            copies.append(
                pltpu.make_async_copy(
                    source.at[:, pl.ds(start, SIDE)],
                    strips.at[end, kind],
                    arrived.at[2 * end + kind],
                )
            )
    for copy in copies:
        copy.start()
    copies[0].wait()
    flags = jnp.where(near_ref[...] >= 0, 1.0, 0.0).astype(F32).reshape(slots * rows, cols)
    flags = jnp.concatenate([flags, jnp.zeros((slots * rows, LANES - cols), F32)], 1)
    flags = jnp.concatenate([flags, jnp.zeros((LANES - slots * rows, LANES), F32)], 0)
    turned = jnp.transpose(flags)[:cols]
    held_ref[...] = turned
    for copy in copies[1:]:
        copy.wait()
    for end, (low, far) in enumerate(STRIPS):
        for row in range(rows):
            base = 2 * STEPS * row
            flat[end, base : base + STEPS] = strips[end, 0, row, low : low + STEPS]
            weight = strips[end, 1, row, low : low + STEPS] - weight_middle
            flat[end, base + STEPS : base + 2 * STEPS] = weight
            column = row + end * (cols - SIDE)
            flat[end, base + STEPS + far, :LANES] = turned[column]
    parity = lax.rem(lax.axis_index("fcol"), 2)
    odd_ref[...] = flat[parity].astype(BF16)
    even_ref[...] = flat[1 - parity].astype(BF16)


def own_kernel(ends, stencil_hbm, right_hbm, weight_hbm, held_ref, *refs):
    whole_refs = refs[:ends]
    stencil_ref, mask, residual, weight, arrived = refs[ends:]
    slots = mask.shape[0]
    own_rows, own_cols, _ = residual.shape
    place, _, _ = row_places(ends, own_rows)
    slot_place = slot_places(ends, slots)
    copies = []
    for row in range(own_rows):
        for source, target in ((right_hbm, residual), (weight_hbm, weight)):
            copies.append(
                pltpu.make_async_copy(
                    source.at[row], target.at[place[row]], arrived.at[3 + len(copies)]
                )
            )
    stencil_copies = [
        pltpu.make_async_copy(
            stencil_hbm.at[pl.ds(slot, 3)],
            stencil_ref.at[pl.ds(slot_place[slot], 3)],
            arrived.at[slot // 3],
        )
        for slot in range(0, slots, 3)
    ]
    for copy in copies + stencil_copies:
        copy.start()
    flags = held_ref[...]
    spread_flags(ends, mask, flags, own_rows, list(enumerate(place)))
    for copy in copies:
        copy.wait()
    for whole_ref, (sent, far) in zip(whole_refs, rows_sent(ends, own_rows)):
        for row, at in enumerate(sent):
            whole_ref[row, :own_cols] = residual[at].astype(BF16)
            if row == far:
                whole_ref[row, own_cols:, :LANES] = flags.astype(BF16)
                whole_ref[row, own_cols:, LANES:] = flags.astype(BF16)
            else:
                whole_ref[row, own_cols:] = (weight[at] - weight_middle).astype(BF16)
    for copy in stencil_copies:
        copy.wait()


def rows_kernel(ends, *refs):
    for index in range(ends):
        whole_ref = refs[index]
        mask, residual, weight = refs[ends + 3 * index : ends + 3 * index + 3]
        own_rows, own_cols = mask.shape[1], residual.shape[1]
        for row in range(STEPS):
            strip = whole_ref[row].astype(F32)
            residual[row] = strip[:own_cols]
            weight[row] = strip[own_cols:] + weight_middle
        far = rows_sent(ends, own_rows)[index][1]
        flags = whole_ref[far, own_cols:, :LANES].astype(F32)
        places = row_places(ends, own_rows)[1][index]
        spread_flags(ends, mask, flags, own_rows, places)


def lay_sides(ends, odd_ref, even_ref, places, own_rows, mask, right, weight, strips, turned):
    first_of_even = lax.rem(lax.axis_index("fcol"), 2) == 0
    strips[0] = jnp.where(first_of_even, even_ref[...], odd_ref[...]).astype(F32)
    strips[1] = jnp.where(first_of_even, odd_ref[...], even_ref[...]).astype(F32)
    right[...] = jnp.zeros(right.shape, F32)
    weight[...] = jnp.zeros(weight.shape, F32)
    for end, (low, far) in enumerate(STRIPS):
        side = slice(end * SIDE + low, end * SIDE + low + STEPS)
        for row, at in places:
            flat = 2 * STEPS * row
            right[at, side, :] = strips[end, flat : flat + STEPS]
            weight[at, side, :] = strips[end, flat + STEPS : flat + 2 * STEPS] + weight_middle
        for column in range(SIDE):
            flat = 2 * STEPS * column + STEPS + far
            turned[end * SIDE + column] = strips[end, flat, :LANES]
    spread_flags(ends, mask, turned[...], own_rows, places)


def sides_kernel(ends, odd_ref, even_ref, mask, right, weight, strips, turned):
    own_rows = right.shape[0]
    places = list(enumerate(row_places(ends, own_rows)[0]))
    lay_sides(ends, odd_ref, even_ref, places, own_rows, mask, right, weight, strips, turned)


def smooth_kernel(ends, *refs):
    stencil_ref, *beside = refs[:4]
    sides = refs[4 : 4 + ends]
    own_block = refs[4 + ends : 7 + ends]
    halo_blocks = [refs[7 + ends + 3 * i : 10 + ends + 3 * i] for i in range(ends)]
    solution_ref, coarse_ref, residual, weight, direction, shifted = refs[7 + 4 * ends :][:6]
    far_masks, far_right, far_weight, strips, turned, smoothed, summed = refs[13 + 4 * ends :]
    own_rows, own_cols, pixels = solution_ref.shape
    slots = beside[0].shape[0]
    rows, cols, _ = residual.shape
    place, halos, ahead = row_places(ends, own_rows)
    blocks = halo_blocks[:ahead] + [own_block] + halo_blocks[ahead:]
    bases = [0]
    for block in blocks:
        bases.append(bases[-1] + block[1].shape[0])
    if bases[-1] < rows:
        unused = jnp.zeros((rows - bases[-1], cols, pixels), F32)
        residual[bases[-1] :] = unused
        weight[bases[-1] :] = unused
    own_start = bases[ahead]

    def flags_of(masks, slot, first, last):
        pieces = []
        for base, block, flags in zip(bases, blocks, masks):
            low, high = max(first - base, 0), min(last - base, block[1].shape[0])
            if low < high:
                pieces.append(flags[slot, low:high])
        return pieces[0] if len(pieces) == 1 else jnp.concatenate(pieces, 0)

    for base, block in zip(bases, blocks):
        here = slice(base, base + block[1].shape[0])
        residual[here, :own_cols, :] = block[1][...]
        weight[here, :own_cols, :] = block[2][...]
    here = slice(own_start, own_start + own_rows)
    residual[here, own_cols:, :] = beside[1][...]
    weight[here, own_cols:, :] = beside[2][...]
    halo_bases = bases[:ahead] + bases[ahead + 1 : -1]
    for index, (base, sides_ref, places) in enumerate(zip(halo_bases, sides, halos)):
        lay_sides(
            ends, sides_ref.at[0], sides_ref.at[1], places, own_rows, far_masks.at[index],
            far_right.at[index], far_weight.at[index], strips.at[index], turned,
        )
        count = halo_blocks[index][1].shape[0]
        residual[base : base + count, own_cols:, :] = far_right[index, :count]
        weight[base : base + count, own_cols:, :] = far_weight[index, :count]
    side_masks = [far_masks.at[index] for index in range(ends)]
    side_masks = side_masks[:ahead] + [beside[0]] + side_masks[ahead:]

    def put_direction(slot, start, count, value):
        here = slice(start + 1, start + 1 + count)
        shifted[slot, 1, here] = value.astype(BF16)
        shifted[slot, 0, here] = pltpu.roll(value, 1, 1).astype(BF16)
        shifted[slot, 2, here] = pltpu.roll(value, cols - 1, 1).astype(BF16)

    edge = jnp.zeros((cols, pixels), BF16)
    for slot in range(2):
        for move in range(3):
            shifted[slot, move, 0] = edge
            shifted[slot, move, rows + 1] = edge
    value = residual[...] * (1.0 / center)
    direction[...] = value
    put_direction(0, 0, rows, value)

    own = slice(own_start, own_start + own_rows)
    factors = step_factors()
    for step in range(STEPS):
        now, later = step % 2, 1 - step % 2
        last = step == STEPS - 1
        moved = direction[own, :own_cols, :]
        smoothed[...] = moved if step == 0 else smoothed[...] + moved
        margin = STEPS - 1 - step
        count = own_rows + ends * margin
        start = own_start - (ends - 1) * margin
        width = own_cols if last else cols
        pieces = -(-count // PIECE_ROWS)
        cuts = [start + count * i // pieces for i in range(pieces + 1)]
        for base, size in zip(cuts, (high - low for low, high in zip(cuts, cuts[1:]))):
            here = slice(base, base + size)
            coupled = jnp.zeros((size * width, pixels), F32)
            for slot in range(slots):
                across, along = slot // 3, slot % 3
                source = shifted[now, along, base + across : base + across + size, :width, :]
                if slot != slots // 2:
                    keep = flags_of([block[0] for block in blocks], slot, base, base + size)
                    if not last:
                        keep_sides = flags_of(side_masks, slot, base, base + size)
                        keep = jnp.concatenate([keep, keep_sides], 1)
                    source = jnp.concatenate(
                        [source[:, :, :LANES] * keep, source[:, :, LANES:] * keep], 2
                    )
                coupled += jnp.dot(
                    source.reshape(size * width, pixels),
                    stencil_ref[slot],
                    preferred_element_type=F32,
                )
            coupled = coupled.reshape(size, width, pixels)
            moved = direction[here, :width, :]
            left = residual[here, :width, :] - (weight[here, :width, :] * moved + coupled)
            residual[here, :width, :] = left
            if not last:
                a, b = factors[step]
                value = b * left if a == 0.0 else a * moved + b * left
                direction[here, :width, :] = value
                put_direction(later, base, size, value)

    fine = residual[own, :own_cols, :].reshape(own_rows * own_cols, pixels)
    high = fine.astype(BF16)
    low = (fine - high.astype(F32)).astype(BF16)
    quarter = pixels // 4
    from_pixel = lax.broadcasted_iota(jnp.int32, (pixels, LANES), 0) // 4
    to_pixel = lax.broadcasted_iota(jnp.int32, (pixels, LANES), 1)
    adder = jnp.where(from_pixel == to_pixel, 1.0, 0.0).astype(BF16)
    total = jnp.dot(high, adder, preferred_element_type=F32) + jnp.dot(
        low, adder, preferred_element_type=F32
    )
    summed[...] = total.reshape(own_rows, own_cols, LANES)
    for row in range(own_rows // 2):
        pieces = []
        for across in range(2):
            for along in range(2):
                at = place[2 * row + across]
                piece = summed[at, pl.ds(along, own_cols // 2, stride=2), :]
                pieces.append(piece[:, :quarter])
        coarse_ref[row] = jnp.concatenate(pieces, 1).astype(BF16)
    for row, at in enumerate(place):
        solution_ref[row] = smoothed[at]


def widen_kernel(block_ref, out_hbm, wide, sent):
    rows, ring, _, _ = wide.shape
    half = ring // 2
    own_half = lax.axis_index("fcol") // half
    copies = []
    for row in range(rows):
        for i in range(half):
            wide[row, own_half * half + i] = block_ref[i, 0, row].astype(F32)
            wide[row, (1 - own_half) * half + i] = block_ref[i, 1, row].astype(F32)
        copies.append(pltpu.make_async_copy(wide.at[row], out_hbm.at[row], sent.at[row]))
        copies[-1].start()
    for copy in copies:
        copy.wait()


def body(right_side, noise_weight, stencils, neighbours):
    rows, cols, pixels = right_side.shape
    slots = stencils.shape[0]
    pairs, ring = lax.axis_size("frow"), lax.axis_size("fcol")
    swaps = [
        [(i, j) for low in range(first, ring - 1, 2) for i, j in ((low, low + 1), (low + 1, low))]
        for first in (0, 1)
    ]
    near = jnp.transpose(neighbours, (2, 0, 1))
    right_hbm, weight_hbm, near_hbm, stencil_hbm = [
        pltpu.with_memory_space_constraint(array, pltpu.HBM)
        for array in (right_side, noise_weight, near, stencils)
    ]
    small = pltpu.CompilerParams(vmem_limit_bytes=8 * 1024 * 1024)

    side = pltpu.VMEM((2 * STEPS * rows, pixels), BF16)
    odd, even, held = pl.pallas_call(
        edge_kernel,
        out_shape=(side, side, pltpu.VMEM((cols, LANES), F32)),
        in_specs=[HBM_SPEC] * 3,
        out_specs=(VMEM_SPEC,) * 3,
        scratch_shapes=[
            pltpu.VMEM((2, 2, rows, SIDE, pixels), F32),
            pltpu.VMEM((2, 2 * STEPS * rows, pixels), F32),
            pltpu.VMEM((slots, rows, cols), jnp.int32),
            pltpu.SemaphoreType.DMA((5,)),
        ],
        compiler_params=small,
        name="edges",
    )(right_hbm, weight_hbm, near_hbm)

    odd_side = lax.ppermute(odd, "fcol", swaps[1])
    even_side = lax.ppermute(even, "fcol", swaps[0])
    if pairs == 2:
        moves = [[(0, 1), (1, 0)]]
    else:
        moves = [
            [(i, i + 1) for i in range(pairs - 1)],
            [(i + 1, i) for i in range(pairs - 1)],
        ]
    ends = len(moves)

    def block_types(count):
        return (
            pltpu.VMEM((slots, rows, cols, LANES), BF16),
            pltpu.VMEM((count, cols, pixels), F32),
            pltpu.VMEM((count, cols, pixels), F32),
        )

    *sent, stencil, mask, right, weight = pl.pallas_call(
        functools.partial(own_kernel, ends),
        out_shape=(pltpu.VMEM((STEPS, 2 * cols, pixels), BF16),) * ends
        + (pltpu.VMEM(stencils.shape, stencils.dtype),)
        + block_types(rows),
        in_specs=[HBM_SPEC] * 3 + [VMEM_SPEC],
        out_specs=(VMEM_SPEC,) * (4 + ends),
        scratch_shapes=[pltpu.SemaphoreType.DMA((3 + 2 * rows,))],
        compiler_params=small,
        cost_estimate=pl.CostEstimate(flops=0, bytes_accessed=6000000, transcendentals=0),
        name="own",
    )(stencil_hbm, right_hbm, weight_hbm, held)

    wholes = [lax.ppermute(whole, "frow", move) for whole, move in zip(sent, moves)]
    sides = jnp.stack([odd_side, even_side])
    sides_held = [lax.ppermute(sides, "frow", move) for move in moves]
    halo_blocks = pl.pallas_call(
        functools.partial(rows_kernel, ends),
        out_shape=block_types(STEPS) * ends,
        in_specs=[VMEM_SPEC] * ends,
        out_specs=(VMEM_SPEC,) * (3 * ends),
        compiler_params=small,
        cost_estimate=pl.CostEstimate(flops=0, bytes_accessed=4000000, transcendentals=0),
        name="rows",
    )(*wholes)

    side_types = (
        pltpu.VMEM((slots, rows, 2 * SIDE, LANES), BF16),
        pltpu.VMEM((rows, 2 * SIDE, pixels), F32),
        pltpu.VMEM((rows, 2 * SIDE, pixels), F32),
    )
    beside = pl.pallas_call(
        functools.partial(sides_kernel, ends),
        out_shape=side_types,
        in_specs=[VMEM_SPEC] * 2,
        out_specs=(VMEM_SPEC,) * 3,
        scratch_shapes=[
            pltpu.VMEM((2, 2 * STEPS * rows, pixels), F32),
            pltpu.VMEM((2 * SIDE, LANES), F32),
        ],
        compiler_params=small,
        cost_estimate=pl.CostEstimate(flops=0, bytes_accessed=1000000, transcendentals=0),
        name="sides",
    )(odd_side, even_side)

    cols_held = cols + 2 * SIDE
    rows_held = 2 * rows if ends == 1 else rows + 2 * STEPS
    solution, coarse = pl.pallas_call(
        functools.partial(smooth_kernel, ends),
        out_shape=(
            jax.ShapeDtypeStruct((rows, cols, pixels), F32),
            pltpu.VMEM((rows // 2, cols // 2, pixels), BF16),
        ),
        in_specs=[VMEM_SPEC] * (7 + 4 * ends),
        out_specs=(VMEM_SPEC,) * 2,
        scratch_shapes=[
            pltpu.VMEM((rows_held, cols_held, pixels), F32),
            pltpu.VMEM((rows_held, cols_held, pixels), F32),
            pltpu.VMEM((rows_held, cols_held, pixels), F32),
            pltpu.VMEM((2, 3, rows_held + 2, cols_held, pixels), BF16),
            pltpu.VMEM((ends, slots, rows, 2 * SIDE, LANES), BF16),
            pltpu.VMEM((ends, rows, 2 * SIDE, pixels), F32),
            pltpu.VMEM((ends, rows, 2 * SIDE, pixels), F32),
            pltpu.VMEM((ends, 2, 2 * STEPS * rows, pixels), F32),
            pltpu.VMEM((2 * SIDE, LANES), F32),
            pltpu.VMEM((rows, cols, pixels), F32),
            pltpu.VMEM((rows, cols, LANES), F32),
        ],
        compiler_params=pltpu.CompilerParams(vmem_limit_bytes=24 * 1024 * 1024),
        name="smooth",
    )(stencil, *beside, *sides_held, mask, right, weight, *halo_blocks)

    half = ring // 2
    across = [(i, (i + half) % ring) for i in range(ring)]
    pair = jnp.stack([coarse, lax.ppermute(coarse, "fcol", across)])
    halves = [list(range(half)), list(range(half, ring))]
    spread = jnp.broadcast_to(pair[None], (half,) + pair.shape)
    block = lax.all_to_all(spread, "fcol", 0, 0, axis_index_groups=halves)
    widened = (rows // 2, ring, cols // 2, pixels)
    gathered = pl.pallas_call(
        widen_kernel,
        out_shape=jax.ShapeDtypeStruct(widened, F32),
        in_specs=[VMEM_SPEC],
        out_specs=HBM_SPEC,
        scratch_shapes=[pltpu.VMEM(widened, F32), pltpu.SemaphoreType.DMA((rows // 2,))],
        compiler_params=small,
        name="widen",
    )(block)
    return solution, gathered.reshape(rows // 2, ring * (cols // 2), pixels)


def solution(mesh):
    placed = (P("frow", "fcol", None), P("frow", "fcol", None), P(), P("frow", "fcol", None))
    return jax.shard_map(
        body,
        mesh=mesh,
        in_specs=placed,
        out_specs=(P("frow", "fcol", None), P("frow", None, None)),
        check_vma=False,
    )
```

```python
import functools

import jax
import jax.numpy as jnp
from jax import lax
from jax.experimental import pallas as pl
from jax.experimental.pallas import tpu as pltpu
from jax.sharding import PartitionSpec as P

DEG = 3
SWEEPS = 2
STEPS = DEG * SWEEPS
SIDE = 8
LANES = 128
STRIPS = ((0, STEPS - 1), (SIDE - STEPS, 0))
PIECE_ROWS = 3

lower_edge = 1.5
upper_edge = 6.0
center = 0.5 * (upper_edge + lower_edge)
half_width = 0.5 * (upper_edge - lower_edge)
weight_middle = 3.75

F32 = jnp.float32
BF16 = jnp.bfloat16
HBM_SPEC = pl.BlockSpec(memory_space=pl.ANY)
VMEM_SPEC = pl.BlockSpec(memory_space=pltpu.VMEM)


def step_factors():
    spread_ratio = center / half_width
    factors = []
    for sweep in range(SWEEPS):
        ratio = 1.0 / spread_ratio
        for step in range(DEG):
            if step < DEG - 1:
                ratio_next = 1.0 / (2.0 * spread_ratio - ratio)
                factors.append((ratio_next * ratio, 2.0 * ratio_next / half_width))
                ratio = ratio_next
            else:
                factors.append((0.0, 1.0 / center))
    return factors


def row_places(ends, own_rows):
    if ends == 1:
        flip = lax.axis_index("frow")
        place = [row + flip * (own_rows - 1 - 2 * row) for row in range(own_rows)]
        return place, [list(enumerate(place))], 0
    above = [(own_rows - STEPS + row, row) for row in range(STEPS)]
    below = [(row, row) for row in range(STEPS)]
    return list(range(own_rows)), [above, below], 1


def rows_sent(ends, own_rows):
    if ends == 1:
        return [([own_rows - 1 - row for row in range(STEPS)], STEPS - 1)]
    return [
        ([own_rows - STEPS + row for row in range(STEPS)], 0),
        (list(range(STEPS)), STEPS - 1),
    ]


def slot_places(ends, slots):
    if ends == 1:
        flip = lax.axis_index("frow")
        return [(slot // 3 + flip * (2 - 2 * (slot // 3))) * 3 + slot % 3 for slot in range(slots)]
    return list(range(slots))


def spread_flags(ends, mask, flags, own_rows, places):
    slots, _, cols, _ = mask.shape
    slot_place = slot_places(ends, slots)
    for slot in range(slots):
        if slot == slots // 2:
            continue
        for row, at in places:
            lane = slot * own_rows + row
            column = jnp.broadcast_to(flags[:, lane : lane + 1], (cols, LANES))
            mask[slot_place[slot], at] = column.astype(BF16)


def edge_kernel(right_hbm, weight_hbm, near_hbm, *refs):
    odd_ref, even_ref, held_ref, strips, flat, near_ref, arrived = refs
    slots, rows, cols = near_ref.shape
    copies = [pltpu.make_async_copy(near_hbm, near_ref, arrived.at[4])]
    for end, start in enumerate((0, cols - SIDE)):
        for kind, source in enumerate((right_hbm, weight_hbm)):
            copies.append(
                pltpu.make_async_copy(
                    source.at[:, pl.ds(start, SIDE)],
                    strips.at[end, kind],
                    arrived.at[2 * end + kind],
                )
            )
    for copy in copies:
        copy.start()
    copies[0].wait()
    flags = jnp.where(near_ref[...] >= 0, 1.0, 0.0).astype(F32).reshape(slots * rows, cols)
    flags = jnp.concatenate([flags, jnp.zeros((slots * rows, LANES - cols), F32)], 1)
    flags = jnp.concatenate([flags, jnp.zeros((LANES - slots * rows, LANES), F32)], 0)
    turned = jnp.transpose(flags)[:cols]
    held_ref[...] = turned
    for copy in copies[1:]:
        copy.wait()
    for end, (low, far) in enumerate(STRIPS):
        for row in range(rows):
            base = 2 * STEPS * row
            flat[end, base : base + STEPS] = strips[end, 0, row, low : low + STEPS]
            weight = strips[end, 1, row, low : low + STEPS] - weight_middle
            flat[end, base + STEPS : base + 2 * STEPS] = weight
            column = row + end * (cols - SIDE)
            flat[end, base + STEPS + far, :LANES] = turned[column]
    parity = lax.rem(lax.axis_index("fcol"), 2)
    odd_ref[...] = flat[parity].astype(BF16)
    even_ref[...] = flat[1 - parity].astype(BF16)


def own_kernel(ends, stencil_hbm, right_hbm, weight_hbm, held_ref, *refs):
    whole_refs = refs[:ends]
    stencil_ref, mask, residual, weight, arrived = refs[ends:]
    slots = mask.shape[0]
    own_rows, own_cols, _ = residual.shape
    place, _, _ = row_places(ends, own_rows)
    slot_place = slot_places(ends, slots)
    copies = []
    for row in range(own_rows):
        for source, target in ((right_hbm, residual), (weight_hbm, weight)):
            copies.append(
                pltpu.make_async_copy(
                    source.at[row], target.at[place[row]], arrived.at[3 + len(copies)]
                )
            )
    stencil_copies = [
        pltpu.make_async_copy(
            stencil_hbm.at[pl.ds(slot, 3)],
            stencil_ref.at[pl.ds(slot_place[slot], 3)],
            arrived.at[slot // 3],
        )
        for slot in range(0, slots, 3)
    ]
    for copy in copies + stencil_copies:
        copy.start()
    flags = held_ref[...]
    spread_flags(ends, mask, flags, own_rows, list(enumerate(place)))
    for copy in copies:
        copy.wait()
    for whole_ref, (sent, far) in zip(whole_refs, rows_sent(ends, own_rows)):
        for row, at in enumerate(sent):
            whole_ref[row, :own_cols] = residual[at].astype(BF16)
            if row == far:
                whole_ref[row, own_cols:, :LANES] = flags.astype(BF16)
                whole_ref[row, own_cols:, LANES:] = flags.astype(BF16)
            else:
                whole_ref[row, own_cols:] = (weight[at] - weight_middle).astype(BF16)
    for copy in stencil_copies:
        copy.wait()


def rows_kernel(ends, *refs):
    for index in range(ends):
        whole_ref = refs[index]
        mask, residual, weight = refs[ends + 3 * index : ends + 3 * index + 3]
        own_rows, own_cols = mask.shape[1], residual.shape[1]
        for row in range(STEPS):
            strip = whole_ref[row].astype(F32)
            residual[row] = strip[:own_cols]
            weight[row] = strip[own_cols:] + weight_middle
        far = rows_sent(ends, own_rows)[index][1]
        flags = whole_ref[far, own_cols:, :LANES].astype(F32)
        places = row_places(ends, own_rows)[1][index]
        spread_flags(ends, mask, flags, own_rows, places)


def lay_sides(ends, odd_ref, even_ref, places, own_rows, mask, right, weight, strips, turned):
    first_of_even = lax.rem(lax.axis_index("fcol"), 2) == 0
    strips[0] = jnp.where(first_of_even, even_ref[...], odd_ref[...]).astype(F32)
    strips[1] = jnp.where(first_of_even, odd_ref[...], even_ref[...]).astype(F32)
    right[...] = jnp.zeros(right.shape, F32)
    weight[...] = jnp.zeros(weight.shape, F32)
    for end, (low, far) in enumerate(STRIPS):
        side = slice(end * SIDE + low, end * SIDE + low + STEPS)
        for row, at in places:
            flat = 2 * STEPS * row
            right[at, side, :] = strips[end, flat : flat + STEPS]
            weight[at, side, :] = strips[end, flat + STEPS : flat + 2 * STEPS] + weight_middle
        for column in range(SIDE):
            flat = 2 * STEPS * column + STEPS + far
            turned[end * SIDE + column] = strips[end, flat, :LANES]
    spread_flags(ends, mask, turned[...], own_rows, places)


def sides_kernel(ends, odd_ref, even_ref, mask, right, weight, strips, turned):
    own_rows = right.shape[0]
    places = list(enumerate(row_places(ends, own_rows)[0]))
    lay_sides(ends, odd_ref, even_ref, places, own_rows, mask, right, weight, strips, turned)


def smooth_kernel(ends, *refs):
    stencil_ref, *beside = refs[:4]
    sides = refs[4 : 4 + ends]
    own_block = refs[4 + ends : 7 + ends]
    halo_blocks = [refs[7 + ends + 3 * i : 10 + ends + 3 * i] for i in range(ends)]
    solution_ref, coarse_ref, residual, weight, direction, shifted = refs[7 + 4 * ends :][:6]
    far_masks, far_right, far_weight, strips, turned, smoothed, summed = refs[13 + 4 * ends :]
    own_rows, own_cols, pixels = solution_ref.shape
    slots = beside[0].shape[0]
    rows, cols, _ = residual.shape
    place, halos, ahead = row_places(ends, own_rows)
    blocks = halo_blocks[:ahead] + [own_block] + halo_blocks[ahead:]
    bases = [0]
    for block in blocks:
        bases.append(bases[-1] + block[1].shape[0])
    if bases[-1] < rows:
        unused = jnp.zeros((rows - bases[-1], cols, pixels), F32)
        residual[bases[-1] :] = unused
        weight[bases[-1] :] = unused
    own_start = bases[ahead]

    def flags_of(masks, slot, first, last):
        pieces = []
        for base, block, flags in zip(bases, blocks, masks):
            low, high = max(first - base, 0), min(last - base, block[1].shape[0])
            if low < high:
                pieces.append(flags[slot, low:high])
        return pieces[0] if len(pieces) == 1 else jnp.concatenate(pieces, 0)

    for base, block in zip(bases, blocks):
        here = slice(base, base + block[1].shape[0])
        residual[here, :own_cols, :] = block[1][...]
        weight[here, :own_cols, :] = block[2][...]
    here = slice(own_start, own_start + own_rows)
    residual[here, own_cols:, :] = beside[1][...]
    weight[here, own_cols:, :] = beside[2][...]
    halo_bases = bases[:ahead] + bases[ahead + 1 : -1]
    for index, (base, sides_ref, places) in enumerate(zip(halo_bases, sides, halos)):
        lay_sides(
            ends, sides_ref.at[0], sides_ref.at[1], places, own_rows, far_masks.at[index],
            far_right.at[index], far_weight.at[index], strips.at[index], turned,
        )
        count = halo_blocks[index][1].shape[0]
        residual[base : base + count, own_cols:, :] = far_right[index, :count]
        weight[base : base + count, own_cols:, :] = far_weight[index, :count]
    side_masks = [far_masks.at[index] for index in range(ends)]
    side_masks = side_masks[:ahead] + [beside[0]] + side_masks[ahead:]

    def put_direction(slot, start, count, value):
        here = slice(start + 1, start + 1 + count)
        shifted[slot, 1, here] = value.astype(BF16)
        shifted[slot, 0, here] = pltpu.roll(value, 1, 1).astype(BF16)
        shifted[slot, 2, here] = pltpu.roll(value, cols - 1, 1).astype(BF16)

    edge = jnp.zeros((cols, pixels), BF16)
    for slot in range(2):
        for move in range(3):
            shifted[slot, move, 0] = edge
            shifted[slot, move, rows + 1] = edge
    value = residual[...] * (1.0 / center)
    direction[...] = value
    put_direction(0, 0, rows, value)

    own = slice(own_start, own_start + own_rows)
    factors = step_factors()
    for step in range(STEPS):
        now, later = step % 2, 1 - step % 2
        last = step == STEPS - 1
        moved = direction[own, :own_cols, :]
        smoothed[...] = moved if step == 0 else smoothed[...] + moved
        margin = STEPS - 1 - step
        count = own_rows + ends * margin
        start = own_start - (ends - 1) * margin
        width = own_cols if last else cols
        pieces = -(-count // PIECE_ROWS)
        cuts = [start + count * i // pieces for i in range(pieces + 1)]
        for base, size in zip(cuts, (high - low for low, high in zip(cuts, cuts[1:]))):
            here = slice(base, base + size)
            coupled = jnp.zeros((size * width, pixels), F32)
            for slot in range(slots):
                across, along = slot // 3, slot % 3
                source = shifted[now, along, base + across : base + across + size, :width, :]
                if slot != slots // 2:
                    keep = flags_of([block[0] for block in blocks], slot, base, base + size)
                    if not last:
                        keep_sides = flags_of(side_masks, slot, base, base + size)
                        keep = jnp.concatenate([keep, keep_sides], 1)
                    source = jnp.concatenate(
                        [source[:, :, :LANES] * keep, source[:, :, LANES:] * keep], 2
                    )
                coupled += jnp.dot(
                    source.reshape(size * width, pixels),
                    stencil_ref[slot],
                    preferred_element_type=F32,
                )
            coupled = coupled.reshape(size, width, pixels)
            moved = direction[here, :width, :]
            left = residual[here, :width, :] - (weight[here, :width, :] * moved + coupled)
            residual[here, :width, :] = left
            if not last:
                a, b = factors[step]
                value = b * left if a == 0.0 else a * moved + b * left
                direction[here, :width, :] = value
                put_direction(later, base, size, value)

    fine = residual[own, :own_cols, :].reshape(own_rows * own_cols, pixels)
    high = fine.astype(BF16)
    low = (fine - high.astype(F32)).astype(BF16)
    quarter = pixels // 4
    from_pixel = lax.broadcasted_iota(jnp.int32, (pixels, LANES), 0) // 4
    to_pixel = lax.broadcasted_iota(jnp.int32, (pixels, LANES), 1)
    adder = jnp.where(from_pixel == to_pixel, 1.0, 0.0).astype(BF16)
    total = jnp.dot(high, adder, preferred_element_type=F32) + jnp.dot(
        low, adder, preferred_element_type=F32
    )
    summed[...] = total.reshape(own_rows, own_cols, LANES)
    for row in range(own_rows // 2):
        pieces = []
        for across in range(2):
            for along in range(2):
                at = place[2 * row + across]
                piece = summed[at, pl.ds(along, own_cols // 2, stride=2), :]
                pieces.append(piece[:, :quarter])
        coarse_ref[row] = jnp.concatenate(pieces, 1).astype(BF16)
    for row, at in enumerate(place):
        solution_ref[row] = smoothed[at]


def widen_kernel(block_ref, out_hbm, wide, sent):
    rows, ring, _, _ = wide.shape
    half = ring // 2
    own_half = lax.axis_index("fcol") // half
    copies = []
    for row in range(rows):
        for i in range(half):
            wide[row, own_half * half + i] = block_ref[i, 0, row].astype(F32)
            wide[row, (1 - own_half) * half + i] = block_ref[i, 1, row].astype(F32)
        copies.append(pltpu.make_async_copy(wide.at[row], out_hbm.at[row], sent.at[row]))
        copies[-1].start()
    for copy in copies:
        copy.wait()


def body(right_side, noise_weight, stencils, neighbours):
    rows, cols, pixels = right_side.shape
    slots = stencils.shape[0]
    pairs, ring = lax.axis_size("frow"), lax.axis_size("fcol")
    swaps = [
        [(i, j) for low in range(first, ring - 1, 2) for i, j in ((low, low + 1), (low + 1, low))]
        for first in (0, 1)
    ]
    near = jnp.transpose(neighbours, (2, 0, 1))
    right_hbm, weight_hbm, near_hbm, stencil_hbm = [
        pltpu.with_memory_space_constraint(array, pltpu.HBM)
        for array in (right_side, noise_weight, near, stencils)
    ]
    small = pltpu.CompilerParams(vmem_limit_bytes=8 * 1024 * 1024)

    side = pltpu.VMEM((2 * STEPS * rows, pixels), BF16)
    odd, even, held = pl.pallas_call(
        edge_kernel,
        out_shape=(side, side, pltpu.VMEM((cols, LANES), F32)),
        in_specs=[HBM_SPEC] * 3,
        out_specs=(VMEM_SPEC,) * 3,
        scratch_shapes=[
            pltpu.VMEM((2, 2, rows, SIDE, pixels), F32),
            pltpu.VMEM((2, 2 * STEPS * rows, pixels), F32),
            pltpu.VMEM((slots, rows, cols), jnp.int32),
            pltpu.SemaphoreType.DMA((5,)),
        ],
        compiler_params=small,
        name="edges",
    )(right_hbm, weight_hbm, near_hbm)

    odd_side = lax.ppermute(odd, "fcol", swaps[1])
    even_side = lax.ppermute(even, "fcol", swaps[0])
    if pairs == 2:
        moves = [[(0, 1), (1, 0)]]
    else:
        moves = [
            [(i, i + 1) for i in range(pairs - 1)],
            [(i + 1, i) for i in range(pairs - 1)],
        ]
    ends = len(moves)

    def block_types(count):
        return (
            pltpu.VMEM((slots, rows, cols, LANES), BF16),
            pltpu.VMEM((count, cols, pixels), F32),
            pltpu.VMEM((count, cols, pixels), F32),
        )

    *sent, stencil, mask, right, weight = pl.pallas_call(
        functools.partial(own_kernel, ends),
        out_shape=(pltpu.VMEM((STEPS, 2 * cols, pixels), BF16),) * ends
        + (pltpu.VMEM(stencils.shape, stencils.dtype),)
        + block_types(rows),
        in_specs=[HBM_SPEC] * 3 + [VMEM_SPEC],
        out_specs=(VMEM_SPEC,) * (4 + ends),
        scratch_shapes=[pltpu.SemaphoreType.DMA((3 + 2 * rows,))],
        compiler_params=small,
        cost_estimate=pl.CostEstimate(flops=0, bytes_accessed=6000000, transcendentals=0),
        name="own",
    )(stencil_hbm, right_hbm, weight_hbm, held)

    wholes = [lax.ppermute(whole, "frow", move) for whole, move in zip(sent, moves)]
    sides = jnp.stack([odd_side, even_side])
    sides_held = [lax.ppermute(sides, "frow", move) for move in moves]
    halo_blocks = pl.pallas_call(
        functools.partial(rows_kernel, ends),
        out_shape=block_types(STEPS) * ends,
        in_specs=[VMEM_SPEC] * ends,
        out_specs=(VMEM_SPEC,) * (3 * ends),
        compiler_params=small,
        cost_estimate=pl.CostEstimate(flops=0, bytes_accessed=4000000, transcendentals=0),
        name="rows",
    )(*wholes)

    side_types = (
        pltpu.VMEM((slots, rows, 2 * SIDE, LANES), BF16),
        pltpu.VMEM((rows, 2 * SIDE, pixels), F32),
        pltpu.VMEM((rows, 2 * SIDE, pixels), F32),
    )
    beside = pl.pallas_call(
        functools.partial(sides_kernel, ends),
        out_shape=side_types,
        in_specs=[VMEM_SPEC] * 2,
        out_specs=(VMEM_SPEC,) * 3,
        scratch_shapes=[
            pltpu.VMEM((2, 2 * STEPS * rows, pixels), F32),
            pltpu.VMEM((2 * SIDE, LANES), F32),
        ],
        compiler_params=small,
        cost_estimate=pl.CostEstimate(flops=0, bytes_accessed=1000000, transcendentals=0),
        name="sides",
    )(odd_side, even_side)

    cols_held = cols + 2 * SIDE
    rows_held = 2 * rows if ends == 1 else rows + 2 * STEPS
    solution, coarse = pl.pallas_call(
        functools.partial(smooth_kernel, ends),
        out_shape=(
            jax.ShapeDtypeStruct((rows, cols, pixels), F32),
            pltpu.VMEM((rows // 2, cols // 2, pixels), BF16),
        ),
        in_specs=[VMEM_SPEC] * (7 + 4 * ends),
        out_specs=(VMEM_SPEC,) * 2,
        scratch_shapes=[
            pltpu.VMEM((rows_held, cols_held, pixels), F32),
            pltpu.VMEM((rows_held, cols_held, pixels), F32),
            pltpu.VMEM((rows_held, cols_held, pixels), F32),
            pltpu.VMEM((2, 3, rows_held + 2, cols_held, pixels), BF16),
            pltpu.VMEM((ends, slots, rows, 2 * SIDE, LANES), BF16),
            pltpu.VMEM((ends, rows, 2 * SIDE, pixels), F32),
            pltpu.VMEM((ends, rows, 2 * SIDE, pixels), F32),
            pltpu.VMEM((ends, 2, 2 * STEPS * rows, pixels), F32),
            pltpu.VMEM((2 * SIDE, LANES), F32),
            pltpu.VMEM((rows, cols, pixels), F32),
            pltpu.VMEM((rows, cols, LANES), F32),
        ],
        compiler_params=pltpu.CompilerParams(vmem_limit_bytes=24 * 1024 * 1024),
        name="smooth",
    )(stencil, *beside, *sides_held, mask, right, weight, *halo_blocks)

    half = ring // 2
    across = [(i, (i + half) % ring) for i in range(ring)]
    pair = jnp.stack([coarse, lax.ppermute(coarse, "fcol", across)])
    halves = [list(range(half)), list(range(half, ring))]
    spread = jnp.broadcast_to(pair[None], (half,) + pair.shape)
    block = lax.all_to_all(spread, "fcol", 0, 0, axis_index_groups=halves)
    widened = (rows // 2, ring, cols // 2, pixels)
    gathered = pl.pallas_call(
        widen_kernel,
        out_shape=jax.ShapeDtypeStruct(widened, F32),
        in_specs=[VMEM_SPEC],
        out_specs=HBM_SPEC,
        scratch_shapes=[pltpu.VMEM(widened, F32), pltpu.SemaphoreType.DMA((rows // 2,))],
        compiler_params=small,
        name="widen",
    )(block)
    return solution, gathered.reshape(rows // 2, ring * (cols // 2), pixels)


def solution(mesh):
    placed = (P("frow", "fcol", None), P("frow", "fcol", None), P(), P("frow", "fcol", None))
    return jax.shard_map(
        body,
        mesh=mesh,
        in_specs=placed,
        out_specs=(P("frow", "fcol", None), P("frow", None, None)),
        check_vma=False,
    )
```

```python
import functools

import jax
import jax.numpy as jnp
from jax import lax
from jax.experimental import pallas as pl
from jax.experimental.pallas import tpu as pltpu
from jax.sharding import PartitionSpec as P

DEG = 3
SWEEPS = 2
STEPS = DEG * SWEEPS
SIDE = 8
LANES = 128
STRIPS = ((0, STEPS - 1), (SIDE - STEPS, 0))
PIECE_ROWS = 4

lower_edge = 1.5
upper_edge = 6.0
center = 0.5 * (upper_edge + lower_edge)
half_width = 0.5 * (upper_edge - lower_edge)
weight_middle = 3.75

F32 = jnp.float32
BF16 = jnp.bfloat16
HBM_SPEC = pl.BlockSpec(memory_space=pl.ANY)
VMEM_SPEC = pl.BlockSpec(memory_space=pltpu.VMEM)


def step_factors():
    spread_ratio = center / half_width
    factors = []
    for sweep in range(SWEEPS):
        ratio = 1.0 / spread_ratio
        for step in range(DEG):
            if step < DEG - 1:
                ratio_next = 1.0 / (2.0 * spread_ratio - ratio)
                factors.append((ratio_next * ratio, 2.0 * ratio_next / half_width))
                ratio = ratio_next
            else:
                factors.append((0.0, 1.0 / center))
    return factors


def row_places(ends, own_rows):
    if ends == 1:
        flip = lax.axis_index("frow")
        place = [row + flip * (own_rows - 1 - 2 * row) for row in range(own_rows)]
        return place, [list(enumerate(place))], 0
    above = [(own_rows - STEPS + row, row) for row in range(STEPS)]
    below = [(row, row) for row in range(STEPS)]
    return list(range(own_rows)), [above, below], 1


def rows_sent(ends, own_rows):
    if ends == 1:
        return [([own_rows - 1 - row for row in range(STEPS)], STEPS - 1)]
    return [
        ([own_rows - STEPS + row for row in range(STEPS)], 0),
        (list(range(STEPS)), STEPS - 1),
    ]


def slot_places(ends, slots):
    if ends == 1:
        flip = lax.axis_index("frow")
        return [(slot // 3 + flip * (2 - 2 * (slot // 3))) * 3 + slot % 3 for slot in range(slots)]
    return list(range(slots))


def spread_flags(ends, mask, flags, own_rows, places):
    slots, _, cols, _ = mask.shape
    slot_place = slot_places(ends, slots)
    for slot in range(slots):
        if slot == slots // 2:
            continue
        for row, at in places:
            lane = slot * own_rows + row
            column = jnp.broadcast_to(flags[:, lane : lane + 1], (cols, LANES))
            mask[slot_place[slot], at] = column.astype(BF16)


def edge_kernel(right_hbm, weight_hbm, near_hbm, *refs):
    odd_ref, even_ref, held_ref, strips, flat, near_ref, arrived = refs
    slots, rows, cols = near_ref.shape
    copies = [pltpu.make_async_copy(near_hbm, near_ref, arrived.at[4])]
    for end, start in enumerate((0, cols - SIDE)):
        for kind, source in enumerate((right_hbm, weight_hbm)):
            copies.append(
                pltpu.make_async_copy(
                    source.at[:, pl.ds(start, SIDE)],
                    strips.at[end, kind],
                    arrived.at[2 * end + kind],
                )
            )
    for copy in copies:
        copy.start()
    copies[0].wait()
    flags = jnp.where(near_ref[...] >= 0, 1.0, 0.0).astype(F32).reshape(slots * rows, cols)
    flags = jnp.concatenate([flags, jnp.zeros((slots * rows, LANES - cols), F32)], 1)
    flags = jnp.concatenate([flags, jnp.zeros((LANES - slots * rows, LANES), F32)], 0)
    turned = jnp.transpose(flags)[:cols]
    held_ref[...] = turned
    for copy in copies[1:]:
        copy.wait()
    for end, (low, far) in enumerate(STRIPS):
        for row in range(rows):
            base = 2 * STEPS * row
            flat[end, base : base + STEPS] = strips[end, 0, row, low : low + STEPS]
            weight = strips[end, 1, row, low : low + STEPS] - weight_middle
            flat[end, base + STEPS : base + 2 * STEPS] = weight
            column = row + end * (cols - SIDE)
            flat[end, base + STEPS + far, :LANES] = turned[column]
    parity = lax.rem(lax.axis_index("fcol"), 2)
    odd_ref[...] = flat[parity].astype(BF16)
    even_ref[...] = flat[1 - parity].astype(BF16)


def own_kernel(ends, stencil_hbm, right_hbm, weight_hbm, held_ref, *refs):
    whole_refs = refs[:ends]
    stencil_ref, mask, residual, weight, arrived = refs[ends:]
    slots = mask.shape[0]
    own_rows, own_cols, _ = residual.shape
    place, _, _ = row_places(ends, own_rows)
    slot_place = slot_places(ends, slots)
    copies = []
    for row in range(own_rows):
        for source, target in ((right_hbm, residual), (weight_hbm, weight)):
            copies.append(
                pltpu.make_async_copy(
                    source.at[row], target.at[place[row]], arrived.at[3 + len(copies)]
                )
            )
    stencil_copies = [
        pltpu.make_async_copy(
            stencil_hbm.at[pl.ds(slot, 3)],
            stencil_ref.at[pl.ds(slot_place[slot], 3)],
            arrived.at[slot // 3],
        )
        for slot in range(0, slots, 3)
    ]
    for copy in copies + stencil_copies:
        copy.start()
    flags = held_ref[...]
    spread_flags(ends, mask, flags, own_rows, list(enumerate(place)))
    for copy in copies:
        copy.wait()
    for whole_ref, (sent, far) in zip(whole_refs, rows_sent(ends, own_rows)):
        for row, at in enumerate(sent):
            whole_ref[row, :own_cols] = residual[at].astype(BF16)
            if row == far:
                whole_ref[row, own_cols:, :LANES] = flags.astype(BF16)
                whole_ref[row, own_cols:, LANES:] = flags.astype(BF16)
            else:
                whole_ref[row, own_cols:] = (weight[at] - weight_middle).astype(BF16)
    for copy in stencil_copies:
        copy.wait()


def rows_kernel(ends, *refs):
    for index in range(ends):
        whole_ref = refs[index]
        mask, residual, weight = refs[ends + 3 * index : ends + 3 * index + 3]
        own_rows, own_cols = mask.shape[1], residual.shape[1]
        for row in range(STEPS):
            strip = whole_ref[row].astype(F32)
            residual[row] = strip[:own_cols]
            weight[row] = strip[own_cols:] + weight_middle
        far = rows_sent(ends, own_rows)[index][1]
        flags = whole_ref[far, own_cols:, :LANES].astype(F32)
        places = row_places(ends, own_rows)[1][index]
        spread_flags(ends, mask, flags, own_rows, places)


def lay_sides(ends, odd_ref, even_ref, places, own_rows, mask, right, weight, strips, turned):
    first_of_even = lax.rem(lax.axis_index("fcol"), 2) == 0
    strips[0] = jnp.where(first_of_even, even_ref[...], odd_ref[...]).astype(F32)
    strips[1] = jnp.where(first_of_even, odd_ref[...], even_ref[...]).astype(F32)
    right[...] = jnp.zeros(right.shape, F32)
    weight[...] = jnp.zeros(weight.shape, F32)
    for end, (low, far) in enumerate(STRIPS):
        side = slice(end * SIDE + low, end * SIDE + low + STEPS)
        for row, at in places:
            flat = 2 * STEPS * row
            right[at, side, :] = strips[end, flat : flat + STEPS]
            weight[at, side, :] = strips[end, flat + STEPS : flat + 2 * STEPS] + weight_middle
        for column in range(SIDE):
            flat = 2 * STEPS * column + STEPS + far
            turned[end * SIDE + column] = strips[end, flat, :LANES]
    spread_flags(ends, mask, turned[...], own_rows, places)


def sides_kernel(ends, odd_ref, even_ref, mask, right, weight, strips, turned):
    own_rows = right.shape[0]
    places = list(enumerate(row_places(ends, own_rows)[0]))
    lay_sides(ends, odd_ref, even_ref, places, own_rows, mask, right, weight, strips, turned)


def smooth_kernel(ends, *refs):
    stencil_ref, *beside = refs[:4]
    sides = refs[4 : 4 + ends]
    own_block = refs[4 + ends : 7 + ends]
    halo_blocks = [refs[7 + ends + 3 * i : 10 + ends + 3 * i] for i in range(ends)]
    solution_ref, coarse_ref, residual, weight, direction, shifted = refs[7 + 4 * ends :][:6]
    far_masks, far_right, far_weight, strips, turned, smoothed, summed, sent = refs[13 + 4 * ends :]
    own_rows, own_cols, pixels = solution_ref.shape
    slots = beside[0].shape[0]
    rows, cols, _ = residual.shape
    place, halos, ahead = row_places(ends, own_rows)
    blocks = halo_blocks[:ahead] + [own_block] + halo_blocks[ahead:]
    bases = [0]
    for block in blocks:
        bases.append(bases[-1] + block[1].shape[0])
    if bases[-1] < rows:
        unused = jnp.zeros((rows - bases[-1], cols, pixels), F32)
        residual[bases[-1] :] = unused
        weight[bases[-1] :] = unused
    own_start = bases[ahead]

    def flags_of(masks, slot, first, last):
        pieces = []
        for base, block, flags in zip(bases, blocks, masks):
            low, high = max(first - base, 0), min(last - base, block[1].shape[0])
            if low < high:
                pieces.append(flags[slot, low:high])
        return pieces[0] if len(pieces) == 1 else jnp.concatenate(pieces, 0)

    for base, block in zip(bases, blocks):
        here = slice(base, base + block[1].shape[0])
        residual[here, :own_cols, :] = block[1][...]
        weight[here, :own_cols, :] = block[2][...]
    here = slice(own_start, own_start + own_rows)
    residual[here, own_cols:, :] = beside[1][...]
    weight[here, own_cols:, :] = beside[2][...]
    halo_bases = bases[:ahead] + bases[ahead + 1 : -1]
    for index, (base, sides_ref, places) in enumerate(zip(halo_bases, sides, halos)):
        lay_sides(
            ends, sides_ref.at[0], sides_ref.at[1], places, own_rows, far_masks.at[index],
            far_right.at[index], far_weight.at[index], strips.at[index], turned,
        )
        count = halo_blocks[index][1].shape[0]
        residual[base : base + count, own_cols:, :] = far_right[index, :count]
        weight[base : base + count, own_cols:, :] = far_weight[index, :count]
    side_masks = [far_masks.at[index] for index in range(ends)]
    side_masks = side_masks[:ahead] + [beside[0]] + side_masks[ahead:]

    def put_direction(slot, start, count, value):
        here = slice(start + 1, start + 1 + count)
        shifted[slot, 1, here] = value.astype(BF16)
        shifted[slot, 0, here] = pltpu.roll(value, 1, 1).astype(BF16)
        shifted[slot, 2, here] = pltpu.roll(value, cols - 1, 1).astype(BF16)

    edge = jnp.zeros((cols, pixels), BF16)
    for slot in range(2):
        for move in range(3):
            shifted[slot, move, 0] = edge
            shifted[slot, move, rows + 1] = edge
    value = residual[...] * (1.0 / center)
    direction[...] = value
    put_direction(0, 0, rows, value)

    own = slice(own_start, own_start + own_rows)
    solution_copies = [
        pltpu.make_async_copy(smoothed.at[at], solution_ref.at[row], sent.at[row])
        for row, at in enumerate(place)
    ]
    factors = step_factors()
    for step in range(STEPS):
        now, later = step % 2, 1 - step % 2
        last = step == STEPS - 1
        moved = direction[own, :own_cols, :]
        smoothed[...] = moved if step == 0 else smoothed[...] + moved
        if last:
            for copy in solution_copies:
                copy.start()
        margin = STEPS - 1 - step
        count = own_rows + ends * margin
        start = own_start - (ends - 1) * margin
        width = own_cols if last else cols
        pieces = -(-count // PIECE_ROWS)
        cuts = [start + count * i // pieces for i in range(pieces + 1)]
        for base, size in zip(cuts, (high - low for low, high in zip(cuts, cuts[1:]))):
            here = slice(base, base + size)
            coupled = jnp.zeros((size * width, pixels), F32)
            for slot in range(slots):
                across, along = slot // 3, slot % 3
                source = shifted[now, along, base + across : base + across + size, :width, :]
                if slot != slots // 2:
                    keep = flags_of([block[0] for block in blocks], slot, base, base + size)
                    if not last:
                        keep_sides = flags_of(side_masks, slot, base, base + size)
                        keep = jnp.concatenate([keep, keep_sides], 1)
                    source = jnp.concatenate(
                        [source[:, :, :LANES] * keep, source[:, :, LANES:] * keep], 2
                    )
                coupled += jnp.dot(
                    source.reshape(size * width, pixels),
                    stencil_ref[slot],
                    preferred_element_type=F32,
                )
            coupled = coupled.reshape(size, width, pixels)
            moved = direction[here, :width, :]
            left = residual[here, :width, :] - (weight[here, :width, :] * moved + coupled)
            residual[here, :width, :] = left
            if not last:
                a, b = factors[step]
                value = b * left if a == 0.0 else a * moved + b * left
                direction[here, :width, :] = value
                put_direction(later, base, size, value)

    fine = residual[own, :own_cols, :].reshape(own_rows * own_cols, pixels)
    high = fine.astype(BF16)
    low = (fine - high.astype(F32)).astype(BF16)
    quarter = pixels // 4
    from_pixel = lax.broadcasted_iota(jnp.int32, (pixels, LANES), 0) // 4
    to_pixel = lax.broadcasted_iota(jnp.int32, (pixels, LANES), 1)
    adder = jnp.where(from_pixel == to_pixel, 1.0, 0.0).astype(BF16)
    total = jnp.dot(high, adder, preferred_element_type=F32) + jnp.dot(
        low, adder, preferred_element_type=F32
    )
    summed[...] = total.reshape(own_rows, own_cols, LANES)
    for row in range(own_rows // 2):
        pieces = []
        for across in range(2):
            for along in range(2):
                at = place[2 * row + across]
                piece = summed[at, pl.ds(along, own_cols // 2, stride=2), :]
                pieces.append(piece[:, :quarter])
        coarse_ref[row] = jnp.concatenate(pieces, 1).astype(BF16)
    for copy in solution_copies:
        copy.wait()


def widen_kernel(block_ref, out_hbm, wide, sent):
    rows, ring, _, _ = wide.shape
    half = ring // 2
    own_half = lax.axis_index("fcol") // half
    copies = []
    for row in range(rows):
        for i in range(half):
            wide[row, own_half * half + i] = block_ref[i, 0, row].astype(F32)
            wide[row, (1 - own_half) * half + i] = block_ref[i, 1, row].astype(F32)
        copies.append(pltpu.make_async_copy(wide.at[row], out_hbm.at[row], sent.at[row]))
        copies[-1].start()
    for copy in copies:
        copy.wait()


def body(right_side, noise_weight, stencils, neighbours):
    rows, cols, pixels = right_side.shape
    slots = stencils.shape[0]
    pairs, ring = lax.axis_size("frow"), lax.axis_size("fcol")
    swaps = [
        [(i, j) for low in range(first, ring - 1, 2) for i, j in ((low, low + 1), (low + 1, low))]
        for first in (0, 1)
    ]
    near = jnp.transpose(neighbours, (2, 0, 1))
    right_hbm, weight_hbm, near_hbm, stencil_hbm = [
        pltpu.with_memory_space_constraint(array, pltpu.HBM)
        for array in (right_side, noise_weight, near, stencils)
    ]
    small = pltpu.CompilerParams(vmem_limit_bytes=8 * 1024 * 1024)

    side = pltpu.VMEM((2 * STEPS * rows, pixels), BF16)
    odd, even, held = pl.pallas_call(
        edge_kernel,
        out_shape=(side, side, pltpu.VMEM((cols, LANES), F32)),
        in_specs=[HBM_SPEC] * 3,
        out_specs=(VMEM_SPEC,) * 3,
        scratch_shapes=[
            pltpu.VMEM((2, 2, rows, SIDE, pixels), F32),
            pltpu.VMEM((2, 2 * STEPS * rows, pixels), F32),
            pltpu.VMEM((slots, rows, cols), jnp.int32),
            pltpu.SemaphoreType.DMA((5,)),
        ],
        compiler_params=small,
        name="edges",
    )(right_hbm, weight_hbm, near_hbm)

    odd_side = lax.ppermute(odd, "fcol", swaps[1])
    even_side = lax.ppermute(even, "fcol", swaps[0])
    if pairs == 2:
        moves = [[(0, 1), (1, 0)]]
    else:
        moves = [
            [(i, i + 1) for i in range(pairs - 1)],
            [(i + 1, i) for i in range(pairs - 1)],
        ]
    ends = len(moves)

    def block_types(count):
        return (
            pltpu.VMEM((slots, rows, cols, LANES), BF16),
            pltpu.VMEM((count, cols, pixels), F32),
            pltpu.VMEM((count, cols, pixels), F32),
        )

    *sent, stencil, mask, right, weight = pl.pallas_call(
        functools.partial(own_kernel, ends),
        out_shape=(pltpu.VMEM((STEPS, 2 * cols, pixels), BF16),) * ends
        + (pltpu.VMEM(stencils.shape, stencils.dtype),)
        + block_types(rows),
        in_specs=[HBM_SPEC] * 3 + [VMEM_SPEC],
        out_specs=(VMEM_SPEC,) * (4 + ends),
        scratch_shapes=[pltpu.SemaphoreType.DMA((3 + 2 * rows,))],
        compiler_params=small,
        cost_estimate=pl.CostEstimate(flops=0, bytes_accessed=6000000, transcendentals=0),
        name="own",
    )(stencil_hbm, right_hbm, weight_hbm, held)

    wholes = [lax.ppermute(whole, "frow", move) for whole, move in zip(sent, moves)]
    sides = jnp.stack([odd_side, even_side])
    sides_held = [lax.ppermute(sides, "frow", move) for move in moves]
    halo_blocks = pl.pallas_call(
        functools.partial(rows_kernel, ends),
        out_shape=block_types(STEPS) * ends,
        in_specs=[VMEM_SPEC] * ends,
        out_specs=(VMEM_SPEC,) * (3 * ends),
        compiler_params=small,
        cost_estimate=pl.CostEstimate(flops=0, bytes_accessed=4000000, transcendentals=0),
        name="rows",
    )(*wholes)

    side_types = (
        pltpu.VMEM((slots, rows, 2 * SIDE, LANES), BF16),
        pltpu.VMEM((rows, 2 * SIDE, pixels), F32),
        pltpu.VMEM((rows, 2 * SIDE, pixels), F32),
    )
    beside = pl.pallas_call(
        functools.partial(sides_kernel, ends),
        out_shape=side_types,
        in_specs=[VMEM_SPEC] * 2,
        out_specs=(VMEM_SPEC,) * 3,
        scratch_shapes=[
            pltpu.VMEM((2, 2 * STEPS * rows, pixels), F32),
            pltpu.VMEM((2 * SIDE, LANES), F32),
        ],
        compiler_params=small,
        cost_estimate=pl.CostEstimate(flops=0, bytes_accessed=1000000, transcendentals=0),
        name="sides",
    )(odd_side, even_side)

    cols_held = cols + 2 * SIDE
    rows_held = 2 * rows if ends == 1 else rows + 2 * STEPS
    solution, coarse = pl.pallas_call(
        functools.partial(smooth_kernel, ends),
        out_shape=(
            jax.ShapeDtypeStruct((rows, cols, pixels), F32),
            pltpu.VMEM((rows // 2, cols // 2, pixels), BF16),
        ),
        in_specs=[VMEM_SPEC] * (7 + 4 * ends),
        out_specs=(HBM_SPEC, VMEM_SPEC),
        scratch_shapes=[
            pltpu.VMEM((rows_held, cols_held, pixels), F32),
            pltpu.VMEM((rows_held, cols_held, pixels), F32),
            pltpu.VMEM((rows_held, cols_held, pixels), F32),
            pltpu.VMEM((2, 3, rows_held + 2, cols_held, pixels), BF16),
            pltpu.VMEM((ends, slots, rows, 2 * SIDE, LANES), BF16),
            pltpu.VMEM((ends, rows, 2 * SIDE, pixels), F32),
            pltpu.VMEM((ends, rows, 2 * SIDE, pixels), F32),
            pltpu.VMEM((ends, 2, 2 * STEPS * rows, pixels), F32),
            pltpu.VMEM((2 * SIDE, LANES), F32),
            pltpu.VMEM((rows, cols, pixels), F32),
            pltpu.VMEM((rows, cols, LANES), F32),
            pltpu.SemaphoreType.DMA((rows,)),
        ],
        compiler_params=pltpu.CompilerParams(vmem_limit_bytes=24 * 1024 * 1024),
        name="smooth",
    )(stencil, *beside, *sides_held, mask, right, weight, *halo_blocks)

    half = ring // 2
    across = [(i, (i + half) % ring) for i in range(ring)]
    pair = jnp.stack([coarse, lax.ppermute(coarse, "fcol", across)])
    halves = [list(range(half)), list(range(half, ring))]
    spread = jnp.broadcast_to(pair[None], (half,) + pair.shape)
    block = lax.all_to_all(spread, "fcol", 0, 0, axis_index_groups=halves)
    widened = (rows // 2, ring, cols // 2, pixels)
    gathered = pl.pallas_call(
        widen_kernel,
        out_shape=jax.ShapeDtypeStruct(widened, F32),
        in_specs=[VMEM_SPEC],
        out_specs=HBM_SPEC,
        scratch_shapes=[pltpu.VMEM(widened, F32), pltpu.SemaphoreType.DMA((rows // 2,))],
        compiler_params=small,
        name="widen",
    )(block)
    return solution, gathered.reshape(rows // 2, ring * (cols // 2), pixels)


def solution(mesh):
    placed = (P("frow", "fcol", None), P("frow", "fcol", None), P(), P("frow", "fcol", None))
    return jax.shard_map(
        body,
        mesh=mesh,
        in_specs=placed,
        out_specs=(P("frow", "fcol", None), P("frow", None, None)),
        check_vma=False,
    )
```

```python
import functools

import jax
import jax.numpy as jnp
from jax import lax
from jax.experimental import pallas as pl
from jax.experimental.pallas import tpu as pltpu
from jax.sharding import PartitionSpec as P

DEG = 3
SWEEPS = 2
STEPS = DEG * SWEEPS
SIDE = 8
LANES = 128
STRIPS = ((0, STEPS - 1), (SIDE - STEPS, 0))
PIECE_ROWS = 4

lower_edge = 1.5
upper_edge = 6.0
center = 0.5 * (upper_edge + lower_edge)
half_width = 0.5 * (upper_edge - lower_edge)
weight_middle = 3.75

F32 = jnp.float32
BF16 = jnp.bfloat16
HBM_SPEC = pl.BlockSpec(memory_space=pl.ANY)
VMEM_SPEC = pl.BlockSpec(memory_space=pltpu.VMEM)


def step_factors():
    spread_ratio = center / half_width
    factors = []
    for sweep in range(SWEEPS):
        ratio = 1.0 / spread_ratio
        for step in range(DEG):
            if step < DEG - 1:
                ratio_next = 1.0 / (2.0 * spread_ratio - ratio)
                factors.append((ratio_next * ratio, 2.0 * ratio_next / half_width))
                ratio = ratio_next
            else:
                factors.append((0.0, 1.0 / center))
    return factors


def row_places(ends, own_rows):
    if ends == 1:
        flip = lax.axis_index("frow")
        place = [row + flip * (own_rows - 1 - 2 * row) for row in range(own_rows)]
        return place, [list(enumerate(place))], 0
    above = [(own_rows - STEPS + row, row) for row in range(STEPS)]
    below = [(row, row) for row in range(STEPS)]
    return list(range(own_rows)), [above, below], 1


def rows_sent(ends, own_rows):
    if ends == 1:
        return [([own_rows - 1 - row for row in range(STEPS)], STEPS - 1)]
    return [
        ([own_rows - STEPS + row for row in range(STEPS)], 0),
        (list(range(STEPS)), STEPS - 1),
    ]


def slot_places(ends, slots):
    if ends == 1:
        flip = lax.axis_index("frow")
        return [(slot // 3 + flip * (2 - 2 * (slot // 3))) * 3 + slot % 3 for slot in range(slots)]
    return list(range(slots))


def spread_flags(ends, mask, flags, own_rows, places):
    slots, _, cols, _ = mask.shape
    slot_place = slot_places(ends, slots)
    for slot in range(slots):
        if slot == slots // 2:
            continue
        for row, at in places:
            lane = slot * own_rows + row
            column = jnp.broadcast_to(flags[:, lane : lane + 1], (cols, LANES))
            mask[slot_place[slot], at] = column.astype(BF16)


def edge_kernel(right_hbm, weight_hbm, near_hbm, *refs):
    odd_ref, even_ref, held_ref, strips, flat, near_ref, arrived = refs
    slots, rows, cols = near_ref.shape
    copies = [pltpu.make_async_copy(near_hbm, near_ref, arrived.at[4])]
    for end, start in enumerate((0, cols - SIDE)):
        for kind, source in enumerate((right_hbm, weight_hbm)):
            copies.append(
                pltpu.make_async_copy(
                    source.at[:, pl.ds(start, SIDE)],
                    strips.at[end, kind],
                    arrived.at[2 * end + kind],
                )
            )
    for copy in copies:
        copy.start()
    copies[0].wait()
    flags = jnp.where(near_ref[...] >= 0, 1.0, 0.0).astype(F32).reshape(slots * rows, cols)
    flags = jnp.concatenate([flags, jnp.zeros((slots * rows, LANES - cols), F32)], 1)
    flags = jnp.concatenate([flags, jnp.zeros((LANES - slots * rows, LANES), F32)], 0)
    turned = jnp.transpose(flags)[:cols]
    held_ref[...] = turned
    for copy in copies[1:]:
        copy.wait()
    for end, (low, far) in enumerate(STRIPS):
        for row in range(rows):
            base = 2 * STEPS * row
            flat[end, base : base + STEPS] = strips[end, 0, row, low : low + STEPS]
            weight = strips[end, 1, row, low : low + STEPS] - weight_middle
            flat[end, base + STEPS : base + 2 * STEPS] = weight
            column = row + end * (cols - SIDE)
            flat[end, base + STEPS + far, :LANES] = turned[column]
    parity = lax.rem(lax.axis_index("fcol"), 2)
    odd_ref[...] = flat[parity].astype(BF16)
    even_ref[...] = flat[1 - parity].astype(BF16)


def own_kernel(ends, stencil_hbm, right_hbm, weight_hbm, held_ref, *refs):
    whole_refs = refs[:ends]
    stencil_ref, mask, residual, weight, arrived = refs[ends:]
    slots = mask.shape[0]
    own_rows, own_cols, _ = residual.shape
    place, _, _ = row_places(ends, own_rows)
    slot_place = slot_places(ends, slots)
    copies = []
    for row in range(own_rows):
        for source, target in ((right_hbm, residual), (weight_hbm, weight)):
            copies.append(
                pltpu.make_async_copy(
                    source.at[row], target.at[place[row]], arrived.at[3 + len(copies)]
                )
            )
    stencil_copies = [
        pltpu.make_async_copy(
            stencil_hbm.at[pl.ds(slot, 3)],
            stencil_ref.at[pl.ds(slot_place[slot], 3)],
            arrived.at[slot // 3],
        )
        for slot in range(0, slots, 3)
    ]
    for copy in copies + stencil_copies:
        copy.start()
    flags = held_ref[...]
    spread_flags(ends, mask, flags, own_rows, list(enumerate(place)))
    for copy in copies:
        copy.wait()
    for whole_ref, (sent, far) in zip(whole_refs, rows_sent(ends, own_rows)):
        for row, at in enumerate(sent):
            whole_ref[row, :own_cols] = residual[at].astype(BF16)
            if row == far:
                whole_ref[row, own_cols:, :LANES] = flags.astype(BF16)
                whole_ref[row, own_cols:, LANES:] = flags.astype(BF16)
            else:
                whole_ref[row, own_cols:] = (weight[at] - weight_middle).astype(BF16)
    for copy in stencil_copies:
        copy.wait()


def rows_kernel(ends, *refs):
    for index in range(ends):
        whole_ref = refs[index]
        mask, residual, weight = refs[ends + 3 * index : ends + 3 * index + 3]
        own_rows, own_cols = mask.shape[1], residual.shape[1]
        for row in range(STEPS):
            strip = whole_ref[row].astype(F32)
            residual[row] = strip[:own_cols]
            weight[row] = strip[own_cols:] + weight_middle
        far = rows_sent(ends, own_rows)[index][1]
        flags = whole_ref[far, own_cols:, :LANES].astype(F32)
        places = row_places(ends, own_rows)[1][index]
        spread_flags(ends, mask, flags, own_rows, places)


def lay_sides(ends, odd_ref, even_ref, places, own_rows, mask, right, weight, strips, turned):
    first_of_even = lax.rem(lax.axis_index("fcol"), 2) == 0
    strips[0] = jnp.where(first_of_even, even_ref[...], odd_ref[...]).astype(F32)
    strips[1] = jnp.where(first_of_even, odd_ref[...], even_ref[...]).astype(F32)
    right[...] = jnp.zeros(right.shape, F32)
    weight[...] = jnp.zeros(weight.shape, F32)
    for end, (low, far) in enumerate(STRIPS):
        side = slice(end * SIDE + low, end * SIDE + low + STEPS)
        for row, at in places:
            flat = 2 * STEPS * row
            right[at, side, :] = strips[end, flat : flat + STEPS]
            weight[at, side, :] = strips[end, flat + STEPS : flat + 2 * STEPS] + weight_middle
        for column in range(SIDE):
            flat = 2 * STEPS * column + STEPS + far
            turned[end * SIDE + column] = strips[end, flat, :LANES]
    spread_flags(ends, mask, turned[...], own_rows, places)


def sides_kernel(ends, odd_ref, even_ref, mask, right, weight, strips, turned):
    own_rows = right.shape[0]
    places = list(enumerate(row_places(ends, own_rows)[0]))
    lay_sides(ends, odd_ref, even_ref, places, own_rows, mask, right, weight, strips, turned)


def smooth_kernel(ends, *refs):
    stencil_ref, *beside = refs[:4]
    sides = refs[4 : 4 + ends]
    own_block = refs[4 + ends : 7 + ends]
    halo_blocks = [refs[7 + ends + 3 * i : 10 + ends + 3 * i] for i in range(ends)]
    solution_ref, coarse_ref, residual, weight, direction, shifted = refs[7 + 4 * ends :][:6]
    far_masks, far_right, far_weight, strips, turned, smoothed, summed = refs[13 + 4 * ends :]
    own_rows, own_cols, pixels = solution_ref.shape
    slots = beside[0].shape[0]
    rows, cols, _ = residual.shape
    place, halos, ahead = row_places(ends, own_rows)
    blocks = halo_blocks[:ahead] + [own_block] + halo_blocks[ahead:]
    bases = [0]
    for block in blocks:
        bases.append(bases[-1] + block[1].shape[0])
    if bases[-1] < rows:
        unused = jnp.zeros((rows - bases[-1], cols, pixels), F32)
        residual[bases[-1] :] = unused
        weight[bases[-1] :] = unused
    own_start = bases[ahead]

    def flags_of(masks, slot, first, last):
        pieces = []
        for base, block, flags in zip(bases, blocks, masks):
            low, high = max(first - base, 0), min(last - base, block[1].shape[0])
            if low < high:
                pieces.append(flags[slot, low:high])
        return pieces[0] if len(pieces) == 1 else jnp.concatenate(pieces, 0)

    for base, block in zip(bases, blocks):
        here = slice(base, base + block[1].shape[0])
        residual[here, :own_cols, :] = block[1][...]
        weight[here, :own_cols, :] = block[2][...]
    here = slice(own_start, own_start + own_rows)
    residual[here, own_cols:, :] = beside[1][...]
    weight[here, own_cols:, :] = beside[2][...]
    halo_bases = bases[:ahead] + bases[ahead + 1 : -1]
    for index, (base, sides_ref, places) in enumerate(zip(halo_bases, sides, halos)):
        lay_sides(
            ends, sides_ref.at[0], sides_ref.at[1], places, own_rows, far_masks.at[index],
            far_right.at[index], far_weight.at[index], strips.at[index], turned,
        )
        count = halo_blocks[index][1].shape[0]
        residual[base : base + count, own_cols:, :] = far_right[index, :count]
        weight[base : base + count, own_cols:, :] = far_weight[index, :count]
    side_masks = [far_masks.at[index] for index in range(ends)]
    side_masks = side_masks[:ahead] + [beside[0]] + side_masks[ahead:]

    def put_direction(slot, start, count, value):
        here = slice(start + 1, start + 1 + count)
        shifted[slot, 1, here] = value.astype(BF16)
        shifted[slot, 0, here] = pltpu.roll(value, 1, 1).astype(BF16)
        shifted[slot, 2, here] = pltpu.roll(value, cols - 1, 1).astype(BF16)

    edge = jnp.zeros((cols, pixels), BF16)
    for slot in range(2):
        for move in range(3):
            shifted[slot, move, 0] = edge
            shifted[slot, move, rows + 1] = edge
    value = residual[...] * (1.0 / center)
    direction[...] = value
    put_direction(0, 0, rows, value)

    own = slice(own_start, own_start + own_rows)
    factors = step_factors()
    for step in range(STEPS):
        now, later = step % 2, 1 - step % 2
        last = step == STEPS - 1
        moved = direction[own, :own_cols, :]
        smoothed[...] = moved if step == 0 else smoothed[...] + moved
        margin = STEPS - 1 - step
        count = own_rows + ends * margin
        start = own_start - (ends - 1) * margin
        width = own_cols if last else cols
        pieces = -(-count // PIECE_ROWS)
        cuts = [start + count * i // pieces for i in range(pieces + 1)]
        for base, size in zip(cuts, (high - low for low, high in zip(cuts, cuts[1:]))):
            here = slice(base, base + size)
            coupled = jnp.zeros((size * width, pixels), F32)
            for slot in range(slots):
                across, along = slot // 3, slot % 3
                source = shifted[now, along, base + across : base + across + size, :width, :]
                if slot != slots // 2:
                    keep = flags_of([block[0] for block in blocks], slot, base, base + size)
                    if not last:
                        keep_sides = flags_of(side_masks, slot, base, base + size)
                        keep = jnp.concatenate([keep, keep_sides], 1)
                    source = jnp.concatenate(
                        [source[:, :, :LANES] * keep, source[:, :, LANES:] * keep], 2
                    )
                coupled += jnp.dot(
                    source.reshape(size * width, pixels),
                    stencil_ref[slot],
                    preferred_element_type=F32,
                )
            coupled = coupled.reshape(size, width, pixels)
            moved = direction[here, :width, :]
            left = residual[here, :width, :] - (weight[here, :width, :] * moved + coupled)
            residual[here, :width, :] = left
            if not last:
                a, b = factors[step]
                value = b * left if a == 0.0 else a * moved + b * left
                direction[here, :width, :] = value
                put_direction(later, base, size, value)

    fine = residual[own, :own_cols, :].reshape(own_rows * own_cols, pixels)
    high = fine.astype(BF16)
    low = (fine - high.astype(F32)).astype(BF16)
    quarter = pixels // 4
    from_pixel = lax.broadcasted_iota(jnp.int32, (pixels, LANES), 0) // 4
    to_pixel = lax.broadcasted_iota(jnp.int32, (pixels, LANES), 1)
    adder = jnp.where(from_pixel == to_pixel, 1.0, 0.0).astype(BF16)
    total = jnp.dot(high, adder, preferred_element_type=F32) + jnp.dot(
        low, adder, preferred_element_type=F32
    )
    summed[...] = total.reshape(own_rows, own_cols, LANES)
    for row in range(own_rows // 2):
        pieces = []
        for across in range(2):
            for along in range(2):
                at = place[2 * row + across]
                piece = summed[at, pl.ds(along, own_cols // 2, stride=2), :]
                pieces.append(piece[:, :quarter])
        coarse_ref[row] = jnp.concatenate(pieces, 1).astype(BF16)
    for row, at in enumerate(place):
        solution_ref[row] = smoothed[at]


def widen_kernel(block_ref, out_hbm, wide, sent):
    rows, ring, _, _ = wide.shape
    half = ring // 2
    own_half = lax.axis_index("fcol") // half
    copies = []
    for row in range(rows):
        for kept, part in enumerate((own_half, 1 - own_half)):
            for i in range(half):
                wide[row, part * half + i] = block_ref[i, kept, row].astype(F32)
            here = pl.ds(part * half, half)
            copies.append(
                pltpu.make_async_copy(
                    wide.at[row, here], out_hbm.at[row, here], sent.at[row, kept]
                )
            )
            copies[-1].start()
    for copy in copies:
        copy.wait()


def body(right_side, noise_weight, stencils, neighbours):
    rows, cols, pixels = right_side.shape
    slots = stencils.shape[0]
    pairs, ring = lax.axis_size("frow"), lax.axis_size("fcol")
    swaps = [
        [(i, j) for low in range(first, ring - 1, 2) for i, j in ((low, low + 1), (low + 1, low))]
        for first in (0, 1)
    ]
    near = jnp.transpose(neighbours, (2, 0, 1))
    right_hbm, weight_hbm, near_hbm, stencil_hbm = [
        pltpu.with_memory_space_constraint(array, pltpu.HBM)
        for array in (right_side, noise_weight, near, stencils)
    ]
    small = pltpu.CompilerParams(vmem_limit_bytes=8 * 1024 * 1024)

    side = pltpu.VMEM((2 * STEPS * rows, pixels), BF16)
    odd, even, held = pl.pallas_call(
        edge_kernel,
        out_shape=(side, side, pltpu.VMEM((cols, LANES), F32)),
        in_specs=[HBM_SPEC] * 3,
        out_specs=(VMEM_SPEC,) * 3,
        scratch_shapes=[
            pltpu.VMEM((2, 2, rows, SIDE, pixels), F32),
            pltpu.VMEM((2, 2 * STEPS * rows, pixels), F32),
            pltpu.VMEM((slots, rows, cols), jnp.int32),
            pltpu.SemaphoreType.DMA((5,)),
        ],
        compiler_params=small,
        name="edges",
    )(right_hbm, weight_hbm, near_hbm)

    odd_side = lax.ppermute(odd, "fcol", swaps[1])
    even_side = lax.ppermute(even, "fcol", swaps[0])
    if pairs == 2:
        moves = [[(0, 1), (1, 0)]]
    else:
        moves = [
            [(i, i + 1) for i in range(pairs - 1)],
            [(i + 1, i) for i in range(pairs - 1)],
        ]
    ends = len(moves)

    def block_types(count):
        return (
            pltpu.VMEM((slots, rows, cols, LANES), BF16),
            pltpu.VMEM((count, cols, pixels), F32),
            pltpu.VMEM((count, cols, pixels), F32),
        )

    *sent, stencil, mask, right, weight = pl.pallas_call(
        functools.partial(own_kernel, ends),
        out_shape=(pltpu.VMEM((STEPS, 2 * cols, pixels), BF16),) * ends
        + (pltpu.VMEM(stencils.shape, stencils.dtype),)
        + block_types(rows),
        in_specs=[HBM_SPEC] * 3 + [VMEM_SPEC],
        out_specs=(VMEM_SPEC,) * (4 + ends),
        scratch_shapes=[pltpu.SemaphoreType.DMA((3 + 2 * rows,))],
        compiler_params=small,
        cost_estimate=pl.CostEstimate(flops=0, bytes_accessed=6000000, transcendentals=0),
        name="own",
    )(stencil_hbm, right_hbm, weight_hbm, held)

    wholes = [lax.ppermute(whole, "frow", move) for whole, move in zip(sent, moves)]
    sides = jnp.stack([odd_side, even_side])
    sides_held = [lax.ppermute(sides, "frow", move) for move in moves]
    halo_blocks = pl.pallas_call(
        functools.partial(rows_kernel, ends),
        out_shape=block_types(STEPS) * ends,
        in_specs=[VMEM_SPEC] * ends,
        out_specs=(VMEM_SPEC,) * (3 * ends),
        compiler_params=small,
        cost_estimate=pl.CostEstimate(flops=0, bytes_accessed=4000000, transcendentals=0),
        name="rows",
    )(*wholes)

    side_types = (
        pltpu.VMEM((slots, rows, 2 * SIDE, LANES), BF16),
        pltpu.VMEM((rows, 2 * SIDE, pixels), F32),
        pltpu.VMEM((rows, 2 * SIDE, pixels), F32),
    )
    beside = pl.pallas_call(
        functools.partial(sides_kernel, ends),
        out_shape=side_types,
        in_specs=[VMEM_SPEC] * 2,
        out_specs=(VMEM_SPEC,) * 3,
        scratch_shapes=[
            pltpu.VMEM((2, 2 * STEPS * rows, pixels), F32),
            pltpu.VMEM((2 * SIDE, LANES), F32),
        ],
        compiler_params=small,
        cost_estimate=pl.CostEstimate(flops=0, bytes_accessed=1000000, transcendentals=0),
        name="sides",
    )(odd_side, even_side)

    cols_held = cols + 2 * SIDE
    rows_held = 2 * rows if ends == 1 else rows + 2 * STEPS
    solution, coarse = pl.pallas_call(
        functools.partial(smooth_kernel, ends),
        out_shape=(
            jax.ShapeDtypeStruct((rows, cols, pixels), F32),
            pltpu.VMEM((rows // 2, cols // 2, pixels), BF16),
        ),
        in_specs=[VMEM_SPEC] * (7 + 4 * ends),
        out_specs=(VMEM_SPEC,) * 2,
        scratch_shapes=[
            pltpu.VMEM((rows_held, cols_held, pixels), F32),
            pltpu.VMEM((rows_held, cols_held, pixels), F32),
            pltpu.VMEM((rows_held, cols_held, pixels), F32),
            pltpu.VMEM((2, 3, rows_held + 2, cols_held, pixels), BF16),
            pltpu.VMEM((ends, slots, rows, 2 * SIDE, LANES), BF16),
            pltpu.VMEM((ends, rows, 2 * SIDE, pixels), F32),
            pltpu.VMEM((ends, rows, 2 * SIDE, pixels), F32),
            pltpu.VMEM((ends, 2, 2 * STEPS * rows, pixels), F32),
            pltpu.VMEM((2 * SIDE, LANES), F32),
            pltpu.VMEM((rows, cols, pixels), F32),
            pltpu.VMEM((rows, cols, LANES), F32),
        ],
        compiler_params=pltpu.CompilerParams(vmem_limit_bytes=24 * 1024 * 1024),
        name="smooth",
    )(stencil, *beside, *sides_held, mask, right, weight, *halo_blocks)

    half = ring // 2
    across = [(i, (i + half) % ring) for i in range(ring)]
    pair = jnp.stack([coarse, lax.ppermute(coarse, "fcol", across)])
    halves = [list(range(half)), list(range(half, ring))]
    spread = jnp.broadcast_to(pair[None], (half,) + pair.shape)
    block = lax.all_to_all(spread, "fcol", 0, 0, axis_index_groups=halves)
    widened = (rows // 2, ring, cols // 2, pixels)
    gathered = pl.pallas_call(
        widen_kernel,
        out_shape=jax.ShapeDtypeStruct(widened, F32),
        in_specs=[VMEM_SPEC],
        out_specs=HBM_SPEC,
        scratch_shapes=[pltpu.VMEM(widened, F32), pltpu.SemaphoreType.DMA((rows // 2, 2))],
        compiler_params=small,
        name="widen",
    )(block)
    return solution, gathered.reshape(rows // 2, ring * (cols // 2), pixels)


def solution(mesh):
    placed = (P("frow", "fcol", None), P("frow", "fcol", None), P(), P("frow", "fcol", None))
    return jax.shard_map(
        body,
        mesh=mesh,
        in_specs=placed,
        out_specs=(P("frow", "fcol", None), P("frow", None, None)),
        check_vma=False,
    )
```

```python
import functools

import jax
import jax.numpy as jnp
from jax import lax
from jax.experimental import pallas as pl
from jax.experimental.pallas import tpu as pltpu
from jax.sharding import PartitionSpec as P

DEG = 3
SWEEPS = 2
STEPS = DEG * SWEEPS
SIDE = 8
LANES = 128
STRIPS = ((0, STEPS - 1), (SIDE - STEPS, 0))
PIECE_ROWS = 5

lower_edge = 1.5
upper_edge = 6.0
center = 0.5 * (upper_edge + lower_edge)
half_width = 0.5 * (upper_edge - lower_edge)
weight_middle = 3.75

F32 = jnp.float32
BF16 = jnp.bfloat16
HBM_SPEC = pl.BlockSpec(memory_space=pl.ANY)
VMEM_SPEC = pl.BlockSpec(memory_space=pltpu.VMEM)


def step_factors():
    spread_ratio = center / half_width
    factors = []
    for sweep in range(SWEEPS):
        ratio = 1.0 / spread_ratio
        for step in range(DEG):
            if step < DEG - 1:
                ratio_next = 1.0 / (2.0 * spread_ratio - ratio)
                factors.append((ratio_next * ratio, 2.0 * ratio_next / half_width))
                ratio = ratio_next
            else:
                factors.append((0.0, 1.0 / center))
    return factors


def row_places(ends, own_rows):
    if ends == 1:
        flip = lax.axis_index("frow")
        place = [row + flip * (own_rows - 1 - 2 * row) for row in range(own_rows)]
        return place, [list(enumerate(place))], 0
    above = [(own_rows - STEPS + row, row) for row in range(STEPS)]
    below = [(row, row) for row in range(STEPS)]
    return list(range(own_rows)), [above, below], 1


def rows_sent(ends, own_rows):
    if ends == 1:
        return [([own_rows - 1 - row for row in range(STEPS)], STEPS - 1)]
    return [
        ([own_rows - STEPS + row for row in range(STEPS)], 0),
        (list(range(STEPS)), STEPS - 1),
    ]


def slot_places(ends, slots):
    if ends == 1:
        flip = lax.axis_index("frow")
        return [(slot // 3 + flip * (2 - 2 * (slot // 3))) * 3 + slot % 3 for slot in range(slots)]
    return list(range(slots))


def spread_flags(ends, mask, flags, own_rows, places):
    slots, _, cols, _ = mask.shape
    slot_place = slot_places(ends, slots)
    for slot in range(slots):
        if slot == slots // 2:
            continue
        for row, at in places:
            lane = slot * own_rows + row
            column = jnp.broadcast_to(flags[:, lane : lane + 1], (cols, LANES))
            mask[slot_place[slot], at] = column.astype(BF16)


def edge_kernel(right_hbm, weight_hbm, near_hbm, *refs):
    odd_ref, even_ref, held_ref, strips, flat, near_ref, arrived = refs
    slots, rows, cols = near_ref.shape
    copies = [pltpu.make_async_copy(near_hbm, near_ref, arrived.at[4])]
    for end, start in enumerate((0, cols - SIDE)):
        for kind, source in enumerate((right_hbm, weight_hbm)):
            copies.append(
                pltpu.make_async_copy(
                    source.at[:, pl.ds(start, SIDE)],
                    strips.at[end, kind],
                    arrived.at[2 * end + kind],
                )
            )
    for copy in copies:
        copy.start()
    copies[0].wait()
    flags = jnp.where(near_ref[...] >= 0, 1.0, 0.0).astype(F32).reshape(slots * rows, cols)
    flags = jnp.concatenate([flags, jnp.zeros((slots * rows, LANES - cols), F32)], 1)
    flags = jnp.concatenate([flags, jnp.zeros((LANES - slots * rows, LANES), F32)], 0)
    turned = jnp.transpose(flags)[:cols]
    held_ref[...] = turned
    for copy in copies[1:]:
        copy.wait()
    for end, (low, far) in enumerate(STRIPS):
        for row in range(rows):
            base = 2 * STEPS * row
            flat[end, base : base + STEPS] = strips[end, 0, row, low : low + STEPS]
            weight = strips[end, 1, row, low : low + STEPS] - weight_middle
            flat[end, base + STEPS : base + 2 * STEPS] = weight
            column = row + end * (cols - SIDE)
            flat[end, base + STEPS + far, :LANES] = turned[column]
    parity = lax.rem(lax.axis_index("fcol"), 2)
    odd_ref[...] = flat[parity].astype(BF16)
    even_ref[...] = flat[1 - parity].astype(BF16)


def own_kernel(ends, stencil_hbm, right_hbm, weight_hbm, held_ref, *refs):
    whole_refs = refs[:ends]
    stencil_ref, mask, residual, weight, arrived = refs[ends:]
    slots = mask.shape[0]
    own_rows, own_cols, _ = residual.shape
    place, _, _ = row_places(ends, own_rows)
    slot_place = slot_places(ends, slots)
    copies = []
    for row in range(own_rows):
        for source, target in ((right_hbm, residual), (weight_hbm, weight)):
            copies.append(
                pltpu.make_async_copy(
                    source.at[row], target.at[place[row]], arrived.at[3 + len(copies)]
                )
            )
    stencil_copies = [
        pltpu.make_async_copy(
            stencil_hbm.at[pl.ds(slot, 3)],
            stencil_ref.at[pl.ds(slot_place[slot], 3)],
            arrived.at[slot // 3],
        )
        for slot in range(0, slots, 3)
    ]
    for copy in copies + stencil_copies:
        copy.start()
    flags = held_ref[...]
    spread_flags(ends, mask, flags, own_rows, list(enumerate(place)))
    for copy in copies:
        copy.wait()
    for whole_ref, (sent, far) in zip(whole_refs, rows_sent(ends, own_rows)):
        for row, at in enumerate(sent):
            whole_ref[row, :own_cols] = residual[at].astype(BF16)
            if row == far:
                whole_ref[row, own_cols:, :LANES] = flags.astype(BF16)
                whole_ref[row, own_cols:, LANES:] = flags.astype(BF16)
            else:
                whole_ref[row, own_cols:] = (weight[at] - weight_middle).astype(BF16)
    for copy in stencil_copies:
        copy.wait()


def rows_kernel(ends, *refs):
    for index in range(ends):
        whole_ref = refs[index]
        mask, residual, weight = refs[ends + 3 * index : ends + 3 * index + 3]
        own_rows, own_cols = mask.shape[1], residual.shape[1]
        for row in range(STEPS):
            strip = whole_ref[row].astype(F32)
            residual[row] = strip[:own_cols]
            weight[row] = strip[own_cols:] + weight_middle
        far = rows_sent(ends, own_rows)[index][1]
        flags = whole_ref[far, own_cols:, :LANES].astype(F32)
        places = row_places(ends, own_rows)[1][index]
        spread_flags(ends, mask, flags, own_rows, places)


def lay_sides(ends, odd_ref, even_ref, places, own_rows, mask, right, weight, strips, turned):
    first_of_even = lax.rem(lax.axis_index("fcol"), 2) == 0
    strips[0] = jnp.where(first_of_even, even_ref[...], odd_ref[...]).astype(F32)
    strips[1] = jnp.where(first_of_even, odd_ref[...], even_ref[...]).astype(F32)
    right[...] = jnp.zeros(right.shape, F32)
    weight[...] = jnp.zeros(weight.shape, F32)
    for end, (low, far) in enumerate(STRIPS):
        side = slice(end * SIDE + low, end * SIDE + low + STEPS)
        for row, at in places:
            flat = 2 * STEPS * row
            right[at, side, :] = strips[end, flat : flat + STEPS]
            weight[at, side, :] = strips[end, flat + STEPS : flat + 2 * STEPS] + weight_middle
        for column in range(SIDE):
            flat = 2 * STEPS * column + STEPS + far
            turned[end * SIDE + column] = strips[end, flat, :LANES]
    spread_flags(ends, mask, turned[...], own_rows, places)


def sides_kernel(ends, odd_ref, even_ref, mask, right, weight, strips, turned):
    own_rows = right.shape[0]
    places = list(enumerate(row_places(ends, own_rows)[0]))
    lay_sides(ends, odd_ref, even_ref, places, own_rows, mask, right, weight, strips, turned)


def smooth_kernel(ends, *refs):
    stencil_ref, *beside = refs[:4]
    sides = refs[4 : 4 + ends]
    own_block = refs[4 + ends : 7 + ends]
    halo_blocks = [refs[7 + ends + 3 * i : 10 + ends + 3 * i] for i in range(ends)]
    solution_ref, coarse_ref, residual, weight, direction, shifted = refs[7 + 4 * ends :][:6]
    far_masks, far_right, far_weight, strips, turned, smoothed, summed = refs[13 + 4 * ends :]
    own_rows, own_cols, pixels = solution_ref.shape
    slots = beside[0].shape[0]
    rows, cols, _ = residual.shape
    place, halos, ahead = row_places(ends, own_rows)
    blocks = halo_blocks[:ahead] + [own_block] + halo_blocks[ahead:]
    bases = [0]
    for block in blocks:
        bases.append(bases[-1] + block[1].shape[0])
    if bases[-1] < rows:
        unused = jnp.zeros((rows - bases[-1], cols, pixels), F32)
        residual[bases[-1] :] = unused
        weight[bases[-1] :] = unused
    own_start = bases[ahead]

    def flags_of(masks, slot, first, last):
        pieces = []
        for base, block, flags in zip(bases, blocks, masks):
            low, high = max(first - base, 0), min(last - base, block[1].shape[0])
            if low < high:
                pieces.append(flags[slot, low:high])
        return pieces[0] if len(pieces) == 1 else jnp.concatenate(pieces, 0)

    for base, block in zip(bases, blocks):
        here = slice(base, base + block[1].shape[0])
        residual[here, :own_cols, :] = block[1][...]
        weight[here, :own_cols, :] = block[2][...]
    here = slice(own_start, own_start + own_rows)
    residual[here, own_cols:, :] = beside[1][...]
    weight[here, own_cols:, :] = beside[2][...]
    halo_bases = bases[:ahead] + bases[ahead + 1 : -1]
    for index, (base, sides_ref, places) in enumerate(zip(halo_bases, sides, halos)):
        lay_sides(
            ends, sides_ref.at[0], sides_ref.at[1], places, own_rows, far_masks.at[index],
            far_right.at[index], far_weight.at[index], strips.at[index], turned,
        )
        count = halo_blocks[index][1].shape[0]
        residual[base : base + count, own_cols:, :] = far_right[index, :count]
        weight[base : base + count, own_cols:, :] = far_weight[index, :count]
    side_masks = [far_masks.at[index] for index in range(ends)]
    side_masks = side_masks[:ahead] + [beside[0]] + side_masks[ahead:]

    def put_direction(slot, start, count, value):
        here = slice(start + 1, start + 1 + count)
        shifted[slot, 1, here] = value.astype(BF16)
        shifted[slot, 0, here] = pltpu.roll(value, 1, 1).astype(BF16)
        shifted[slot, 2, here] = pltpu.roll(value, cols - 1, 1).astype(BF16)

    edge = jnp.zeros((cols, pixels), BF16)
    for slot in range(2):
        for move in range(3):
            shifted[slot, move, 0] = edge
            shifted[slot, move, rows + 1] = edge
    value = residual[...] * (1.0 / center)
    direction[...] = value
    put_direction(0, 0, rows, value)

    own = slice(own_start, own_start + own_rows)
    factors = step_factors()
    for step in range(STEPS):
        now, later = step % 2, 1 - step % 2
        last = step == STEPS - 1
        moved = direction[own, :own_cols, :]
        smoothed[...] = moved if step == 0 else smoothed[...] + moved
        margin = STEPS - 1 - step
        count = own_rows + ends * margin
        start = own_start - (ends - 1) * margin
        width = own_cols if last else cols
        pieces = -(-count // PIECE_ROWS)
        cuts = [start + count * i // pieces for i in range(pieces + 1)]
        for base, size in zip(cuts, (high - low for low, high in zip(cuts, cuts[1:]))):
            here = slice(base, base + size)
            coupled = jnp.zeros((size * width, pixels), F32)
            for slot in range(slots):
                across, along = slot // 3, slot % 3
                source = shifted[now, along, base + across : base + across + size, :width, :]
                if slot != slots // 2:
                    keep = flags_of([block[0] for block in blocks], slot, base, base + size)
                    if not last:
                        keep_sides = flags_of(side_masks, slot, base, base + size)
                        keep = jnp.concatenate([keep, keep_sides], 1)
                    source = jnp.concatenate(
                        [source[:, :, :LANES] * keep, source[:, :, LANES:] * keep], 2
                    )
                coupled += jnp.dot(
                    source.reshape(size * width, pixels),
                    stencil_ref[slot],
                    preferred_element_type=F32,
                )
            coupled = coupled.reshape(size, width, pixels)
            moved = direction[here, :width, :]
            left = residual[here, :width, :] - (weight[here, :width, :] * moved + coupled)
            residual[here, :width, :] = left
            if not last:
                a, b = factors[step]
                value = b * left if a == 0.0 else a * moved + b * left
                direction[here, :width, :] = value
                put_direction(later, base, size, value)

    fine = residual[own, :own_cols, :].reshape(own_rows * own_cols, pixels)
    high = fine.astype(BF16)
    low = (fine - high.astype(F32)).astype(BF16)
    quarter = pixels // 4
    from_pixel = lax.broadcasted_iota(jnp.int32, (pixels, LANES), 0) // 4
    to_pixel = lax.broadcasted_iota(jnp.int32, (pixels, LANES), 1)
    adder = jnp.where(from_pixel == to_pixel, 1.0, 0.0).astype(BF16)
    total = jnp.dot(high, adder, preferred_element_type=F32) + jnp.dot(
        low, adder, preferred_element_type=F32
    )
    summed[...] = total.reshape(own_rows, own_cols, LANES)
    for row in range(own_rows // 2):
        pieces = []
        for across in range(2):
            for along in range(2):
                at = place[2 * row + across]
                piece = summed[at, pl.ds(along, own_cols // 2, stride=2), :]
                pieces.append(piece[:, :quarter])
        coarse_ref[row] = jnp.concatenate(pieces, 1).astype(BF16)
    for row, at in enumerate(place):
        solution_ref[row] = smoothed[at]


def widen_kernel(block_ref, out_hbm, wide, sent):
    rows, ring, _, _ = wide.shape
    half = ring // 2
    own_half = lax.axis_index("fcol") // half
    copies = []
    for row in range(rows):
        for i in range(half):
            wide[row, own_half * half + i] = block_ref[i, 0, row].astype(F32)
            wide[row, (1 - own_half) * half + i] = block_ref[i, 1, row].astype(F32)
        copies.append(pltpu.make_async_copy(wide.at[row], out_hbm.at[row], sent.at[row]))
        copies[-1].start()
    for copy in copies:
        copy.wait()


def body(right_side, noise_weight, stencils, neighbours):
    rows, cols, pixels = right_side.shape
    slots = stencils.shape[0]
    pairs, ring = lax.axis_size("frow"), lax.axis_size("fcol")
    swaps = [
        [(i, j) for low in range(first, ring - 1, 2) for i, j in ((low, low + 1), (low + 1, low))]
        for first in (0, 1)
    ]
    near = jnp.transpose(neighbours, (2, 0, 1))
    right_hbm, weight_hbm, near_hbm, stencil_hbm = [
        pltpu.with_memory_space_constraint(array, pltpu.HBM)
        for array in (right_side, noise_weight, near, stencils)
    ]
    small = pltpu.CompilerParams(vmem_limit_bytes=8 * 1024 * 1024)

    side = pltpu.VMEM((2 * STEPS * rows, pixels), BF16)
    odd, even, held = pl.pallas_call(
        edge_kernel,
        out_shape=(side, side, pltpu.VMEM((cols, LANES), F32)),
        in_specs=[HBM_SPEC] * 3,
        out_specs=(VMEM_SPEC,) * 3,
        scratch_shapes=[
            pltpu.VMEM((2, 2, rows, SIDE, pixels), F32),
            pltpu.VMEM((2, 2 * STEPS * rows, pixels), F32),
            pltpu.VMEM((slots, rows, cols), jnp.int32),
            pltpu.SemaphoreType.DMA((5,)),
        ],
        compiler_params=small,
        name="edges",
    )(right_hbm, weight_hbm, near_hbm)

    odd_side = lax.ppermute(odd, "fcol", swaps[1])
    even_side = lax.ppermute(even, "fcol", swaps[0])
    if pairs == 2:
        moves = [[(0, 1), (1, 0)]]
    else:
        moves = [
            [(i, i + 1) for i in range(pairs - 1)],
            [(i + 1, i) for i in range(pairs - 1)],
        ]
    ends = len(moves)

    def block_types(count):
        return (
            pltpu.VMEM((slots, rows, cols, LANES), BF16),
            pltpu.VMEM((count, cols, pixels), F32),
            pltpu.VMEM((count, cols, pixels), F32),
        )

    *sent, stencil, mask, right, weight = pl.pallas_call(
        functools.partial(own_kernel, ends),
        out_shape=(pltpu.VMEM((STEPS, 2 * cols, pixels), BF16),) * ends
        + (pltpu.VMEM(stencils.shape, stencils.dtype),)
        + block_types(rows),
        in_specs=[HBM_SPEC] * 3 + [VMEM_SPEC],
        out_specs=(VMEM_SPEC,) * (4 + ends),
        scratch_shapes=[pltpu.SemaphoreType.DMA((3 + 2 * rows,))],
        compiler_params=small,
        cost_estimate=pl.CostEstimate(flops=0, bytes_accessed=6000000, transcendentals=0),
        name="own",
    )(stencil_hbm, right_hbm, weight_hbm, held)

    wholes = [lax.ppermute(whole, "frow", move) for whole, move in zip(sent, moves)]
    sides = jnp.stack([odd_side, even_side])
    sides_held = [lax.ppermute(sides, "frow", move) for move in moves]
    halo_blocks = pl.pallas_call(
        functools.partial(rows_kernel, ends),
        out_shape=block_types(STEPS) * ends,
        in_specs=[VMEM_SPEC] * ends,
        out_specs=(VMEM_SPEC,) * (3 * ends),
        compiler_params=small,
        cost_estimate=pl.CostEstimate(flops=0, bytes_accessed=4000000, transcendentals=0),
        name="rows",
    )(*wholes)

    side_types = (
        pltpu.VMEM((slots, rows, 2 * SIDE, LANES), BF16),
        pltpu.VMEM((rows, 2 * SIDE, pixels), F32),
        pltpu.VMEM((rows, 2 * SIDE, pixels), F32),
    )
    beside = pl.pallas_call(
        functools.partial(sides_kernel, ends),
        out_shape=side_types,
        in_specs=[VMEM_SPEC] * 2,
        out_specs=(VMEM_SPEC,) * 3,
        scratch_shapes=[
            pltpu.VMEM((2, 2 * STEPS * rows, pixels), F32),
            pltpu.VMEM((2 * SIDE, LANES), F32),
        ],
        compiler_params=small,
        cost_estimate=pl.CostEstimate(flops=0, bytes_accessed=1000000, transcendentals=0),
        name="sides",
    )(odd_side, even_side)

    cols_held = cols + 2 * SIDE
    rows_held = 2 * rows if ends == 1 else rows + 2 * STEPS
    solution, coarse = pl.pallas_call(
        functools.partial(smooth_kernel, ends),
        out_shape=(
            jax.ShapeDtypeStruct((rows, cols, pixels), F32),
            pltpu.VMEM((rows // 2, cols // 2, pixels), BF16),
        ),
        in_specs=[VMEM_SPEC] * (7 + 4 * ends),
        out_specs=(VMEM_SPEC,) * 2,
        scratch_shapes=[
            pltpu.VMEM((rows_held, cols_held, pixels), F32),
            pltpu.VMEM((rows_held, cols_held, pixels), F32),
            pltpu.VMEM((rows_held, cols_held, pixels), F32),
            pltpu.VMEM((2, 3, rows_held + 2, cols_held, pixels), BF16),
            pltpu.VMEM((ends, slots, rows, 2 * SIDE, LANES), BF16),
            pltpu.VMEM((ends, rows, 2 * SIDE, pixels), F32),
            pltpu.VMEM((ends, rows, 2 * SIDE, pixels), F32),
            pltpu.VMEM((ends, 2, 2 * STEPS * rows, pixels), F32),
            pltpu.VMEM((2 * SIDE, LANES), F32),
            pltpu.VMEM((rows, cols, pixels), F32),
            pltpu.VMEM((rows, cols, LANES), F32),
        ],
        compiler_params=pltpu.CompilerParams(vmem_limit_bytes=24 * 1024 * 1024),
        name="smooth",
    )(stencil, *beside, *sides_held, mask, right, weight, *halo_blocks)

    half = ring // 2
    across = [(i, (i + half) % ring) for i in range(ring)]
    pair = jnp.stack([coarse, lax.ppermute(coarse, "fcol", across)])
    halves = [list(range(half)), list(range(half, ring))]
    spread = jnp.broadcast_to(pair[None], (half,) + pair.shape)
    block = lax.all_to_all(spread, "fcol", 0, 0, axis_index_groups=halves)
    widened = (rows // 2, ring, cols // 2, pixels)
    gathered = pl.pallas_call(
        widen_kernel,
        out_shape=jax.ShapeDtypeStruct(widened, F32),
        in_specs=[VMEM_SPEC],
        out_specs=HBM_SPEC,
        scratch_shapes=[pltpu.VMEM(widened, F32), pltpu.SemaphoreType.DMA((rows // 2,))],
        compiler_params=small,
        name="widen",
    )(block)
    return solution, gathered.reshape(rows // 2, ring * (cols // 2), pixels)


def solution(mesh):
    placed = (P("frow", "fcol", None), P("frow", "fcol", None), P(), P("frow", "fcol", None))
    return jax.shard_map(
        body,
        mesh=mesh,
        in_specs=placed,
        out_specs=(P("frow", "fcol", None), P("frow", None, None)),
        check_vma=False,
    )
```
